32 devices in a mesh: rep: 2 (over x), shard: 16 (over z, y, core).
Axes of the slice: x: 2, y: 2, z: 4, core: 2. Of those that a mesh axis runs over, the one named last changes fastest.
Arguments:
- tokens: bfloat16 [16384, 1024], P(('shard', 'rep')), may hold values from -6 to 6
- segments: int32 [16384], P(('shard', 'rep')), may hold values from 0 to 17, as said below
- cotangent: bfloat16 [16384, 1024], P(('shard', 'rep')), may hold values from -6 to 6
- w_qkv: float32 [1024, 3072], P('shard'), may hold values from -0.1875 to 0.1875
- b_qkv: float32 [3072], P('shard'), may hold values from -1.2 to 1.2
- w_out: float32 [1024, 1024], P('shard'), may hold values from -1 to 1
- b_out: float32 [1024], P('shard'), may hold values from -1.2 to 1.2
- gain_one: float32 [1024], P('shard'), may hold values from 0.5 to 1.5
- shift_one: float32 [1024], P('shard'), may hold values from -1.2 to 1.2
- w_up: float32 [1024, 4096], P('shard'), may hold values from -0.1875 to 0.1875
- b_up: float32 [4096], P('shard'), may hold values from -1.2 to 1.2
- w_down: float32 [4096, 1024], P('shard'), may hold values from -0.09375 to 0.09375
- b_down: float32 [1024], P('shard'), may hold values from -1.2 to 1.2
- gain_two: float32 [1024], P('shard'), may hold values from 0.5 to 1.5
- shift_two: float32 [1024], P('shard'), may hold values from -1.2 to 1.2
Outputs:
- result: bfloat16 [16384, 1024], P(('shard', 'rep'))
- input_grad: float32 [16384, 1024], P(('shard', 'rep'))
- grad_w_qkv: float32 [1024, 3072], P('shard')
- grad_b_qkv: float32 [3072], P('shard')
- grad_w_out: float32 [1024, 1024], P('shard')
- grad_b_out: float32 [1024], P('shard')
- grad_gain_one: float32 [1024], P('shard')
- grad_shift_one: float32 [1024], P('shard')
- grad_w_up: float32 [1024, 4096], P('shard')
- grad_b_up: float32 [4096], P('shard')
- grad_w_down: float32 [4096, 1024], P('shard')
- grad_b_down: float32 [1024], P('shard')
- grad_gain_two: float32 [1024], P('shard')
- grad_shift_two: float32 [1024], P('shard')
The draws below stay inside these ranges and needn't reach their ends.
Inputs may be any that keep to these rules, and one draw needn't show every extreme that they name: `segments`: within each sequence of 1024 slots the segment numbers start at 0, never fall and rise by one from one document to the next; every document has 60 to 800 slots except the last of its sequence, which may be shorter; some document has exactly 800 slots.
All inputs are finite; a program needn't handle non-finite values.
Results may differ from the reference program's by a relative error of at most 0.015.
The reference program's roundings to bfloat16 on the way count: a program that leaves them out, or rounds other values in their place, can miss the bound.
Values may be sent and summed in bfloat16 or wider, within the bound.
A program may use at most 192 MiB of HBM per device.

```python
import math
import jax
import jax.numpy as jnp
from jax import lax

D = 1024
HEADS = 16
HEAD_DIM = 64
FF = 4096
SEQ = 1024
DOC_LEAST = 60
DOC_MOST = 800
TOKENS = 16384
SEQS = 16


def draw_segments(key, part):
    seq_count = TOKENS // SEQ
    doc_count = SEQ // DOC_LEAST + 1
    lengths = jax.random.randint(key, (seq_count, doc_count), DOC_LEAST, DOC_MOST + 1)
    lengths = lengths.at[seq_count - 1].set(DOC_LEAST)
    lengths = lengths.at[0, 0].set(DOC_MOST)
    ends = jnp.cumsum(lengths, axis=1)
    position = jnp.arange(SEQ, dtype=jnp.int32)
    passed = (ends[:, None, :] <= position[None, :, None]).astype(jnp.int32)
    return jnp.sum(passed, axis=2).reshape(TOKENS).astype(jnp.int32)


def steps_of(rng, extent, pieces, smallest, top_value):
    factor_of = 1.0
    for axis_at, shards_of in pieces:
        draws = jax.random.uniform(jax.random.fold_in(jax.random.fold_in(rng, 6), axis_at), (shards_of,), jnp.float32, smallest / len(pieces), top_value / len(pieces))
        factor_of = factor_of * jnp.repeat(jnp.exp(draws), extent[axis_at] // shards_of).reshape((-1,) + (1,) * (len(extent) - 1 - axis_at))
    return factor_of


def scatter_about(own_key, shape, deviation, limit, cuts=(), kind=jnp.bfloat16):
    drawn = deviation * jax.random.normal(own_key, shape, jnp.float32)
    if cuts:
        drawn = drawn * steps_of(own_key, shape, cuts, -0.22, 0.18)
    return jnp.clip(drawn, -limit, limit).astype(kind)


def setup_inputs(seed: int = 0) -> dict:
    splits = jax.random.split(jax.random.key(seed), 16)
    return {
        "tokens": scatter_about(splits[0], (TOKENS, D), 1.0, 6.0, ((0, 32),)),
        "segments": draw_segments(jax.random.fold_in(splits[15], 71), 0),
        "cotangent": scatter_about(splits[2], (TOKENS, D), 1.0, 6.0, ((0, 32),)),
        "w_qkv": scatter_about(splits[3], (D, 3 * D), D ** -0.5, 0.1875, ((0, 16),), jnp.float32),
        "b_qkv": scatter_about(splits[4], (3 * D,), 0.2, 1.2, ((0, 16),), jnp.float32),
        "w_out": scatter_about(splits[5], (D, D), (D // 32) ** -0.5, 1.0, ((0, 16),), jnp.float32),
        "b_out": scatter_about(splits[6], (D,), 0.2, 1.2, ((0, 16),), jnp.float32),
        "gain_one": jnp.clip(1.0 + 0.1 * jax.random.normal(splits[7], (D,), jnp.float32), 0.5, 1.5),
        "shift_one": scatter_about(splits[8], (D,), 0.2, 1.2, ((0, 16),), jnp.float32),
        "w_up": scatter_about(splits[9], (D, FF), D ** -0.5, 0.1875, ((0, 16),), jnp.float32),
        "b_up": scatter_about(splits[10], (FF,), 0.2, 1.2, ((0, 16),), jnp.float32),
        "w_down": scatter_about(splits[11], (FF, D), FF ** -0.5, 0.09375, ((0, 16),), jnp.float32),
        "b_down": scatter_about(splits[12], (D,), 0.2, 1.2, ((0, 16),), jnp.float32),
        "gain_two": jnp.clip(1.0 + 0.1 * jax.random.normal(splits[13], (D,), jnp.float32), 0.5, 1.5),
        "shift_two": scatter_about(splits[14], (D,), 0.2, 1.2, ((0, 16),), jnp.float32),
    }


@jax.custom_vjp
def low(v):
    return lax.optimization_barrier(v.astype(jnp.bfloat16)).astype(jnp.float32)

@jax.custom_vjp
def low_back(v):
    return v

def low_keep(v):
    return (low(v), None)

def low_pass(kept, grad):
    return (grad,)

def back_keep(v):
    return (v, None)

def back_low(kept, grad):
    return (low(grad),)
low.defvjp(low_keep, low_pass)
low_back.defvjp(back_keep, back_low)
exact_prec = lax.Precision.HIGHEST

def turn(vectors):
    halfway = vectors.shape[-1] // 2
    return jnp.concatenate([-vectors[..., halfway:], vectors[..., :halfway]], axis=-1)

def rope_tables(first_pos, tok_count):
    position = (first_pos + jnp.arange(tok_count, dtype=jnp.int32)).astype(jnp.float32)
    frequency = jnp.exp(jnp.arange(HEAD_DIM // 2, dtype=jnp.float32) * (-2.0 * math.log(10000.0) / HEAD_DIM))
    angles = position[:, None] * frequency[None, :]
    angles = jnp.concatenate([angles, angles], axis=1)
    return (jnp.cos(angles), jnp.sin(angles))

def normalize(residual, gain_vec, shift_vec):
    mean_val = lax.optimization_barrier(jnp.mean(residual, axis=-1, keepdims=True))
    centred = residual - mean_val
    variance = lax.optimization_barrier(jnp.mean(centred * centred, axis=-1, keepdims=True))
    normed = centred * lax.rsqrt(variance + 1e-05)
    return normed * gain_vec + shift_vec

def layer(params, inputs, seg_ids):
    qkv_w, qkv_b, out_w, out_b, gain_a, shift_a, up_w, up_b, down_w, down_b, gain_b, shift_b = [low(member) for member in params]
    blocks = inputs.shape[0] // SEQ
    score_scale = HEAD_DIM ** (-0.5)
    joined = low_back(jnp.dot(inputs, qkv_w, precision=exact_prec) + qkv_b)
    cosine, sine_table = rope_tables(0, SEQ)
    cosine = cosine[None, :, None, :]
    sine_table = sine_table[None, :, None, :]

    def split_heads(part):
        return part.reshape(blocks, SEQ, HEADS, HEAD_DIM)
    q_raw = split_heads(joined[:, :D])
    k_raw = split_heads(joined[:, D:2 * D])
    queries = low(q_raw * cosine + turn(q_raw) * sine_table)
    key_vecs = low(k_raw * cosine + turn(k_raw) * sine_table)
    values = low(split_heads(joined[:, 2 * D:]))
    same_doc = (seg_ids[:, :, None] == seg_ids[:, None, :])[:, None]
    scores = low_back(jnp.einsum('bqhd,bkhd->bhqk', queries, key_vecs, precision=exact_prec) * score_scale)
    masked = jnp.where(same_doc, scores, -1e+30)
    row_max = lax.optimization_barrier(jnp.max(masked, axis=-1, keepdims=True))
    exponent = jnp.exp(masked - row_max)
    attn_prob = low(exponent / lax.optimization_barrier(jnp.sum(exponent, axis=-1, keepdims=True)))
    context = jnp.einsum('bhqk,bkhd->bqhd', attn_prob, values, precision=exact_prec).reshape(inputs.shape[0], D)
    context = low(low_back(context))
    attn_out = low_back(jnp.dot(context, out_w, precision=exact_prec) + out_b)
    first_norm = normalize(inputs + attn_out, gain_a, shift_a)
    hidden = low_back(jnp.dot(low(first_norm), up_w, precision=exact_prec) + up_b)
    active = low(jax.nn.gelu(hidden, approximate=False))
    ffn_out = low_back(jnp.dot(active, down_w, precision=exact_prec) + down_b)
    return normalize(first_norm + ffn_out, gain_b, shift_b)

def reference(tokens, segments, cotangent, w_qkv, b_qkv, w_out, b_out, gain_one, shift_one, w_up, b_up, w_down, b_down, gain_two, shift_two):
    params = (w_qkv, b_qkv, w_out, b_out, gain_one, shift_one, w_up, b_up, w_down, b_down, gain_two, shift_two)
    groups = SEQS // 2
    inputs = tokens.astype(jnp.float32).reshape(groups, 2 * SEQ, D)
    seg_all = segments.reshape(groups, 2, SEQ)
    upstream = cotangent.astype(jnp.float32).reshape(groups, 2 * SEQ, D)

    def block_step(totals, member):
        block_in, block_seg, block_up = member
        output, pullback = jax.vjp(lambda weights, acts: layer(weights, acts, block_seg), params, block_in)
        weight_grads, input_part = pullback(block_up)
        totals = tuple((a + b for a, b in zip(totals, weight_grads)))
        return (totals, (output, input_part))
    start_sums = tuple((jnp.zeros_like(member) for member in params))
    sums, (outputs, input_parts) = lax.scan(block_step, start_sums, (inputs, seg_all, upstream))
    return (outputs.reshape(TOKENS, D).astype(jnp.bfloat16), input_parts.reshape(TOKENS, D), sums[0], sums[1], sums[2], sums[3], sums[4], sums[5], sums[6], sums[7], sums[8], sums[9], sums[10], sums[11])
```

```python
import functools
import math

import jax
import jax.numpy as jnp
from jax import lax
from jax.experimental import pallas as pl
from jax.experimental.pallas import tpu as pltpu
from jax.sharding import PartitionSpec as P

D = 1024
HEADS = 16
HEAD_DIM = 64
FF = 4096
SLABS = 12
LANES = 128
MASKED = -1e30
MESH = pl.DeviceIdType.MESH
VMEM = 60 * 1024 * 1024
BF = jnp.bfloat16
F32 = jnp.float32

ERFC_P = 0.33
ERFC_Q = (
    0.1863661,
    0.182837329,
    0.20192357,
    0.0450108379,
    0.412542064,
    -0.355440048,
    0.462689118,
    -0.135929052,
)


def dot(a, b):
    return lax.dot_general(a, b, (((1,), (0,)), ((), ())), preferred_element_type=F32)


def dot_nt(a, b):
    return lax.dot_general(a, b, (((1,), (1,)), ((), ())), preferred_element_type=F32)


def dot_tn(a, b):
    return lax.dot_general(a, b, (((0,), (0,)), ((), ())), preferred_element_type=F32)


def swap_halves(a):
    width = a.shape[1]
    lane = lax.broadcasted_iota(jnp.int32, a.shape, 1) % HEAD_DIM
    return jnp.where(
        lane < HEAD_DIM // 2,
        pltpu.roll(a, width - HEAD_DIM // 2, 1),
        pltpu.roll(a, HEAD_DIM // 2, 1),
    )


def split3(a):
    hi = a.astype(BF)
    rest = a - hi.astype(F32)
    mid = rest.astype(BF)
    low = (rest - mid.astype(F32)).astype(BF)
    return hi, mid, low


def swap_width(slab):
    return 384 if slab % 2 == 0 else 256


def remote(src, dst, send, recv, device):
    return pltpu.make_async_remote_copy(
        src_ref=src, dst_ref=dst, send_sem=send, recv_sem=recv, device_id=device, device_id_type=MESH
    )


def place(hi_count):
    index = lax.axis_index("shard")
    return index // 4, (index // 2) % 2, index % 2, lax.axis_index("rep")


def shard_of(hi, mid, core):
    return {"shard": hi * 4 + mid * 2 + core}


def entry_barrier(hi_count, hi, mid, core, rep):
    barrier = pltpu.get_barrier_semaphore()
    for m in range(1, hi_count):
        pl.semaphore_signal(
            barrier, inc=1, device_id=shard_of((hi + m) % hi_count, mid, core), device_id_type=MESH
        )
    pl.semaphore_signal(barrier, inc=1, device_id=shard_of(hi, 1 - mid, core), device_id_type=MESH)
    pl.semaphore_signal(barrier, inc=1, device_id=shard_of(hi, mid, 1 - core), device_id_type=MESH)
    pl.semaphore_signal(barrier, inc=1, device_id={"rep": 1 - rep}, device_id_type=MESH)
    pl.semaphore_wait(barrier, hi_count + 2)


SWAP = 256
PARTS = 2


class Gather:
    def __init__(self, hi_count, packed, full, sems, swap=SWAP):
        self.hi_count = hi_count
        self.packed, self.full = packed, full
        (self.up_send, self.up_recv, self.down_send, self.down_recv, self.y_send, self.y_recv,
         self.x_send, self.x_recv, self.c_send, self.c_recv) = sems
        self.hi, self.mid, self.core, self.rep = place(hi_count)
        slabs, self.depth, width = packed.shape
        self.parts = self.parts_of(self.depth, swap)
        self.rows = self.depth // self.parts
        self.count = slabs * self.parts
        self.swap = swap
        self.mine = slice(None)
        if swap:
            self.mine = pl.ds(pl.multiple_of(self.rep * swap, LANES), width - swap)

    @staticmethod
    def parts_of(depth, swap):
        return PARTS if swap and depth % (16 * PARTS) == 0 else 1

    @staticmethod
    def scratch(hi_count, slabs, depth, swap=SWAP):
        count = slabs * Gather.parts_of(depth, swap)
        dma = pltpu.SemaphoreType.DMA
        hops = dma((count, hi_count - 1))
        return [hops] * 4 + [dma((count,))] * 4 + [dma((count, 2))] * 2

    def only(self, which):
        return pl.ds(pl.multiple_of(which * (D - self.swap), LANES), self.swap)

    def spot(self, chunk):
        start = (chunk % self.parts) * self.rows
        if not isinstance(start, int):
            start = pl.multiple_of(start, self.rows)
        return chunk // self.parts, pl.ds(start, self.rows)

    def hop(self, chunk, distance, up):
        slab, rows = self.spot(chunk)
        origin = self.hi - distance if up else self.hi + distance
        block = self.full.at[slab, origin, self.mid, self.core, rows, self.mine]
        source = self.packed.at[slab, rows, self.mine] if distance == 0 else block
        send, recv = (self.up_send, self.up_recv) if up else (self.down_send, self.down_recv)
        device = shard_of(self.hi + 1 if up else self.hi - 1, self.mid, self.core)
        return remote(source, block, send.at[chunk, distance], recv.at[chunk, distance], device)

    def landed_hop(self, chunk, distance, up):
        slab, rows = self.spot(chunk)
        origin = self.hi - distance - 1 if up else self.hi + distance + 1
        block = self.full.at[slab, origin, self.mid, self.core, rows, self.mine]
        send, recv = (self.up_send, self.up_recv) if up else (self.down_send, self.down_recv)
        device = shard_of(self.hi, self.mid, self.core)
        return remote(block, block, send.at[chunk, distance], recv.at[chunk, distance], device)

    def sends(self, distance, up):
        if up:
            return (self.hi - distance >= 0) & (self.hi + 1 < self.hi_count)
        return (self.hi + distance < self.hi_count) & (self.hi - 1 >= 0)

    def lands(self, distance, up):
        if up:
            return self.hi - distance - 1 >= 0
        return self.hi + distance + 1 < self.hi_count

    def y_copy(self, chunk, landed):
        slab, rows = self.spot(chunk)
        which = 1 - self.mid if landed else self.mid
        block = self.full.at[slab, :, which, self.core, rows, self.mine]
        device = shard_of(self.hi, 1 - self.mid, self.core)
        return remote(block, block, self.y_send.at[chunk], self.y_recv.at[chunk], device)

    def x_copy(self, chunk, landed):
        slab, rows = self.spot(chunk)
        columns = self.only(1 - self.rep if landed else self.rep)
        block = self.full.at[slab, :, :, self.core, rows, columns]
        return remote(block, block, self.x_send.at[chunk], self.x_recv.at[chunk], {"rep": 1 - self.rep})

    def c_copy(self, chunk, part, landed):
        slab, rows = self.spot(chunk)
        which = 1 - self.core if landed else self.core
        columns = self.mine if part == 0 else self.only(1 - self.rep)
        block = self.full.at[slab, :, :, which, rows, columns]
        device = shard_of(self.hi, self.mid, 1 - self.core)
        return remote(block, block, self.c_send.at[chunk, part], self.c_recv.at[chunk, part], device)

    @property
    def lag(self):
        return self.hi_count + 2

    def own_copy(self, sem):
        target = self.full.at[:, self.hi, self.mid, self.core, :, self.mine]
        return pltpu.make_async_copy(self.packed.at[:, :, self.mine], target, sem)

    def tick(self, t):
        def stage(offset, act):
            if not isinstance(t, int):
                act(t - offset)
            elif 0 <= t - offset < self.count:
                act(t - offset)

        def own(chunk):
            for up in (True, False):
                pl.when(self.sends(0, up))(lambda: self.hop(chunk, 0, up).start())

        def forward(distance, chunk):
            for up in (True, False):
                pl.when(self.lands(distance - 1, up))(
                    lambda: self.landed_hop(chunk, distance - 1, up).wait_recv()
                )
                if distance < self.hi_count - 1:
                    pl.when(self.sends(distance, up))(lambda: self.hop(chunk, distance, up).start())
            if distance == self.hi_count - 1:
                self.y_copy(chunk, False).start()

        def after_y(chunk):
            self.y_copy(chunk, True).wait_recv()
            if self.swap:
                self.x_copy(chunk, False).start()
            self.c_copy(chunk, 0, False).start()

        def after_x(chunk):
            if self.swap:
                self.x_copy(chunk, True).wait_recv()
                self.c_copy(chunk, 1, False).start()

        def after_c(chunk):
            for part in range(2 if self.swap else 1):
                self.c_copy(chunk, part, True).wait_recv()

        stage(0, own)
        for distance in range(1, self.hi_count):
            stage(distance, functools.partial(forward, distance))
        stage(self.hi_count, after_y)
        stage(self.hi_count + 1, after_x)
        stage(self.hi_count + 2, after_c)

    def drain(self):
        @pl.loop(0, self.count)
        def _(chunk):
            for distance in range(self.hi_count - 1):
                for up in (True, False):
                    pl.when(self.sends(distance, up))(
                        lambda: self.hop(chunk, distance, up).wait_send()
                    )
            self.y_copy(chunk, False).wait_send()
            if self.swap:
                self.x_copy(chunk, False).wait_send()
            for part in range(2 if self.swap else 1):
                self.c_copy(chunk, part, False).wait_send()


def near_barrier(hi_count):
    hi, mid, core, rep = place(hi_count)
    barrier = pltpu.get_barrier_semaphore()

    def greet(device):
        pl.semaphore_signal(barrier, inc=1, device_id=device, device_id_type=MESH)

    pl.when(hi + 1 < hi_count)(lambda: greet(shard_of(hi + 1, mid, core)))
    pl.when(hi - 1 >= 0)(lambda: greet(shard_of(hi - 1, mid, core)))
    greet(shard_of(hi, 1 - mid, core))
    greet(shard_of(hi, mid, 1 - core))
    greet({"rep": 1 - rep})
    first, last = hi == 0, hi == hi_count - 1
    pl.semaphore_wait(barrier, 5 - first.astype(jnp.int32) - last.astype(jnp.int32))


def gather_kernel(hi_count, packed, vec, tokens, full, vec_full, tokens_all, local_sem, t_sem, *sems):
    rep = lax.axis_index("rep")
    gather = Gather(hi_count, packed, full, sems[:10])
    small = Gather(hi_count, vec, vec_full, sems[10:], swap=0)
    near_barrier(hi_count)
    token_copy = remote(tokens, tokens_all.at[1], t_sem.at[0], t_sem.at[1], {"rep": 1 - rep})
    token_copy.start()
    copies = [
        pltpu.make_async_copy(tokens, tokens_all.at[0], local_sem.at[0]),
        small.own_copy(local_sem.at[1]),
        gather.own_copy(local_sem.at[2]),
    ]
    for copy in copies:
        copy.start()
    for copy in copies:
        copy.wait()
    for t in range(gather.lag + 1):
        small.tick(t)
        gather.tick(t)

    @pl.loop(gather.lag + 1, gather.count)
    def _(t):
        gather.tick(t)

    for t in range(gather.count, gather.count + gather.lag):
        gather.tick(t)
    token_copy.wait()
    small.drain()
    gather.drain()


def gather(hi_count, packed, vec, tokens):
    rows = packed.shape[1]
    anywhere = pl.BlockSpec(memory_space=pl.ANY)
    return pl.pallas_call(
        functools.partial(gather_kernel, hi_count),
        out_shape=(
            jax.ShapeDtypeStruct((SLABS, hi_count, 2, 2, rows, D), BF),
            jax.ShapeDtypeStruct((1, hi_count, 2, 2) + vec.shape, BF),
            jax.ShapeDtypeStruct((2,) + tokens.shape, BF),
        ),
        in_specs=[pl.BlockSpec(memory_space=pltpu.VMEM)] * 3,
        out_specs=(anywhere,) * 3,
        scratch_shapes=[pltpu.SemaphoreType.DMA((3,)), pltpu.SemaphoreType.DMA((2,))]
        + Gather.scratch(hi_count, SLABS, rows)
        + Gather.scratch(hi_count, 1, vec.shape[0], swap=0),
        compiler_params=pltpu.CompilerParams(collective_id=0, has_side_effects=True),
        name="gather",
    )(packed, vec[None], tokens)


def scatter_kernel(
    hi_count,
    g_qkv,
    g_out,
    g_up,
    g_down,
    g_vec,
    total,
    vec_total,
    held,
    from_core,
    from_x,
    from_y,
    from_z,
    own,
    other,
    v_held,
    v_core,
    v_y,
    v_z,
    v_own,
    v_other,
    load_sem,
    c_send,
    c_recv,
    x_send,
    x_recv,
    y_send,
    y_recv,
    z_send,
    z_recv,
    f_send,
    f_recv,
):
    hi, mid, core, rep = place(hi_count)
    own[...] = jnp.zeros_like(own)
    other[...] = jnp.zeros_like(other)
    entry_barrier(hi_count, hi, mid, core, rep)
    sent = []

    def source(slab, which):
        if slab < 3:
            return g_qkv.at[:, :, which, :, slab * D : (slab + 1) * D]
        if slab == 3:
            return g_out.at[:, :, which]
        if slab < 8:
            return g_up.at[:, :, which, :, (slab - 4) * D : (slab - 3) * D]
        if slab < SLABS:
            return g_down.at[slab - 8, :, :, which]
        return g_vec.at[:, :, which]

    def c_copy(slab):
        land = from_core.at[slab] if slab < SLABS else v_core
        return remote(
            source(slab, 1 - core),
            land,
            c_send.at[slab],
            c_recv.at[slab],
            shard_of(hi, mid, 1 - core),
        )

    def load(slab):
        land = held.at[slab] if slab < SLABS else v_held
        return pltpu.make_async_copy(source(slab, core), land, load_sem.at[slab])

    def mine(slab):
        width = D - swap_width(slab)
        return pl.ds(pl.multiple_of(rep * swap_width(slab), LANES), width)

    def only(slab, which):
        width = swap_width(slab)
        return pl.ds(pl.multiple_of(which * (D - width), LANES), width)

    def x_copy(slab):
        width = swap_width(slab)
        return remote(
            held.at[slab, :, :, :, only(slab, 1 - rep)],
            from_x.at[slab, :, :, :, :width],
            x_send.at[slab],
            x_recv.at[slab],
            {"rep": 1 - rep},
        )

    def y_copy(slab):
        if slab < SLABS:
            width = D - swap_width(slab)
            src = held.at[slab, :, 1 - mid, :, mine(slab)]
            dst = from_y.at[slab, :, :, :width]
        else:
            src, dst = v_held.at[:, 1 - mid], v_y
        return remote(src, dst, y_send.at[slab], y_recv.at[slab], shard_of(hi, 1 - mid, core))

    def z_copy(slab, m):
        there = (hi + m) % hi_count
        if slab < SLABS:
            width = D - swap_width(slab)
            src = held.at[slab, there, mid, :, mine(slab)]
            dst = from_z.at[slab, m - 1, :, :width]
        else:
            src, dst = v_held.at[there, mid], v_z.at[m - 1]
        return remote(
            src, dst, z_send.at[slab, m - 1], z_recv.at[slab, m - 1], shard_of(there, mid, core)
        )

    def f_copy(slab):
        if slab < SLABS:
            src, dst = own.at[slab, :, mine(slab)], other.at[slab, :, mine(slab)]
        else:
            src, dst = v_own, v_other
        return remote(src, dst, f_send.at[slab], f_recv.at[slab], {"rep": 1 - rep})

    def f_land(slab):
        if slab < SLABS:
            width = D - swap_width(slab)
            columns = pl.ds(pl.multiple_of((1 - rep) * swap_width(slab), LANES), width)
            dst = other.at[slab, :, columns]
        else:
            dst = v_other
        return remote(dst, dst, f_send.at[slab], f_recv.at[slab], {"rep": 1 - rep})

    def start(copy):
        copy.start()
        sent.append(copy)

    def add_core(slab):
        if slab == SLABS:
            v_held[...] += v_core[...]
            return

        @pl.loop(0, hi_count)
        def _(h):
            for m in range(2):
                held[slab, h, m] = (
                    held[slab, h, m].astype(F32) + from_core[slab, h, m].astype(F32)
                ).astype(BF)

    def add_x(slab):
        width = swap_width(slab)

        @pl.loop(0, hi_count)
        def _(h):
            for m in range(2):
                held[slab, h, m, :, only(slab, rep)] = (
                    held[slab, h, m, :, only(slab, rep)].astype(F32)
                    + from_x[slab, h, m, :, :width].astype(F32)
                ).astype(BF)

    def add_y(slab):
        if slab == SLABS:
            v_held[:, mid] += v_y[...]
            return
        width = D - swap_width(slab)

        @pl.loop(0, hi_count)
        def _(h):
            held[slab, h, mid, :, mine(slab)] = (
                held[slab, h, mid, :, mine(slab)].astype(F32)
                + from_y[slab, h, :, :width].astype(F32)
            ).astype(BF)

    def add_z(slab):
        if slab == SLABS:
            v_own[...] = v_held[hi, mid] + jnp.sum(v_z[...], axis=0)
            return
        width = D - swap_width(slab)
        value = held[slab, hi, mid, :, mine(slab)].astype(F32)
        for m in range(hi_count - 1):
            value += from_z[slab, m, :, :width].astype(F32)
        own[slab, :, mine(slab)] = value.astype(BF)

    order = [8, 9, 10, 11, 4, 5, 6, 7, 3, 0, 1, 2, SLABS]
    count = len(order)
    for slab in order:
        start(c_copy(slab))
        load(slab).start()
    for tick in range(count + 4):
        if tick < count:
            slab = order[tick]
            c_copy(slab).wait_recv()
            load(slab).wait()
            add_core(slab)
            if slab < SLABS:
                start(x_copy(slab))
        if 0 <= tick - 1 < count:
            slab = order[tick - 1]
            if slab < SLABS:
                x_copy(slab).wait_recv()
                add_x(slab)
            start(y_copy(slab))
        if 0 <= tick - 2 < count:
            slab = order[tick - 2]
            y_copy(slab).wait_recv()
            add_y(slab)
            for m in range(1, hi_count):
                start(z_copy(slab, m))
        if 0 <= tick - 3 < count:
            slab = order[tick - 3]
            for m in range(1, hi_count):
                z_copy(slab, m).wait_recv()
            add_z(slab)
            start(f_copy(slab))
        if 0 <= tick - 4 < count:
            slab = order[tick - 4]
            f_land(slab).wait_recv()
            if slab < SLABS:
                total[slab] = own[slab].astype(F32) + other[slab].astype(F32)
            else:
                vec_total[...] = v_own[...] + v_other[...]
    for copy in sent:
        copy.wait_send()


def scatter(hi_count, g_qkv, g_out, g_up, g_down, g_vec):
    rows = D // (4 * hi_count)
    dma = pltpu.SemaphoreType.DMA
    anywhere = pl.BlockSpec(memory_space=pl.ANY)
    vmem = pl.BlockSpec(memory_space=pltpu.VMEM)
    most, least = D - swap_width(1), swap_width(0)
    vec = g_vec.shape[1:]

    def blocks(a):
        return a.reshape((hi_count, 2, 2, rows, a.shape[-1]))

    return pl.pallas_call(
        functools.partial(scatter_kernel, hi_count),
        out_shape=(
            jax.ShapeDtypeStruct((SLABS, rows, D), F32),
            jax.ShapeDtypeStruct(vec, F32),
        ),
        in_specs=[anywhere] * 5,
        out_specs=(vmem,) * 2,
        scratch_shapes=[
            pltpu.VMEM((SLABS, hi_count, 2, rows, D), BF),
            pltpu.VMEM((SLABS, hi_count, 2, rows, D), BF),
            pltpu.VMEM((SLABS, hi_count, 2, rows, least), BF),
            pltpu.VMEM((SLABS, hi_count, rows, most), BF),
            pltpu.VMEM((SLABS, hi_count - 1, rows, most), BF),
            pltpu.VMEM((SLABS, rows, D), BF),
            pltpu.VMEM((SLABS, rows, D), BF),
            pltpu.VMEM((hi_count, 2) + vec, F32),
            pltpu.VMEM((hi_count, 2) + vec, F32),
            pltpu.VMEM((hi_count,) + vec, F32),
            pltpu.VMEM((hi_count - 1,) + vec, F32),
            pltpu.VMEM(vec, F32),
            pltpu.VMEM(vec, F32),
            dma((SLABS + 1,)),
            dma((SLABS + 1,)),
            dma((SLABS + 1,)),
            dma((SLABS + 1,)),
            dma((SLABS + 1,)),
            dma((SLABS + 1,)),
            dma((SLABS + 1,)),
            dma((SLABS + 1, hi_count - 1)),
            dma((SLABS + 1, hi_count - 1)),
            dma((SLABS + 1,)),
            dma((SLABS + 1,)),
        ],
        compiler_params=pltpu.CompilerParams(
            collective_id=1, has_side_effects=True, vmem_limit_bytes=VMEM
        ),
        name="scatter",
    )(
        blocks(g_qkv),
        blocks(g_out),
        blocks(g_up),
        g_down.reshape(4, hi_count, 2, 2, rows, D),
        g_vec.reshape((hi_count, 2, 2) + vec),
    )


QUAD = 4 * HEAD_DIM


def attend_kernel(
    tokens, w_q, w_k, w_v, bias, cosine, sine, q_doc, k_doc, q_out, k_out, v_out, context, q_ext
):
    own_rows = q_out.shape[0]
    x = tokens[...]
    cos_all = jnp.concatenate([cosine[...], cosine[...]], axis=1)
    sin_all = jnp.concatenate([sine[...], sine[...]], axis=1)

    def rope(a, count):
        return a * cos_all[:count] + swap_halves(a) * sin_all[:count]

    q_rows = rope(dot(x[:own_rows], w_q[0]) + bias[0:1], own_rows) * HEAD_DIM**-0.5
    q_out[...] = q_rows.astype(BF)
    k_out[...] = rope(dot(x, w_k[0]) + bias[1:2], 2 * own_rows).astype(BF)
    v_out[...] = (dot(x, w_v[0]) + bias[2:3]).astype(BF)
    doc_k = k_doc[...]
    ones = jnp.ones((2 * own_rows, LANES), BF)
    piece = 256
    for pair in range(2):
        lanes = slice(pair * LANES, (pair + 1) * LANES)
        keys = jnp.concatenate([k_out[:, lanes], doc_k], axis=1)
        values = jnp.concatenate([v_out[:, lanes], ones], axis=1)
        for start in range(0, own_rows, piece):
            rows = slice(start, start + piece)
            q_pair = q_out[rows, lanes]
            lane = lax.broadcasted_iota(jnp.int32, q_pair.shape, 1)
            doc_q = q_doc[rows, :]
            mixed = []
            for head in range(2):
                in_head = (lane // HEAD_DIM) == head
                queries = jnp.concatenate([jnp.where(in_head, q_pair, 0), doc_q], axis=1)
                scores = dot_nt(queries, keys)
                row_max = jnp.max(scores, axis=1, keepdims=True)
                prob = jnp.exp(scores - row_max).astype(BF)
                both = dot(prob, values)
                row_sum = both[:, LANES:]
                mixed.append(both[:, :LANES] / row_sum)
                log_total = row_max + jnp.log(row_sum)
                hi, mid, low = split3(-log_total)
                ext = jnp.where(lane == 61, hi, doc_q)
                ext = jnp.where(lane == 62, mid, ext)
                ext = jnp.where(lane == 63, low, ext)
                q_ext[pair * 2 + head, rows, :] = ext
            context[rows, lanes] = jnp.where(lane < HEAD_DIM, mixed[0], mixed[1]).astype(BF)


def attend(tokens_all, full, bias, cosine, sine, q_doc, k_doc):
    rows = tokens_all.shape[0] // 2
    whole = lambda *shape: pl.BlockSpec(shape, lambda i: (0,) * len(shape))
    weight = lambda slab: pl.BlockSpec((1, D, QUAD), lambda i: (slab, 0, i))
    columns = lambda count: pl.BlockSpec((count, QUAD), lambda i: (0, i))
    return pl.pallas_call(
        attend_kernel,
        grid=(HEADS // 4,),
        out_shape=(
            jax.ShapeDtypeStruct((rows, D), BF),
            jax.ShapeDtypeStruct((2 * rows, D), BF),
            jax.ShapeDtypeStruct((2 * rows, D), BF),
            jax.ShapeDtypeStruct((rows, D), BF),
            jax.ShapeDtypeStruct((HEADS, rows, LANES), BF),
        ),
        in_specs=[
            whole(2 * rows, D),
            weight(0),
            weight(1),
            weight(2),
            columns(3),
            whole(2 * rows, LANES),
            whole(2 * rows, LANES),
            whole(rows, LANES),
            whole(2 * rows, LANES),
        ],
        out_specs=(
            columns(rows),
            columns(2 * rows),
            columns(2 * rows),
            columns(rows),
            pl.BlockSpec((4, rows, LANES), lambda i: (i, 0, 0)),
        ),
        compiler_params=pltpu.CompilerParams(vmem_limit_bytes=VMEM),
        name="attend",
    )(tokens_all, full, full, full, bias, cosine, sine, q_doc, k_doc)


def attend_back_kernel(
    q_in, k_in, v_in, context, d_context, q_ext, k_doc, cosine, sine, d_q, d_k, d_v
):
    own_rows = q_in.shape[0]
    doc_k = k_doc[...]
    for pair in range(2):
        lanes = slice(pair * LANES, (pair + 1) * LANES)
        k_pair, v_pair = k_in[:, lanes], v_in[:, lanes]
        q_pair, g_pair = q_in[:, lanes], d_context[:, lanes]
        lane = lax.broadcasted_iota(jnp.int32, q_pair.shape, 1)
        k_lane = lax.broadcasted_iota(jnp.int32, k_pair.shape, 1)
        keys = jnp.concatenate([k_pair, doc_k], axis=1)
        minus = jnp.where(k_lane < 3, -1.0, 0.0).astype(BF)
        values = jnp.concatenate([v_pair, minus], axis=1)
        product = g_pair.astype(F32) * context[:, lanes].astype(F32)
        dq = jnp.zeros(q_pair.shape, F32)
        dk = jnp.zeros(k_pair.shape, F32)
        dv = jnp.zeros(k_pair.shape, F32)
        for head in range(2):
            in_head = (lane // HEAD_DIM) == head
            q_head = jnp.where(in_head, q_pair, 0)
            g_head = jnp.where(in_head, g_pair, 0)
            inner = jnp.sum(jnp.where(in_head, product, 0.0), axis=1, keepdims=True)
            hi, mid, low = split3(jnp.broadcast_to(inner, q_pair.shape))
            g_ext = jnp.where(lane == 0, hi, jnp.where(lane == 1, mid, low))
            g_ext = jnp.where(lane < 3, g_ext, 0)
            scores = dot_nt(keys, jnp.concatenate([q_head, q_ext[pair * 2 + head]], axis=1))
            prob = jnp.exp(scores)
            dv += dot(prob.astype(BF), g_head)
            d_prob = dot_nt(values, jnp.concatenate([g_head, g_ext], axis=1))
            d_score = (prob * d_prob).astype(BF)
            dk += dot(d_score, q_head)
            k_head = jnp.where((k_lane // HEAD_DIM) == head, k_pair, 0)
            dq += dot_tn(d_score, k_head)
        dq *= HEAD_DIM**-0.5
        cos_all, sin_all = cosine[...], sine[...]
        d_q[:, lanes] = (dq * cos_all[:own_rows] + swap_halves(dq * sin_all[:own_rows])).astype(BF)
        d_k[:, lanes] = (dk * cos_all + swap_halves(dk * sin_all)).astype(BF)
        d_v[:, lanes] = dv.astype(BF)


def attend_back(q, k, v, context, d_context, q_ext, k_doc, cosine, sine):
    rows = q.shape[0]
    whole = lambda *shape: pl.BlockSpec(shape, lambda i: (0,) * len(shape))
    columns = lambda count: pl.BlockSpec((count, QUAD), lambda i: (0, i))
    return pl.pallas_call(
        attend_back_kernel,
        grid=(HEADS // 4,),
        out_shape=(
            jax.ShapeDtypeStruct((rows, D), BF),
            jax.ShapeDtypeStruct((2 * rows, D), BF),
            jax.ShapeDtypeStruct((2 * rows, D), BF),
        ),
        in_specs=[
            columns(rows),
            columns(2 * rows),
            columns(2 * rows),
            columns(rows),
            columns(rows),
            pl.BlockSpec((4, rows, LANES), lambda i: (i, 0, 0)),
            whole(2 * rows, LANES),
            whole(2 * rows, LANES),
            whole(2 * rows, LANES),
        ],
        out_specs=(columns(rows), columns(2 * rows), columns(2 * rows)),
        compiler_params=pltpu.CompilerParams(vmem_limit_bytes=VMEM),
        name="attend_back",
    )(q, k, v, context, d_context, q_ext, k_doc, cosine, sine)


def normed_rows(residual):
    mean_val = jnp.mean(residual, axis=-1, keepdims=True)
    centred = residual - mean_val
    variance = jnp.mean(centred * centred, axis=-1, keepdims=True)
    inv_std = lax.rsqrt(variance + 1e-05)
    return centred * inv_std, inv_std


def norm_back(upstream, normed, inv_std, gain_vec):
    scaled = upstream * gain_vec
    return inv_std * (
        scaled
        - jnp.mean(scaled, axis=-1, keepdims=True)
        - normed * jnp.mean(scaled * normed, axis=-1, keepdims=True)
    )


def column_sum(a):
    return jnp.sum(a, axis=0, keepdims=True)


CHUNK = 512
CHUNKS = FF // CHUNK


def forward_kernel(
    tokens,
    context,
    w_out,
    cotangent,
    vectors,
    b_up,
    w_up,
    w_down,
    result,
    first_out,
    normed_out,
    inv_out,
    active,
    slope,
    d_second,
    d_ffn,
    sums,
    first,
    total,
):
    step = pl.program_id(0)

    @pl.when(step == 0)
    def _():
        attn = dot(context[...], w_out[0]) + vectors[0:1]
        normed, inv_std = normed_rows(tokens[0].astype(F32) + attn)
        first[...] = normed * vectors[1:2] + vectors[2:3]
        first_out[...] = first[...].astype(BF)
        normed_out[...] = normed
        inv_out[...] = jnp.broadcast_to(inv_std, inv_out.shape)

    hidden = dot(first_out[...], w_up[0]) + b_up[...]
    gauss = jnp.exp(hidden * hidden * -0.5)
    t = 1.0 / (1.0 + (ERFC_P * math.sqrt(0.5)) * jnp.abs(hidden))
    poly = jnp.full_like(t, ERFC_Q[-1])
    for coefficient in ERFC_Q[-2::-1]:
        poly = poly * t + coefficient
    tail = 0.5 * t * poly * gauss
    cdf = jnp.where(hidden >= 0, 1.0 - tail, tail)
    act = (hidden * cdf).astype(BF)
    active[...] = act
    slope[...] = (cdf + hidden * gauss * (1.0 / math.sqrt(2.0 * math.pi))).astype(slope.dtype)
    part = dot(act, w_down[0])

    @pl.when(step == 0)
    def _():
        total[...] = part

    @pl.when(step > 0)
    def _():
        total[...] += part

    @pl.when(step == CHUNKS - 1)
    def _():
        gain = vectors[4:5]
        normed, inv_std = normed_rows(first[...] + total[...] + vectors[3:4])
        result[...] = (normed * gain + vectors[5:6]).astype(BF)
        up = cotangent[...].astype(F32)
        sums[0:1] = column_sum(up * normed)
        sums[1:2] = column_sum(up)
        grad = norm_back(up, normed, inv_std, gain)
        d_second[...] = grad
        low = grad.astype(BF)
        d_ffn[...] = low
        sums[2:3] = column_sum(low.astype(F32))


def forward(tokens_all, context, full, cotangent, vectors, b_up):
    rows = context.shape[0]
    per = D // CHUNK
    whole = lambda *shape: pl.BlockSpec(shape, lambda i: (0,) * len(shape))
    wide = pl.BlockSpec((rows, CHUNK), lambda i: (0, i))
    return pl.pallas_call(
        forward_kernel,
        grid=(CHUNKS,),
        out_shape=(
            jax.ShapeDtypeStruct((rows, D), BF),
            jax.ShapeDtypeStruct((rows, D), BF),
            jax.ShapeDtypeStruct((rows, D), F32),
            jax.ShapeDtypeStruct((rows, LANES), F32),
            jax.ShapeDtypeStruct((rows, FF), BF),
            jax.ShapeDtypeStruct((rows, FF), F32),
            jax.ShapeDtypeStruct((rows, D), F32),
            jax.ShapeDtypeStruct((rows, D), BF),
            jax.ShapeDtypeStruct((3, D), F32),
        ),
        in_specs=[
            pl.BlockSpec((1, rows, D), lambda i: (0, 0, 0)),
            whole(rows, D),
            pl.BlockSpec((1, D, D), lambda i: (3, 0, 0)),
            whole(rows, D),
            whole(6, D),
            pl.BlockSpec((1, CHUNK), lambda i: (0, i)),
            pl.BlockSpec((1, D, CHUNK), lambda i: (4 + i // per, 0, i % per)),
            pl.BlockSpec((1, CHUNK, D), lambda i: (8 + i // per, i % per, 0)),
        ],
        out_specs=(
            whole(rows, D),
            whole(rows, D),
            whole(rows, D),
            whole(rows, LANES),
            wide,
            wide,
            whole(rows, D),
            whole(rows, D),
            whole(3, D),
        ),
        scratch_shapes=[pltpu.VMEM((rows, D), F32), pltpu.VMEM((rows, D), F32)],
        compiler_params=pltpu.CompilerParams(vmem_limit_bytes=VMEM),
        name="forward",
    )(tokens_all, context, full, cotangent, vectors, b_up, full, full)


def backward_kernel(
    d_ffn,
    d_second,
    first,
    normed,
    inv_std,
    context,
    vectors,
    w_out,
    active,
    slope,
    w_up,
    w_down,
    g_down,
    g_up,
    g_b_up,
    g_out,
    d_resid,
    d_context,
    sums,
    total,
):
    step = pl.program_id(0)
    low = d_ffn[...]
    d_hidden = (dot_nt(low, w_down[0]) * slope[...]).astype(BF)
    g_down[...] = dot_tn(active[...], low).astype(BF)
    g_up[...] = dot_tn(first[...], d_hidden).astype(BF)
    g_b_up[...] = column_sum(d_hidden.astype(F32))
    part = dot_nt(d_hidden, w_up[0])

    @pl.when(step == 0)
    def _():
        total[...] = d_second[...] + part

    @pl.when(step > 0)
    def _():
        total[...] += part

    @pl.when(step == CHUNKS - 1)
    def _():
        up = total[...]
        sums[0:1] = column_sum(up * normed[...])
        sums[1:2] = column_sum(up)
        grad = norm_back(up, normed[...], inv_std[:, 0:1], vectors[1:2])
        d_resid[...] = grad
        d_attn = grad.astype(BF)
        sums[2:3] = column_sum(d_attn.astype(F32))
        g_out[...] = dot_tn(context[...], d_attn).astype(BF)
        d_context[...] = dot_nt(d_attn, w_out[0]).astype(BF)


def backward(d_ffn, d_second, first, normed, inv_std, context, vectors, full, active, slope):
    rows = context.shape[0]
    per = D // CHUNK
    whole = lambda *shape: pl.BlockSpec(shape, lambda i: (0,) * len(shape))
    wide = pl.BlockSpec((rows, CHUNK), lambda i: (0, i))
    return pl.pallas_call(
        backward_kernel,
        grid=(CHUNKS,),
        out_shape=(
            jax.ShapeDtypeStruct((FF, D), BF),
            jax.ShapeDtypeStruct((D, FF), BF),
            jax.ShapeDtypeStruct((1, FF), F32),
            jax.ShapeDtypeStruct((D, D), BF),
            jax.ShapeDtypeStruct((rows, D), F32),
            jax.ShapeDtypeStruct((rows, D), BF),
            jax.ShapeDtypeStruct((3, D), F32),
        ),
        in_specs=[
            whole(rows, D),
            whole(rows, D),
            whole(rows, D),
            whole(rows, D),
            whole(rows, LANES),
            whole(rows, D),
            whole(6, D),
            pl.BlockSpec((1, D, D), lambda i: (3, 0, 0)),
            wide,
            wide,
            pl.BlockSpec((1, D, CHUNK), lambda i: (4 + i // per, 0, i % per)),
            pl.BlockSpec((1, CHUNK, D), lambda i: (8 + i // per, i % per, 0)),
        ],
        out_specs=(
            pl.BlockSpec((CHUNK, D), lambda i: (i, 0)),
            pl.BlockSpec((D, CHUNK), lambda i: (0, i)),
            pl.BlockSpec((1, CHUNK), lambda i: (0, i)),
            whole(D, D),
            whole(rows, D),
            whole(rows, D),
            whole(3, D),
        ),
        scratch_shapes=[pltpu.VMEM((rows, D), F32)],
        compiler_params=pltpu.CompilerParams(vmem_limit_bytes=VMEM),
        name="backward",
    )(d_ffn, d_second, first, normed, inv_std, context, vectors, full, active, slope, full, full)


def project_back_kernel(tokens, d_joined, d_resid, weight, g_qkv, g_bias, input_grad):
    step = pl.program_id(0)
    low = d_joined[...]
    g_qkv[...] = dot_tn(tokens[0], low).astype(BF)
    g_bias[...] = column_sum(low.astype(F32))
    part = dot_nt(low, weight[0])

    @pl.when(step == 0)
    def _():
        input_grad[...] = d_resid[...] + part

    @pl.when(step > 0)
    def _():
        input_grad[...] += part


def project_back(tokens_all, d_joined, d_resid, full):
    rows = d_joined.shape[0]
    per = D // CHUNK
    whole = lambda *shape: pl.BlockSpec(shape, lambda i: (0,) * len(shape))
    return pl.pallas_call(
        project_back_kernel,
        grid=(3 * per,),
        out_shape=(
            jax.ShapeDtypeStruct((D, 3 * D), BF),
            jax.ShapeDtypeStruct((1, 3 * D), F32),
            jax.ShapeDtypeStruct((rows, D), F32),
        ),
        in_specs=[
            pl.BlockSpec((1, rows, D), lambda i: (0, 0, 0)),
            pl.BlockSpec((rows, CHUNK), lambda i: (0, i)),
            whole(rows, D),
            pl.BlockSpec((1, D, CHUNK), lambda i: (i // per, 0, i % per)),
        ],
        out_specs=(
            pl.BlockSpec((D, CHUNK), lambda i: (0, i)),
            pl.BlockSpec((1, CHUNK), lambda i: (0, i)),
            whole(rows, D),
        ),
        compiler_params=pltpu.CompilerParams(vmem_limit_bytes=VMEM),
        name="project_back",
    )(tokens_all, d_joined, d_resid, full)


def rope_tables(rows):
    half = lax.axis_index("rep")
    index = jnp.arange(2 * rows, dtype=jnp.int32)
    position = ((index + half * rows) % (2 * rows)).astype(F32)
    frequency = jnp.exp(
        jnp.arange(HEAD_DIM // 2, dtype=F32) * (-2.0 * math.log(10000.0) / HEAD_DIM)
    )
    angles = position[:, None] * frequency[None, :]
    cosine, sine = jnp.cos(angles), jnp.sin(angles)
    return (
        jnp.concatenate([cosine] * 4, axis=1),
        jnp.concatenate([-sine, sine, -sine, sine], axis=1),
    )


def local(
    tokens,
    segments,
    cotangent,
    w_qkv,
    b_qkv,
    w_out,
    b_out,
    gain_one,
    shift_one,
    w_up,
    b_up,
    w_down,
    b_down,
    gain_two,
    shift_two,
):
    rows = tokens.shape[0]
    shards = lax.axis_size("shard")
    hi_count = shards // 4
    depth = D // shards
    packed = jnp.concatenate(
        [
            w_qkv.astype(BF).reshape(depth, 3, D).transpose(1, 0, 2),
            w_out.astype(BF)[None],
            w_up.astype(BF).reshape(depth, shards, 4, depth).transpose(2, 0, 1, 3).reshape(4, depth, D),
            w_down.astype(BF).reshape(4, depth, D),
        ],
        axis=0,
    )
    small = (b_qkv, b_out, gain_one, shift_one, b_up, b_down, gain_two, shift_two)
    widths = [a.shape[0] for a in small]
    flat = jnp.concatenate([a.astype(BF) for a in small])
    flat = jnp.pad(flat, (0, -flat.shape[0] % (16 * LANES)))
    full, vec_full, tokens_all = gather(hi_count, packed, flat.reshape(-1, LANES), tokens)
    full = full.reshape(SLABS, D, D)
    vec_rows = vec_full.reshape(shards, flat.shape[0]).astype(F32)
    parts = []
    at = 0
    for width in widths:
        parts.append(vec_rows[:, at : at + width])
        at += width
    bias_qkv = parts[0].reshape(3, D)
    bias_up = parts[4].reshape(shards, 4, depth).transpose(1, 0, 2).reshape(1, FF)
    vectors = jnp.stack([parts[i].reshape(D) for i in (1, 2, 3, 5, 6, 7)])

    seg_peer = lax.ppermute(segments, "rep", [(0, 1), (1, 0)])
    seg_all = jnp.concatenate([segments, seg_peer])
    lane = jnp.arange(LANES, dtype=jnp.int32)[None, :]
    q_doc = (segments[:, None] == lane).astype(BF)
    k_doc = jnp.where((seg_all[:, None] == lane) | (lane >= 64), 0.0, MASKED)
    k_doc = jnp.where((lane >= 61) & (lane < 64), 1.0, k_doc).astype(BF)
    cosine, sine = rope_tables(rows)
    both = tokens_all.reshape(2 * rows, D)
    q, k, v, context, q_ext = attend(both, full, bias_qkv, cosine, sine, q_doc, k_doc)
    result, first, normed, inv_std, active, slope, d_second, d_ffn, sums_two = forward(
        tokens_all, context, full, cotangent, vectors, bias_up
    )
    g_down, g_up, g_b_up, g_out, d_resid, d_context, sums_one = backward(
        d_ffn, d_second, first, normed, inv_std, context, vectors, full, active, slope
    )
    d_q, d_k, d_v = attend_back(q, k, v, context, d_context, q_ext, k_doc, cosine, sine)
    peer = lax.ppermute(
        jnp.concatenate([d_k[rows:], d_v[rows:]], axis=1), "rep", [(0, 1), (1, 0)]
    ).astype(F32)
    own = jnp.concatenate([d_k[:rows], d_v[:rows]], axis=1).astype(F32)
    d_joined = jnp.concatenate([d_q, (own + peer).astype(BF)], axis=1)
    g_qkv, g_b_qkv, input_grad = project_back(tokens_all, d_joined, d_resid, full)

    g_b_up = g_b_up.reshape(4, shards, depth).transpose(1, 0, 2)
    g_small = (
        g_b_qkv,
        sums_one[2],
        sums_one[0],
        sums_one[1],
        g_b_up,
        sums_two[2],
        sums_two[0],
        sums_two[1],
    )
    g_vec = jnp.concatenate([a.reshape(shards, -1) for a in g_small], axis=1)
    g_vec = jnp.pad(g_vec, ((0, 0), (0, -g_vec.shape[1] % (8 * LANES))))
    total, vec_total = scatter(
        hi_count, g_qkv, g_out, g_up, g_down, g_vec.reshape(shards, -1, LANES)
    )
    vec_total = vec_total.reshape(-1)
    outs = []
    at = 0
    for width in widths:
        outs.append(vec_total[at : at + width])
        at += width
    grad_qkv = total[0:3].transpose(1, 0, 2).reshape(depth, 3 * D)
    grad_up = total[4:8].reshape(4, depth, shards, depth).transpose(1, 2, 0, 3).reshape(depth, FF)
    grad_down = total[8:12].reshape(4 * depth, D)
    return (
        result,
        input_grad,
        grad_qkv,
        outs[0],
        total[3],
        outs[1],
        outs[2],
        outs[3],
        grad_up,
        outs[4],
        grad_down,
        outs[5],
        outs[6],
        outs[7],
    )


def solution(mesh):
    act = P(("shard", "rep"), None)
    matrix = P("shard", None)
    vector = P("shard")
    params = (matrix, vector, matrix, vector, vector, vector, matrix, vector, matrix, vector, vector, vector)
    return jax.shard_map(
        local,
        mesh=mesh,
        in_specs=(act, P(("shard", "rep")), act) + params,
        out_specs=(act, act) + params,
        check_vma=False,
    )
```

```python
import functools
import math

import jax
import jax.numpy as jnp
import numpy as np
from jax import lax
from jax.experimental import pallas as pl
from jax.experimental.pallas import tpu as pltpu
from jax.sharding import PartitionSpec as P

D = 1024
HEADS = 16
HEAD_DIM = 64
FF = 4096
SLABS = 12
LANES = 128
MASKED = -1e30
MESH = pl.DeviceIdType.MESH
VMEM = 60 * 1024 * 1024
BF = jnp.bfloat16
F32 = jnp.float32

ERFC_P = 0.33
ERFC_Q = (
    0.1863661,
    0.182837329,
    0.20192357,
    0.0450108379,
    0.412542064,
    -0.355440048,
    0.462689118,
    -0.135929052,
)


def dot(a, b):
    return lax.dot_general(a, b, (((1,), (0,)), ((), ())), preferred_element_type=F32)


def dot_nt(a, b):
    return lax.dot_general(a, b, (((1,), (1,)), ((), ())), preferred_element_type=F32)


def dot_tn(a, b):
    return lax.dot_general(a, b, (((0,), (0,)), ((), ())), preferred_element_type=F32)


def swap_halves(a):
    width = a.shape[1]
    lane = lax.broadcasted_iota(jnp.int32, a.shape, 1) % HEAD_DIM
    return jnp.where(
        lane < HEAD_DIM // 2,
        pltpu.roll(a, width - HEAD_DIM // 2, 1),
        pltpu.roll(a, HEAD_DIM // 2, 1),
    )


def split3(a):
    hi = a.astype(BF)
    rest = a - hi.astype(F32)
    mid = rest.astype(BF)
    low = (rest - mid.astype(F32)).astype(BF)
    return hi, mid, low


def swap_width(slab):
    return 384 if slab % 2 == 0 else 256


def remote(src, dst, send, recv, device):
    return pltpu.make_async_remote_copy(
        src_ref=src, dst_ref=dst, send_sem=send, recv_sem=recv, device_id=device, device_id_type=MESH
    )


def place(hi_count):
    index = lax.axis_index("shard")
    return index // 4, (index // 2) % 2, index % 2, lax.axis_index("rep")


def shard_of(hi, mid, core):
    return {"shard": hi * 4 + mid * 2 + core}


def entry_barrier(hi_count, hi, mid, core, rep):
    barrier = pltpu.get_barrier_semaphore()
    for m in range(1, hi_count):
        pl.semaphore_signal(
            barrier, inc=1, device_id=shard_of((hi + m) % hi_count, mid, core), device_id_type=MESH
        )
    pl.semaphore_signal(barrier, inc=1, device_id=shard_of(hi, 1 - mid, core), device_id_type=MESH)
    pl.semaphore_signal(barrier, inc=1, device_id=shard_of(hi, mid, 1 - core), device_id_type=MESH)
    pl.semaphore_signal(barrier, inc=1, device_id={"rep": 1 - rep}, device_id_type=MESH)
    pl.semaphore_wait(barrier, hi_count + 2)


SWAP = 256
PARTS = 2


def normed_rows(residual):
    mean_val = jnp.mean(residual, axis=-1, keepdims=True)
    centred = residual - mean_val
    variance = jnp.mean(centred * centred, axis=-1, keepdims=True)
    inv_std = lax.rsqrt(variance + 1e-05)
    return centred * inv_std, inv_std


def norm_back(upstream, normed, inv_std, gain_vec):
    scaled = upstream * gain_vec
    return inv_std * (
        scaled
        - jnp.mean(scaled, axis=-1, keepdims=True)
        - normed * jnp.mean(scaled * normed, axis=-1, keepdims=True)
    )


def column_sum(a):
    return jnp.sum(a, axis=0, keepdims=True)


class Gather:
    def __init__(self, hi_count, packed, full, sems, swap=SWAP):
        self.hi_count = hi_count
        self.packed, self.full = packed, full
        (self.up_send, self.up_recv, self.down_send, self.down_recv, self.y_send, self.y_recv,
         self.x_send, self.x_recv, self.c_send, self.c_recv) = sems
        self.hi, self.mid, self.core, self.rep = place(hi_count)
        slabs, self.depth, width = packed.shape
        self.parts = self.parts_of(self.depth, swap)
        self.rows = self.depth // self.parts
        self.count = slabs * self.parts
        self.swap = swap
        self.mine = slice(None)
        if swap:
            self.mine = pl.ds(pl.multiple_of(self.rep * swap, LANES), width - swap)

    @staticmethod
    def parts_of(depth, swap):
        return PARTS if swap and depth % (16 * PARTS) == 0 else 1

    @staticmethod
    def scratch(hi_count, slabs, depth, swap=SWAP):
        count = slabs * Gather.parts_of(depth, swap)
        dma = pltpu.SemaphoreType.DMA
        hops = dma((count, hi_count - 1))
        return [hops] * 4 + [dma((count,))] * 4 + [dma((count, 2))] * 2

    def only(self, which):
        return pl.ds(pl.multiple_of(which * (D - self.swap), LANES), self.swap)

    def spot(self, chunk):
        start = (chunk % self.parts) * self.rows
        if not isinstance(start, int):
            start = pl.multiple_of(start, self.rows)
        return chunk // self.parts, pl.ds(start, self.rows)

    def hop(self, chunk, distance, up):
        slab, rows = self.spot(chunk)
        origin = self.hi - distance if up else self.hi + distance
        block = self.full.at[slab, origin, self.mid, self.core, rows, self.mine]
        source = self.packed.at[slab, rows, self.mine] if distance == 0 else block
        send, recv = (self.up_send, self.up_recv) if up else (self.down_send, self.down_recv)
        device = shard_of(self.hi + 1 if up else self.hi - 1, self.mid, self.core)
        return remote(source, block, send.at[chunk, distance], recv.at[chunk, distance], device)

    def landed_hop(self, chunk, distance, up):
        slab, rows = self.spot(chunk)
        origin = self.hi - distance - 1 if up else self.hi + distance + 1
        block = self.full.at[slab, origin, self.mid, self.core, rows, self.mine]
        send, recv = (self.up_send, self.up_recv) if up else (self.down_send, self.down_recv)
        device = shard_of(self.hi, self.mid, self.core)
        return remote(block, block, send.at[chunk, distance], recv.at[chunk, distance], device)

    def sends(self, distance, up):
        if up:
            return (self.hi - distance >= 0) & (self.hi + 1 < self.hi_count)
        return (self.hi + distance < self.hi_count) & (self.hi - 1 >= 0)

    def lands(self, distance, up):
        if up:
            return self.hi - distance - 1 >= 0
        return self.hi + distance + 1 < self.hi_count

    def y_copy(self, chunk, landed):
        slab, rows = self.spot(chunk)
        which = 1 - self.mid if landed else self.mid
        block = self.full.at[slab, :, which, self.core, rows, self.mine]
        device = shard_of(self.hi, 1 - self.mid, self.core)
        return remote(block, block, self.y_send.at[chunk], self.y_recv.at[chunk], device)

    def x_copy(self, chunk, landed):
        slab, rows = self.spot(chunk)
        columns = self.only(1 - self.rep if landed else self.rep)
        block = self.full.at[slab, :, :, self.core, rows, columns]
        return remote(block, block, self.x_send.at[chunk], self.x_recv.at[chunk], {"rep": 1 - self.rep})

    def c_copy(self, chunk, part, landed):
        slab, rows = self.spot(chunk)
        which = 1 - self.core if landed else self.core
        columns = self.mine if part == 0 else self.only(1 - self.rep)
        block = self.full.at[slab, :, :, which, rows, columns]
        device = shard_of(self.hi, self.mid, 1 - self.core)
        return remote(block, block, self.c_send.at[chunk, part], self.c_recv.at[chunk, part], device)

    @property
    def lag(self):
        return 2 * self.hi_count + 4

    def own_copy(self, sem):
        target = self.full.at[:, self.hi, self.mid, self.core, :, self.mine]
        return pltpu.make_async_copy(self.packed.at[:, :, self.mine], target, sem)

    def tick(self, t):
        def stage(offset, act):
            if not isinstance(t, int):
                chunk = t - offset
                pl.when((chunk >= 0) & (chunk < self.count))(lambda: act(chunk))
            elif 0 <= t - offset < self.count:
                act(t - offset)

        def own(chunk):
            for up in (True, False):
                pl.when(self.sends(0, up))(lambda: self.hop(chunk, 0, up).start())

        def forward(distance, chunk):
            for up in (True, False):
                pl.when(self.lands(distance - 1, up))(
                    lambda: self.landed_hop(chunk, distance - 1, up).wait_recv()
                )
                if distance < self.hi_count - 1:
                    pl.when(self.sends(distance, up))(lambda: self.hop(chunk, distance, up).start())
            if distance == self.hi_count - 1:
                self.y_copy(chunk, False).start()

        def after_y(chunk):
            self.y_copy(chunk, True).wait_recv()
            if self.swap:
                self.x_copy(chunk, False).start()
            self.c_copy(chunk, 0, False).start()

        def after_x(chunk):
            if self.swap:
                self.x_copy(chunk, True).wait_recv()
                self.c_copy(chunk, 1, False).start()

        def after_c(chunk):
            for part in range(2 if self.swap else 1):
                self.c_copy(chunk, part, True).wait_recv()

        stage(0, own)
        for distance in range(1, self.hi_count):
            stage(2 * distance, functools.partial(forward, distance))
        stage(2 * self.hi_count, after_y)
        stage(2 * self.hi_count + 2, after_x)
        stage(2 * self.hi_count + 4, after_c)

    def drain(self):
        @pl.loop(0, self.count)
        def _(chunk):
            for distance in range(self.hi_count - 1):
                for up in (True, False):
                    pl.when(self.sends(distance, up))(
                        lambda: self.hop(chunk, distance, up).wait_send()
                    )
            self.y_copy(chunk, False).wait_send()
            if self.swap:
                self.x_copy(chunk, False).wait_send()
            for part in range(2 if self.swap else 1):
                self.c_copy(chunk, part, False).wait_send()


def near_barrier(hi_count):
    hi, mid, core, rep = place(hi_count)
    barrier = pltpu.get_barrier_semaphore()

    def greet(device):
        pl.semaphore_signal(barrier, inc=1, device_id=device, device_id_type=MESH)

    pl.when(hi + 1 < hi_count)(lambda: greet(shard_of(hi + 1, mid, core)))
    pl.when(hi - 1 >= 0)(lambda: greet(shard_of(hi - 1, mid, core)))
    greet(shard_of(hi, 1 - mid, core))
    greet(shard_of(hi, mid, 1 - core))
    greet({"rep": 1 - rep})
    first, last = hi == 0, hi == hi_count - 1
    pl.semaphore_wait(barrier, 5 - first.astype(jnp.int32) - last.astype(jnp.int32))


UP, DOWN = 4, 5
HALF = D // 2
QUAD = 4 * HEAD_DIM
B_OUT, GAIN_ONE, SHIFT_ONE, B_UP, B_DOWN, GAIN_TWO, SHIFT_TWO = 3, 4, 5, 6, 10, 11, 12
VEC_ROWS = 16


def regroup(pieces, depth):
    out = None
    for u, (tile, start) in enumerate(pieces):
        shift = (u * depth - start) % LANES
        moved = pltpu.roll(tile, shift, 1) if shift else tile
        lane = lax.broadcasted_iota(jnp.int32, moved.shape, 1)
        out = moved if out is None else jnp.where(lane // depth == u, moved, out)
    return out


def tile_of(at):
    return slice(at // LANES * LANES, at // LANES * LANES + LANES)


def pack(packed, w_qkv, w_out, w_up, w_down):
    depth = w_qkv.shape[0]
    for slab in range(3):
        packed[slab] = w_qkv[:, slab * D : (slab + 1) * D].astype(BF)
    packed[3] = w_out[...].astype(BF)
    each = LANES // depth
    for j in range(4):
        packed[DOWN + 2 * j] = w_down[j * depth : (j + 1) * depth].astype(BF)
        for t in range(D // LANES):
            starts = [4 * depth * (t * each + u) + depth * j for u in range(each)]
            pieces = [(w_up[:, tile_of(at)], at % LANES) for at in starts]
            packed[UP + 2 * j, :, t * LANES : (t + 1) * LANES] = regroup(pieces, depth).astype(BF)


def unpack_vectors(vec_full, rows_out, bias, depth):
    hi_count = vec_full.shape[1]
    each = LANES // depth

    def of_shard(shard):
        return vec_full[0, shard // 4, shard // 2 % 2, shard % 2].astype(F32)

    def join(pieces):
        lane = lax.broadcasted_iota(jnp.int32, pieces[0].shape, 1)
        out = pieces[0]
        for u in range(1, each):
            out = jnp.where(lane // depth == u, pieces[u], out)
        return out

    for t in range(D // LANES):
        tile = slice(t * LANES, (t + 1) * LANES)
        rows_out[:, tile] = join([of_shard(t * each + u) for u in range(each)])
        for j in range(3):
            chunks = [(j * D + t * LANES) // depth + u for u in range(each)]
            bias[j : j + 1, tile] = join([of_shard(m // 3)[m % 3 : m % 3 + 1] for m in chunks])


def gelu_parts(hidden):
    gauss = jnp.exp(hidden * hidden * -0.5)
    t = 1.0 / (1.0 + (ERFC_P * math.sqrt(0.5)) * jnp.abs(hidden))
    poly = jnp.full_like(t, ERFC_Q[-1])
    for coefficient in ERFC_Q[-2::-1]:
        poly = poly * t + coefficient
    tail = 0.5 * t * poly * gauss
    cdf = jnp.where(hidden >= 0, 1.0 - tail, tail)
    return hidden * cdf, cdf + hidden * gauss * (1.0 / math.sqrt(2.0 * math.pi))


def forward_kernel(
    hi_count,
    w_qkv,
    w_out,
    w_up,
    w_down,
    vec,
    tokens,
    cotangent,
    q_doc,
    cosine,
    sine,
    full,
    q_all,
    k_all,
    v_all,
    q_ext_all,
    active_all,
    slope_all,
    k_doc,
    context,
    first_low,
    normed_out,
    inv_out,
    result,
    d_second,
    d_ffn,
    sums,
    vectors,
    packed,
    vec_full,
    x_peer,
    slots,
    q_buf,
    k_buf,
    v_buf,
    ext_buf,
    first,
    total,
    act_buf,
    slope_buf,
    bias,
    local_sem,
    load_sem,
    flush_sem,
    t_sem,
    *sems,
):
    rows = tokens.shape[0]
    depth = w_qkv.shape[0]
    rep = lax.axis_index("rep")
    gather = Gather(hi_count, packed, full, sems[:10])
    small = Gather(hi_count, vec, vec_full, sems[10:], swap=0)
    lane_doc = lax.broadcasted_iota(jnp.int32, (rows, LANES), 1)
    other = jnp.where(q_doc[...] > 0.5, 0.0, MASKED)
    other = jnp.where(lane_doc < 61, other, jnp.where(lane_doc < 64, 1.0, 0.0))
    k_doc[:rows] = other.astype(BF)
    pack(packed, w_qkv, w_out, w_up, w_down)
    near_barrier(hi_count)
    peer = {"rep": 1 - rep}
    token_copy = remote(tokens, x_peer, t_sem.at[0], t_sem.at[1], peer)
    doc_copy = remote(k_doc.at[:rows], k_doc.at[rows:], t_sem.at[2], t_sem.at[3], peer)
    copies = [small.own_copy(local_sem.at[0]), gather.own_copy(local_sem.at[1])]
    for copy in copies:
        copy.start()
    doc_copy.start()
    token_copy.start()
    for copy in copies:
        copy.wait()
    warm = gather.lag + 1
    for t in range(warm):
        small.tick(t)
        gather.tick(t)
    unpack_vectors(vec_full, vectors, bias, depth)
    doc_copy.wait()
    token_copy.wait()
    ready = 3 * gather.parts + gather.lag

    @pl.loop(warm, ready)
    def _(t):
        gather.tick(t)

    def load_whole(slab, slot):
        return pltpu.make_async_copy(full.at[slab], slots.at[slot], load_sem.at[slot])

    for slab in range(3):
        load_whole(slab, slab).start()
    for slab in range(3):
        load_whole(slab, slab).wait()

    def weight(slot, columns):
        return slots[slot, :, :, :, :, columns].reshape(D, -1)

    own_rows = pl.ds(pl.multiple_of(rep * rows, rows), rows)
    peer_rows = pl.ds(pl.multiple_of((1 - rep) * rows, rows), rows)

    def rope(a, table_rows):
        cos_part, sin_part = cosine[table_rows, :], sine[table_rows, :]
        cos_part = jnp.concatenate([cos_part, cos_part], axis=1)
        sin_part = jnp.concatenate([sin_part, sin_part], axis=1)
        return a * cos_part + swap_halves(a) * sin_part

    def flushes(i):
        return [
            pltpu.make_async_copy(q_buf.at[i], q_all.at[i], flush_sem.at[0, i]),
            pltpu.make_async_copy(k_buf.at[i], k_all.at[i], flush_sem.at[1, i]),
            pltpu.make_async_copy(v_buf.at[i], v_all.at[i], flush_sem.at[2, i]),
            pltpu.make_async_copy(
                ext_buf.at[pl.ds(4 * i, 4)], q_ext_all.at[pl.ds(4 * i, 4)], flush_sem.at[3, i]
            ),
        ]

    ones = jnp.ones((2 * rows, LANES), BF)
    piece = 256

    @pl.loop(0, HEADS // 4)
    def _(i):
        columns = pl.ds(pl.multiple_of(i * QUAD, QUAD), QUAD)
        own_x, peer_x = tokens[...], x_peer[...]
        w = weight(0, columns)
        q_rows = rope(dot(own_x, w) + bias[0:1, columns], own_rows) * HEAD_DIM**-0.5
        q_buf[i] = q_rows.astype(BF)
        w = weight(1, columns)
        k_buf[i, :rows] = rope(dot(own_x, w) + bias[1:2, columns], own_rows).astype(BF)
        k_buf[i, rows:] = rope(dot(peer_x, w) + bias[1:2, columns], peer_rows).astype(BF)
        w = weight(2, columns)
        v_buf[i, :rows] = (dot(own_x, w) + bias[2:3, columns]).astype(BF)
        v_buf[i, rows:] = (dot(peer_x, w) + bias[2:3, columns]).astype(BF)
        for pair in range(2):
            gather.tick(ready + 2 * i + pair)
            lanes = slice(pair * LANES, (pair + 1) * LANES)
            keys = jnp.concatenate([k_buf[i, :, lanes], k_doc[...]], axis=1)
            values = jnp.concatenate([v_buf[i, :, lanes], ones], axis=1)
            for start in range(0, rows, piece):
                part = slice(start, start + piece)
                q_pair = q_buf[i, part, lanes]
                lane = lax.broadcasted_iota(jnp.int32, q_pair.shape, 1)
                doc_q = q_doc[part, :]
                mixed = []
                for head in range(2):
                    in_head = (lane // HEAD_DIM) == head
                    queries = jnp.concatenate([jnp.where(in_head, q_pair, 0), doc_q], axis=1)
                    scores = dot_nt(queries, keys)
                    row_max = jnp.max(scores, axis=1, keepdims=True)
                    prob = jnp.exp(scores - row_max).astype(BF)
                    both = dot(prob, values)
                    row_sum = both[:, LANES:]
                    mixed.append(both[:, :LANES] / row_sum)
                    hi, mid, low = split3(-(row_max + jnp.log(row_sum)))
                    ext = jnp.where(lane == 61, hi, doc_q)
                    ext = jnp.where(lane == 62, mid, ext)
                    ext = jnp.where(lane == 63, low, ext)
                    ext_buf[4 * i + pair * 2 + head, part, :] = ext
                pair_lanes = pl.ds(pl.multiple_of(i * QUAD + pair * LANES, LANES), LANES)
                context[part, pair_lanes] = jnp.where(lane < HEAD_DIM, mixed[0], mixed[1]).astype(BF)
        for copy in flushes(i):
            copy.start()

    done = ready + HEADS // 2

    def vector(row):
        return vectors[row : row + 1, :]

    load_whole(3, 3).start()
    for slot in range(2):
        load_whole(UP + slot, slot).start()
    load_whole(3, 3).wait()
    attn = dot(context[...], weight(3, slice(None))) + vector(B_OUT)
    normed, inv_std = normed_rows(tokens[...].astype(F32) + attn)
    first[...] = normed * vector(GAIN_ONE) + vector(SHIFT_ONE)
    first_low[...] = first[...].astype(BF)
    normed_out[...] = normed
    inv_out[...] = jnp.broadcast_to(inv_std, inv_out.shape)
    total[...] = first[...] + vector(B_DOWN)

    def keeps(j, half):
        return [
            pltpu.make_async_copy(
                act_buf.at[half], active_all.at[2 * j + half], flush_sem.at[4, 2 * half]
            ),
            pltpu.make_async_copy(
                slope_buf.at[half], slope_all.at[2 * j + half], flush_sem.at[4, 2 * half + 1]
            ),
        ]

    @pl.loop(0, 4)
    def _(j):
        base = lax.rem(j, 2) * 2

        for slot in range(2):
            load_whole(UP + 2 * j + slot, base + slot).wait()
        for half in range(2):
            @pl.when(j > 0)
            def _():
                for copy in keeps(j - 1, half):
                    copy.wait()

            columns = slice(half * HALF, (half + 1) * HALF)
            hidden = dot(first_low[...], weight(base, columns)) + vectors[pl.ds(B_UP + j, 1), columns]
            act, slope = gelu_parts(hidden)
            act_buf[half] = act.astype(BF)
            slope_buf[half] = slope.astype(BF)
            down = slots[base + 1, half * (hi_count // 2) : (half + 1) * (hi_count // 2)].reshape(HALF, D)
            total[...] += dot(act_buf[half], down)
            for copy in keeps(j, half):
                copy.start()
            for step in range(2):
                t = 6 * gather.parts + gather.lag + 2 * gather.parts * j + gather.parts * half + step
                if step < gather.parts:
                    pl.when(t >= done)(lambda: gather.tick(t))

        @pl.when(j < 3)
        def _():
            for slot in range(2):
                load_whole(UP + 2 * j + 2 + slot, 2 - base + slot).start()

    for half in range(2):
        for copy in keeps(3, half):
            copy.wait()
    gain = vector(GAIN_TWO)
    normed, inv_std = normed_rows(total[...])
    result[...] = (normed * gain + vector(SHIFT_TWO)).astype(BF)
    up = cotangent[...].astype(F32)
    sums[0:1] = column_sum(up * normed)
    sums[1:2] = column_sum(up)
    grad = norm_back(up, normed, inv_std, gain)
    d_second[...] = grad
    low = grad.astype(BF)
    d_ffn[...] = low
    sums[2:3] = column_sum(low.astype(F32))
    small.drain()
    gather.drain()

    @pl.loop(0, HEADS // 4)
    def _(i):
        for copy in flushes(i):
            copy.wait()


def forward(hi_count, weights, vec, tokens, cotangent, q_doc, cosine, sine):
    rows = tokens.shape[0]
    depth = weights[0].shape[0]
    anywhere = pl.BlockSpec(memory_space=pl.ANY)
    vmem = pl.BlockSpec(memory_space=pltpu.VMEM)
    dma = pltpu.SemaphoreType.DMA
    quads = HEADS // 4
    shape = jax.ShapeDtypeStruct
    blocks = (hi_count, 2, 2, depth, D)
    return pl.pallas_call(
        functools.partial(forward_kernel, hi_count),
        out_shape=(
            shape((SLABS,) + blocks, BF),
            shape((quads, rows, QUAD), BF),
            shape((quads, 2 * rows, QUAD), BF),
            shape((quads, 2 * rows, QUAD), BF),
            shape((HEADS, rows, LANES), BF),
            shape((8, rows, HALF), BF),
            shape((8, rows, HALF), BF),
            shape((2 * rows, LANES), BF),
            shape((rows, D), BF),
            shape((rows, D), BF),
            shape((rows, D), F32),
            shape((rows, LANES), F32),
            shape((rows, D), BF),
            shape((rows, D), F32),
            shape((rows, D), BF),
            shape((3, D), F32),
            shape((VEC_ROWS, D), F32),
        ),
        in_specs=[vmem] * 10,
        out_specs=(anywhere,) * 7 + (vmem,) * 10,
        scratch_shapes=[
            pltpu.VMEM((SLABS, depth, D), BF),
            pltpu.VMEM((1, hi_count, 2, 2) + vec.shape[1:], BF),
            pltpu.VMEM((rows, D), BF),
            pltpu.VMEM((4,) + blocks, BF),
            pltpu.VMEM((quads, rows, QUAD), BF),
            pltpu.VMEM((quads, 2 * rows, QUAD), BF),
            pltpu.VMEM((quads, 2 * rows, QUAD), BF),
            pltpu.VMEM((HEADS, rows, LANES), BF),
            pltpu.VMEM((rows, D), F32),
            pltpu.VMEM((rows, D), F32),
            pltpu.VMEM((2, rows, HALF), BF),
            pltpu.VMEM((2, rows, HALF), BF),
            pltpu.VMEM((3, D), F32),
            dma((2,)),
            dma((4,)),
            dma((5, quads)),
            dma((4,)),
        ]
        + Gather.scratch(hi_count, SLABS, depth)
        + Gather.scratch(hi_count, 1, vec.shape[1], swap=0),
        compiler_params=pltpu.CompilerParams(
            collective_id=0, has_side_effects=True, vmem_limit_bytes=VMEM
        ),
        name="forward",
    )(*weights, vec, tokens, cotangent, q_doc, cosine, sine)


def scatter_kernel(
    hi_count,
    g_qkv,
    g_out,
    g_up,
    g_down,
    g_vec,
    total,
    vec_total,
    held,
    from_core,
    from_x,
    from_y,
    from_z,
    own,
    other,
    v_held,
    v_core,
    v_y,
    v_z,
    v_own,
    v_other,
    load_sem,
    c_send,
    c_recv,
    x_send,
    x_recv,
    y_send,
    y_recv,
    z_send,
    z_recv,
    f_send,
    f_recv,
):
    hi, mid, core, rep = place(hi_count)
    own[...] = jnp.zeros_like(own)
    other[...] = jnp.zeros_like(other)
    entry_barrier(hi_count, hi, mid, core, rep)
    sent = []

    def source(slab, which):
        if slab < 3:
            return g_qkv.at[:, :, which, :, slab * D : (slab + 1) * D]
        if slab == 3:
            return g_out.at[:, :, which]
        if slab < 8:
            return g_up.at[:, :, which, :, (slab - 4) * D : (slab - 3) * D]
        if slab < SLABS:
            return g_down.at[slab - 8, :, :, which]
        return g_vec.at[:, :, which]

    def c_copy(slab):
        land = from_core.at[slab] if slab < SLABS else v_core
        return remote(
            source(slab, 1 - core),
            land,
            c_send.at[slab],
            c_recv.at[slab],
            shard_of(hi, mid, 1 - core),
        )

    def load(slab):
        land = held.at[slab] if slab < SLABS else v_held
        return pltpu.make_async_copy(source(slab, core), land, load_sem.at[slab])

    def mine(slab):
        width = D - swap_width(slab)
        return pl.ds(pl.multiple_of(rep * swap_width(slab), LANES), width)

    def only(slab, which):
        width = swap_width(slab)
        return pl.ds(pl.multiple_of(which * (D - width), LANES), width)

    def x_copy(slab):
        width = swap_width(slab)
        return remote(
            held.at[slab, :, :, :, only(slab, 1 - rep)],
            from_x.at[slab, :, :, :, :width],
            x_send.at[slab],
            x_recv.at[slab],
            {"rep": 1 - rep},
        )

    def y_copy(slab):
        if slab < SLABS:
            width = D - swap_width(slab)
            src = held.at[slab, :, 1 - mid, :, mine(slab)]
            dst = from_y.at[slab, :, :, :width]
        else:
            src, dst = v_held.at[:, 1 - mid], v_y
        return remote(src, dst, y_send.at[slab], y_recv.at[slab], shard_of(hi, 1 - mid, core))

    def z_copy(slab, m):
        there = (hi + m) % hi_count
        if slab < SLABS:
            width = D - swap_width(slab)
            src = held.at[slab, there, mid, :, mine(slab)]
            dst = from_z.at[slab, m - 1, :, :width]
        else:
            src, dst = v_held.at[there, mid], v_z.at[m - 1]
        return remote(
            src, dst, z_send.at[slab, m - 1], z_recv.at[slab, m - 1], shard_of(there, mid, core)
        )

    def f_copy(slab):
        if slab < SLABS:
            src, dst = own.at[slab, :, mine(slab)], other.at[slab, :, mine(slab)]
        else:
            src, dst = v_own, v_other
        return remote(src, dst, f_send.at[slab], f_recv.at[slab], {"rep": 1 - rep})

    def f_land(slab):
        if slab < SLABS:
            width = D - swap_width(slab)
            columns = pl.ds(pl.multiple_of((1 - rep) * swap_width(slab), LANES), width)
            dst = other.at[slab, :, columns]
        else:
            dst = v_other
        return remote(dst, dst, f_send.at[slab], f_recv.at[slab], {"rep": 1 - rep})

    def start(copy):
        copy.start()
        sent.append(copy)

    def add_core(slab):
        if slab == SLABS:
            v_held[...] += v_core[...]
            return

        @pl.loop(0, hi_count)
        def _(h):
            for m in range(2):
                held[slab, h, m] = (
                    held[slab, h, m].astype(F32) + from_core[slab, h, m].astype(F32)
                ).astype(BF)

    def add_x(slab):
        width = swap_width(slab)

        @pl.loop(0, hi_count)
        def _(h):
            for m in range(2):
                held[slab, h, m, :, only(slab, rep)] = (
                    held[slab, h, m, :, only(slab, rep)].astype(F32)
                    + from_x[slab, h, m, :, :width].astype(F32)
                ).astype(BF)

    def add_y(slab):
        if slab == SLABS:
            v_held[:, mid] += v_y[...]
            return
        width = D - swap_width(slab)

        @pl.loop(0, hi_count)
        def _(h):
            held[slab, h, mid, :, mine(slab)] = (
                held[slab, h, mid, :, mine(slab)].astype(F32)
                + from_y[slab, h, :, :width].astype(F32)
            ).astype(BF)

    def add_z(slab):
        if slab == SLABS:
            v_own[...] = v_held[hi, mid] + jnp.sum(v_z[...], axis=0)
            return
        width = D - swap_width(slab)
        value = held[slab, hi, mid, :, mine(slab)].astype(F32)
        for m in range(hi_count - 1):
            value += from_z[slab, m, :, :width].astype(F32)
        own[slab, :, mine(slab)] = value.astype(BF)

    order = [8, 9, 10, 11, 4, 5, 6, 7, 3, 0, 1, 2, SLABS]
    count = len(order)
    for slab in order:
        start(c_copy(slab))
        load(slab).start()
    for tick in range(count + 4):
        if tick < count:
            slab = order[tick]
            c_copy(slab).wait_recv()
            load(slab).wait()
            add_core(slab)
            if slab < SLABS:
                start(x_copy(slab))
        if 0 <= tick - 1 < count:
            slab = order[tick - 1]
            if slab < SLABS:
                x_copy(slab).wait_recv()
                add_x(slab)
            start(y_copy(slab))
        if 0 <= tick - 2 < count:
            slab = order[tick - 2]
            y_copy(slab).wait_recv()
            add_y(slab)
            for m in range(1, hi_count):
                start(z_copy(slab, m))
        if 0 <= tick - 3 < count:
            slab = order[tick - 3]
            for m in range(1, hi_count):
                z_copy(slab, m).wait_recv()
            add_z(slab)
            start(f_copy(slab))
        if 0 <= tick - 4 < count:
            slab = order[tick - 4]
            f_land(slab).wait_recv()
            if slab < SLABS:
                total[slab] = own[slab].astype(F32) + other[slab].astype(F32)
            else:
                vec_total[...] = v_own[...] + v_other[...]
    for copy in sent:
        copy.wait_send()


def scatter(hi_count, g_qkv, g_out, g_up, g_down, g_vec):
    rows = D // (4 * hi_count)
    dma = pltpu.SemaphoreType.DMA
    anywhere = pl.BlockSpec(memory_space=pl.ANY)
    vmem = pl.BlockSpec(memory_space=pltpu.VMEM)
    most, least = D - swap_width(1), swap_width(0)
    vec = g_vec.shape[1:]

    def blocks(a):
        return a.reshape((hi_count, 2, 2, rows, a.shape[-1]))

    return pl.pallas_call(
        functools.partial(scatter_kernel, hi_count),
        out_shape=(
            jax.ShapeDtypeStruct((SLABS, rows, D), F32),
            jax.ShapeDtypeStruct(vec, F32),
        ),
        in_specs=[anywhere] * 5,
        out_specs=(vmem,) * 2,
        scratch_shapes=[
            pltpu.VMEM((SLABS, hi_count, 2, rows, D), BF),
            pltpu.VMEM((SLABS, hi_count, 2, rows, D), BF),
            pltpu.VMEM((SLABS, hi_count, 2, rows, least), BF),
            pltpu.VMEM((SLABS, hi_count, rows, most), BF),
            pltpu.VMEM((SLABS, hi_count - 1, rows, most), BF),
            pltpu.VMEM((SLABS, rows, D), BF),
            pltpu.VMEM((SLABS, rows, D), BF),
            pltpu.VMEM((hi_count, 2) + vec, F32),
            pltpu.VMEM((hi_count, 2) + vec, F32),
            pltpu.VMEM((hi_count,) + vec, F32),
            pltpu.VMEM((hi_count - 1,) + vec, F32),
            pltpu.VMEM(vec, F32),
            pltpu.VMEM(vec, F32),
            dma((SLABS + 1,)),
            dma((SLABS + 1,)),
            dma((SLABS + 1,)),
            dma((SLABS + 1,)),
            dma((SLABS + 1,)),
            dma((SLABS + 1,)),
            dma((SLABS + 1,)),
            dma((SLABS + 1, hi_count - 1)),
            dma((SLABS + 1, hi_count - 1)),
            dma((SLABS + 1,)),
            dma((SLABS + 1,)),
        ],
        compiler_params=pltpu.CompilerParams(
            collective_id=1, has_side_effects=True, vmem_limit_bytes=VMEM
        ),
        name="scatter",
    )(
        blocks(g_qkv),
        blocks(g_out),
        blocks(g_up),
        g_down.reshape(4, hi_count, 2, 2, rows, D),
        g_vec.reshape((hi_count, 2, 2) + vec),
    )


def attend_back_kernel(
    q_in, k_in, v_in, context, d_context, q_ext, k_doc, cosine, sine, d_q, d_k, d_v
):
    own_rows = q_in.shape[1]
    doc_k = k_doc[...]
    for pair in range(2):
        lanes = slice(pair * LANES, (pair + 1) * LANES)
        k_pair, v_pair = k_in[0, :, lanes], v_in[0, :, lanes]
        q_pair, g_pair = q_in[0, :, lanes], d_context[:, lanes]
        lane = lax.broadcasted_iota(jnp.int32, q_pair.shape, 1)
        k_lane = lax.broadcasted_iota(jnp.int32, k_pair.shape, 1)
        keys = jnp.concatenate([k_pair, doc_k], axis=1)
        minus = jnp.where(k_lane < 3, -1.0, 0.0).astype(BF)
        values = jnp.concatenate([v_pair, minus], axis=1)
        product = g_pair.astype(F32) * context[:, lanes].astype(F32)
        dq = jnp.zeros(q_pair.shape, F32)
        dk = jnp.zeros(k_pair.shape, F32)
        dv = jnp.zeros(k_pair.shape, F32)
        for head in range(2):
            in_head = (lane // HEAD_DIM) == head
            q_head = jnp.where(in_head, q_pair, 0)
            g_head = jnp.where(in_head, g_pair, 0)
            inner = jnp.sum(jnp.where(in_head, product, 0.0), axis=1, keepdims=True)
            hi, mid, low = split3(jnp.broadcast_to(inner, q_pair.shape))
            g_ext = jnp.where(lane == 0, hi, jnp.where(lane == 1, mid, low))
            g_ext = jnp.where(lane < 3, g_ext, 0)
            scores = dot_nt(keys, jnp.concatenate([q_head, q_ext[pair * 2 + head]], axis=1))
            prob = jnp.exp(scores)
            dv += dot(prob.astype(BF), g_head)
            d_prob = dot_nt(values, jnp.concatenate([g_head, g_ext], axis=1))
            d_score = (prob * d_prob).astype(BF)
            dk += dot(d_score, q_head)
            k_head = jnp.where((k_lane // HEAD_DIM) == head, k_pair, 0)
            dq += dot_tn(d_score, k_head)
        dq *= HEAD_DIM**-0.5
        cos_all, sin_all = cosine[...], sine[...]
        d_q[:, lanes] = (dq * cos_all[:own_rows] + swap_halves(dq * sin_all[:own_rows])).astype(BF)
        d_k[:, lanes] = (dk * cos_all + swap_halves(dk * sin_all)).astype(BF)
        d_v[:, lanes] = dv.astype(BF)


def attend_back(q, k, v, context, d_context, q_ext, k_doc, cosine, sine):
    rows = q.shape[1]
    whole = lambda *shape: pl.BlockSpec(shape, lambda i: (0,) * len(shape))
    columns = lambda count: pl.BlockSpec((count, QUAD), lambda i: (0, i))
    return pl.pallas_call(
        attend_back_kernel,
        grid=(HEADS // 4,),
        out_shape=(
            jax.ShapeDtypeStruct((rows, D), BF),
            jax.ShapeDtypeStruct((2 * rows, D), BF),
            jax.ShapeDtypeStruct((2 * rows, D), BF),
        ),
        in_specs=[
            pl.BlockSpec((1, rows, QUAD), lambda i: (i, 0, 0)),
            pl.BlockSpec((1, 2 * rows, QUAD), lambda i: (i, 0, 0)),
            pl.BlockSpec((1, 2 * rows, QUAD), lambda i: (i, 0, 0)),
            columns(rows),
            columns(rows),
            pl.BlockSpec((4, rows, LANES), lambda i: (i, 0, 0)),
            whole(2 * rows, LANES),
            whole(2 * rows, LANES),
            whole(2 * rows, LANES),
        ],
        out_specs=(columns(rows), columns(2 * rows), columns(2 * rows)),
        compiler_params=pltpu.CompilerParams(vmem_limit_bytes=VMEM),
        name="attend_back",
    )(q, k, v, context, d_context, q_ext, k_doc, cosine, sine)


CHUNK = 512
CHUNKS = FF // CHUNK


def backward_kernel(
    d_ffn,
    d_second,
    first,
    normed,
    inv_std,
    context,
    vectors,
    w_out,
    active,
    slope,
    w_up,
    w_down,
    g_down,
    g_up,
    g_b_up,
    g_out,
    d_resid,
    d_context,
    sums,
    total,
):
    step = pl.program_id(0)
    low = d_ffn[...]
    d_hidden = (dot_nt(low, w_down[0]) * slope[0].astype(F32)).astype(BF)
    g_down[...] = dot_tn(active[0], low).astype(BF)
    g_up[...] = dot_tn(first[...], d_hidden).astype(BF)
    g_b_up[...] = column_sum(d_hidden.astype(F32))
    part = dot_nt(d_hidden, w_up[0])

    @pl.when(step == 0)
    def _():
        total[...] = d_second[...] + part

    @pl.when(step > 0)
    def _():
        total[...] += part

    @pl.when(step == CHUNKS - 1)
    def _():
        up = total[...]
        sums[0:1] = column_sum(up * normed[...])
        sums[1:2] = column_sum(up)
        grad = norm_back(up, normed[...], inv_std[:, 0:1], vectors[GAIN_ONE : GAIN_ONE + 1])
        d_resid[...] = grad
        d_attn = grad.astype(BF)
        sums[2:3] = column_sum(d_attn.astype(F32))
        g_out[...] = dot_tn(context[...], d_attn).astype(BF)
        d_context[...] = dot_nt(d_attn, w_out[0]).astype(BF)


def backward(d_ffn, d_second, first, normed, inv_std, context, vectors, full, active, slope):
    rows = context.shape[0]
    per = D // CHUNK
    whole = lambda *shape: pl.BlockSpec(shape, lambda i: (0,) * len(shape))
    wide = pl.BlockSpec((1, rows, HALF), lambda i: (i, 0, 0))
    return pl.pallas_call(
        backward_kernel,
        grid=(CHUNKS,),
        out_shape=(
            jax.ShapeDtypeStruct((FF, D), BF),
            jax.ShapeDtypeStruct((D, FF), BF),
            jax.ShapeDtypeStruct((1, FF), F32),
            jax.ShapeDtypeStruct((D, D), BF),
            jax.ShapeDtypeStruct((rows, D), F32),
            jax.ShapeDtypeStruct((rows, D), BF),
            jax.ShapeDtypeStruct((3, D), F32),
        ),
        in_specs=[
            whole(rows, D),
            whole(rows, D),
            whole(rows, D),
            whole(rows, D),
            whole(rows, LANES),
            whole(rows, D),
            whole(VEC_ROWS, D),
            pl.BlockSpec((1, D, D), lambda i: (3, 0, 0)),
            wide,
            wide,
            pl.BlockSpec((1, D, CHUNK), lambda i: (UP + 2 * (i // per), 0, i % per)),
            pl.BlockSpec((1, CHUNK, D), lambda i: (DOWN + 2 * (i // per), i % per, 0)),
        ],
        out_specs=(
            pl.BlockSpec((CHUNK, D), lambda i: (i, 0)),
            pl.BlockSpec((D, CHUNK), lambda i: (0, i)),
            pl.BlockSpec((1, CHUNK), lambda i: (0, i)),
            whole(D, D),
            whole(rows, D),
            whole(rows, D),
            whole(3, D),
        ),
        scratch_shapes=[pltpu.VMEM((rows, D), F32)],
        compiler_params=pltpu.CompilerParams(vmem_limit_bytes=VMEM),
        name="backward",
    )(d_ffn, d_second, first, normed, inv_std, context, vectors, full, active, slope, full, full)


def project_back_kernel(tokens, d_joined, d_resid, weight, g_qkv, g_bias, input_grad):
    step = pl.program_id(0)
    low = d_joined[...]
    g_qkv[...] = dot_tn(tokens[...], low).astype(BF)
    g_bias[...] = column_sum(low.astype(F32))
    part = dot_nt(low, weight[0])

    @pl.when(step == 0)
    def _():
        input_grad[...] = d_resid[...] + part

    @pl.when(step > 0)
    def _():
        input_grad[...] += part


def project_back(tokens_all, d_joined, d_resid, full):
    rows = d_joined.shape[0]
    per = D // CHUNK
    whole = lambda *shape: pl.BlockSpec(shape, lambda i: (0,) * len(shape))
    return pl.pallas_call(
        project_back_kernel,
        grid=(3 * per,),
        out_shape=(
            jax.ShapeDtypeStruct((D, 3 * D), BF),
            jax.ShapeDtypeStruct((1, 3 * D), F32),
            jax.ShapeDtypeStruct((rows, D), F32),
        ),
        in_specs=[
            whole(rows, D),
            pl.BlockSpec((rows, CHUNK), lambda i: (0, i)),
            whole(rows, D),
            pl.BlockSpec((1, D, CHUNK), lambda i: (i // per, 0, i % per)),
        ],
        out_specs=(
            pl.BlockSpec((D, CHUNK), lambda i: (0, i)),
            pl.BlockSpec((1, CHUNK), lambda i: (0, i)),
            whole(rows, D),
        ),
        compiler_params=pltpu.CompilerParams(vmem_limit_bytes=VMEM),
        name="project_back",
    )(tokens_all, d_joined, d_resid, full)


def rope_tables(count):
    position = np.arange(count, dtype=np.float32)
    frequency = np.exp(np.arange(HEAD_DIM // 2, dtype=np.float32) * np.float32(-2.0 * math.log(10000.0) / HEAD_DIM))
    angles = position[:, None] * frequency[None, :].astype(np.float32)
    cosine, sine = np.cos(angles).astype(np.float32), np.sin(angles).astype(np.float32)
    return (
        jnp.asarray(np.concatenate([cosine] * 4, axis=1)),
        jnp.asarray(np.concatenate([-sine, sine, -sine, sine], axis=1)),
    )


def local(
    tokens,
    segments,
    cotangent,
    w_qkv,
    b_qkv,
    w_out,
    b_out,
    gain_one,
    shift_one,
    w_up,
    b_up,
    w_down,
    b_down,
    gain_two,
    shift_two,
):
    rows = tokens.shape[0]
    shards = lax.axis_size("shard")
    hi_count = shards // 4
    depth = D // shards
    small = (b_qkv, b_out, gain_one, shift_one, b_up, b_down, gain_two, shift_two)
    widths = [a.shape[0] for a in small]
    vec = jnp.concatenate(small).astype(BF).reshape(-1, depth)
    vec = jnp.tile(jnp.pad(vec, ((0, VEC_ROWS - vec.shape[0]), (0, 0))), (1, LANES // depth))
    lane = jnp.arange(LANES, dtype=jnp.int32)[None, :]
    q_doc = (segments[:, None] == lane).astype(BF)
    cosine, sine = rope_tables(2 * rows)
    (
        full, q, k, v, q_ext, active, slope, k_doc, context, first, normed, inv_std, result,
        d_second, d_ffn, sums_two, vectors,
    ) = forward(hi_count, (w_qkv, w_out, w_up, w_down), vec[None], tokens, cotangent, q_doc, cosine, sine)
    full = full.reshape(SLABS, D, D)
    g_down, g_up, g_b_up, g_out, d_resid, d_context, sums_one = backward(
        d_ffn, d_second, first, normed, inv_std, context, vectors, full, active, slope
    )
    half = lax.axis_index("rep")
    cosine, sine = jnp.roll(cosine, half * rows, axis=0), jnp.roll(sine, half * rows, axis=0)
    d_q, d_k, d_v = attend_back(q, k, v, context, d_context, q_ext, k_doc, cosine, sine)
    peer = lax.ppermute(
        jnp.concatenate([d_k[rows:], d_v[rows:]], axis=1), "rep", [(0, 1), (1, 0)]
    ).astype(F32)
    own = jnp.concatenate([d_k[:rows], d_v[:rows]], axis=1).astype(F32)
    d_joined = jnp.concatenate([d_q, (own + peer).astype(BF)], axis=1)
    g_qkv, g_b_qkv, input_grad = project_back(tokens, d_joined, d_resid, full)

    g_b_up = g_b_up.reshape(4, shards, depth).transpose(1, 0, 2)
    g_small = (
        g_b_qkv,
        sums_one[2],
        sums_one[0],
        sums_one[1],
        g_b_up,
        sums_two[2],
        sums_two[0],
        sums_two[1],
    )
    g_vec = jnp.concatenate([a.reshape(shards, -1) for a in g_small], axis=1)
    g_vec = jnp.pad(g_vec, ((0, 0), (0, -g_vec.shape[1] % (8 * LANES))))
    total, vec_total = scatter(
        hi_count, g_qkv, g_out, g_up, g_down, g_vec.reshape(shards, -1, LANES)
    )
    vec_total = vec_total.reshape(-1)
    outs = []
    at = 0
    for width in widths:
        outs.append(vec_total[at : at + width])
        at += width
    grad_qkv = total[0:3].transpose(1, 0, 2).reshape(depth, 3 * D)
    grad_up = total[4:8].reshape(4, depth, shards, depth).transpose(1, 2, 0, 3).reshape(depth, FF)
    grad_down = total[8:12].reshape(4 * depth, D)
    return (
        result,
        input_grad,
        grad_qkv,
        outs[0],
        total[3],
        outs[1],
        outs[2],
        outs[3],
        grad_up,
        outs[4],
        grad_down,
        outs[5],
        outs[6],
        outs[7],
    )


def solution(mesh):
    act = P(("shard", "rep"), None)
    matrix = P("shard", None)
    vector = P("shard")
    params = (matrix, vector, matrix, vector, vector, vector, matrix, vector, matrix, vector, vector, vector)
    return jax.shard_map(
        local,
        mesh=mesh,
        in_specs=(act, P(("shard", "rep")), act) + params,
        out_specs=(act, act) + params,
        check_vma=False,
    )
```

```python
import functools
import math

import jax
import jax.numpy as jnp
import numpy as np
from jax import lax
from jax.experimental import pallas as pl
from jax.experimental.pallas import tpu as pltpu
from jax.sharding import PartitionSpec as P

D = 1024
HEADS = 16
HEAD_DIM = 64
FF = 4096
SLABS = 12
LANES = 128
MASKED = -1e30
MESH = pl.DeviceIdType.MESH
VMEM = 60 * 1024 * 1024
BF = jnp.bfloat16
F32 = jnp.float32

ERFC_P = 0.33
ERFC_Q = (
    0.1863661,
    0.182837329,
    0.20192357,
    0.0450108379,
    0.412542064,
    -0.355440048,
    0.462689118,
    -0.135929052,
)


def dot(a, b):
    return lax.dot_general(a, b, (((1,), (0,)), ((), ())), preferred_element_type=F32)


def dot_nt(a, b):
    return lax.dot_general(a, b, (((1,), (1,)), ((), ())), preferred_element_type=F32)


def dot_tn(a, b):
    return lax.dot_general(a, b, (((0,), (0,)), ((), ())), preferred_element_type=F32)


def swap_halves(a):
    width = a.shape[1]
    lane = lax.broadcasted_iota(jnp.int32, a.shape, 1) % HEAD_DIM
    return jnp.where(
        lane < HEAD_DIM // 2,
        pltpu.roll(a, width - HEAD_DIM // 2, 1),
        pltpu.roll(a, HEAD_DIM // 2, 1),
    )


def split3(a):
    hi = a.astype(BF)
    rest = a - hi.astype(F32)
    mid = rest.astype(BF)
    low = (rest - mid.astype(F32)).astype(BF)
    return hi, mid, low


def remote(src, dst, send, recv, device):
    return pltpu.make_async_remote_copy(
        src_ref=src, dst_ref=dst, send_sem=send, recv_sem=recv, device_id=device, device_id_type=MESH
    )


def place(hi_count):
    index = lax.axis_index("shard")
    return index // 4, (index // 2) % 2, index % 2, lax.axis_index("rep")


def shard_of(hi, mid, core):
    return {"shard": hi * 4 + mid * 2 + core}


def entry_barrier(hi_count, hi, mid, core, rep):
    barrier = pltpu.get_barrier_semaphore()
    for m in range(1, hi_count):
        pl.semaphore_signal(
            barrier, inc=1, device_id=shard_of((hi + m) % hi_count, mid, core), device_id_type=MESH
        )
    pl.semaphore_signal(barrier, inc=1, device_id=shard_of(hi, 1 - mid, core), device_id_type=MESH)
    pl.semaphore_signal(barrier, inc=1, device_id=shard_of(hi, mid, 1 - core), device_id_type=MESH)
    pl.semaphore_signal(barrier, inc=1, device_id={"rep": 1 - rep}, device_id_type=MESH)
    pl.semaphore_wait(barrier, hi_count + 2)


SWAP = 256
PARTS = 2


def normed_rows(residual):
    mean_val = jnp.mean(residual, axis=-1, keepdims=True)
    centred = residual - mean_val
    variance = jnp.mean(centred * centred, axis=-1, keepdims=True)
    inv_std = lax.rsqrt(variance + 1e-05)
    return centred * inv_std, inv_std


def norm_back(upstream, normed, inv_std, gain_vec):
    scaled = upstream * gain_vec
    return inv_std * (
        scaled
        - jnp.mean(scaled, axis=-1, keepdims=True)
        - normed * jnp.mean(scaled * normed, axis=-1, keepdims=True)
    )


def column_sum(a):
    return jnp.sum(a, axis=0, keepdims=True)


class Gather:
    def __init__(self, hi_count, packed, full, sems, swap=SWAP):
        self.hi_count = hi_count
        self.packed, self.full = packed, full
        (self.up_send, self.up_recv, self.down_send, self.down_recv, self.y_send, self.y_recv,
         self.x_send, self.x_recv, self.c_send, self.c_recv) = sems
        self.hi, self.mid, self.core, self.rep = place(hi_count)
        slabs, self.depth, width = packed.shape
        self.parts = self.parts_of(self.depth, swap)
        self.rows = self.depth // self.parts
        self.count = slabs * self.parts
        self.swap = swap
        self.mine = slice(None)
        if swap:
            self.mine = pl.ds(pl.multiple_of(self.rep * swap, LANES), width - swap)

    @staticmethod
    def parts_of(depth, swap):
        return PARTS if swap and depth % (16 * PARTS) == 0 else 1

    @staticmethod
    def scratch(hi_count, slabs, depth, swap=SWAP):
        count = slabs * Gather.parts_of(depth, swap)
        dma = pltpu.SemaphoreType.DMA
        hops = dma((count, hi_count - 1))
        return [hops] * 4 + [dma((count,))] * 4 + [dma((count, 2))] * 2

    def only(self, which):
        return pl.ds(pl.multiple_of(which * (D - self.swap), LANES), self.swap)

    def spot(self, chunk):
        start = (chunk % self.parts) * self.rows
        if not isinstance(start, int):
            start = pl.multiple_of(start, self.rows)
        return chunk // self.parts, pl.ds(start, self.rows)

    def hop(self, chunk, distance, up):
        slab, rows = self.spot(chunk)
        origin = self.hi - distance if up else self.hi + distance
        block = self.full.at[slab, origin, self.mid, self.core, rows, self.mine]
        source = self.packed.at[slab, rows, self.mine] if distance == 0 else block
        send, recv = (self.up_send, self.up_recv) if up else (self.down_send, self.down_recv)
        device = shard_of(self.hi + 1 if up else self.hi - 1, self.mid, self.core)
        return remote(source, block, send.at[chunk, distance], recv.at[chunk, distance], device)

    def landed_hop(self, chunk, distance, up):
        slab, rows = self.spot(chunk)
        origin = self.hi - distance - 1 if up else self.hi + distance + 1
        block = self.full.at[slab, origin, self.mid, self.core, rows, self.mine]
        send, recv = (self.up_send, self.up_recv) if up else (self.down_send, self.down_recv)
        device = shard_of(self.hi, self.mid, self.core)
        return remote(block, block, send.at[chunk, distance], recv.at[chunk, distance], device)

    def sends(self, distance, up):
        if up:
            return (self.hi - distance >= 0) & (self.hi + 1 < self.hi_count)
        return (self.hi + distance < self.hi_count) & (self.hi - 1 >= 0)

    def lands(self, distance, up):
        if up:
            return self.hi - distance - 1 >= 0
        return self.hi + distance + 1 < self.hi_count

    def y_copy(self, chunk, landed):
        slab, rows = self.spot(chunk)
        which = 1 - self.mid if landed else self.mid
        block = self.full.at[slab, :, which, self.core, rows, self.mine]
        device = shard_of(self.hi, 1 - self.mid, self.core)
        return remote(block, block, self.y_send.at[chunk], self.y_recv.at[chunk], device)

    def x_copy(self, chunk, landed):
        slab, rows = self.spot(chunk)
        columns = self.only(1 - self.rep if landed else self.rep)
        block = self.full.at[slab, :, :, self.core, rows, columns]
        return remote(block, block, self.x_send.at[chunk], self.x_recv.at[chunk], {"rep": 1 - self.rep})

    def c_copy(self, chunk, part, landed):
        slab, rows = self.spot(chunk)
        which = 1 - self.core if landed else self.core
        columns = self.mine if part == 0 else self.only(1 - self.rep)
        block = self.full.at[slab, :, :, which, rows, columns]
        device = shard_of(self.hi, self.mid, 1 - self.core)
        return remote(block, block, self.c_send.at[chunk, part], self.c_recv.at[chunk, part], device)

    @property
    def lag(self):
        return 2 * self.hi_count + 4

    def own_copy(self, sem):
        target = self.full.at[:, self.hi, self.mid, self.core, :, self.mine]
        return pltpu.make_async_copy(self.packed.at[:, :, self.mine], target, sem)

    def tick(self, t):
        def stage(offset, act):
            if not isinstance(t, int):
                chunk = t - offset
                pl.when((chunk >= 0) & (chunk < self.count))(lambda: act(chunk))
            elif 0 <= t - offset < self.count:
                act(t - offset)

        def own(chunk):
            for up in (True, False):
                pl.when(self.sends(0, up))(lambda: self.hop(chunk, 0, up).start())

        def forward(distance, chunk):
            for up in (True, False):
                pl.when(self.lands(distance - 1, up))(
                    lambda: self.landed_hop(chunk, distance - 1, up).wait_recv()
                )
                if distance < self.hi_count - 1:
                    pl.when(self.sends(distance, up))(lambda: self.hop(chunk, distance, up).start())
            if distance == self.hi_count - 1:
                self.y_copy(chunk, False).start()

        def after_y(chunk):
            self.y_copy(chunk, True).wait_recv()
            if self.swap:
                self.x_copy(chunk, False).start()
            self.c_copy(chunk, 0, False).start()

        def after_x(chunk):
            if self.swap:
                self.x_copy(chunk, True).wait_recv()
                self.c_copy(chunk, 1, False).start()

        def after_c(chunk):
            for part in range(2 if self.swap else 1):
                self.c_copy(chunk, part, True).wait_recv()

        stage(0, own)
        for distance in range(1, self.hi_count):
            stage(2 * distance, functools.partial(forward, distance))
        stage(2 * self.hi_count, after_y)
        stage(2 * self.hi_count + 2, after_x)
        stage(2 * self.hi_count + 4, after_c)

    def drain(self):
        @pl.loop(0, self.count)
        def _(chunk):
            for distance in range(self.hi_count - 1):
                for up in (True, False):
                    pl.when(self.sends(distance, up))(
                        lambda: self.hop(chunk, distance, up).wait_send()
                    )
            self.y_copy(chunk, False).wait_send()
            if self.swap:
                self.x_copy(chunk, False).wait_send()
            for part in range(2 if self.swap else 1):
                self.c_copy(chunk, part, False).wait_send()


def near_barrier(hi_count):
    hi, mid, core, rep = place(hi_count)
    barrier = pltpu.get_barrier_semaphore()

    def greet(device):
        pl.semaphore_signal(barrier, inc=1, device_id=device, device_id_type=MESH)

    pl.when(hi + 1 < hi_count)(lambda: greet(shard_of(hi + 1, mid, core)))
    pl.when(hi - 1 >= 0)(lambda: greet(shard_of(hi - 1, mid, core)))
    greet(shard_of(hi, 1 - mid, core))
    greet(shard_of(hi, mid, 1 - core))
    greet({"rep": 1 - rep})
    first, last = hi == 0, hi == hi_count - 1
    pl.semaphore_wait(barrier, 5 - first.astype(jnp.int32) - last.astype(jnp.int32))


UP, DOWN = 4, 5
HALF = D // 2
QUAD = 4 * HEAD_DIM
B_OUT, GAIN_ONE, SHIFT_ONE, B_UP, B_DOWN, GAIN_TWO, SHIFT_TWO = 3, 4, 5, 6, 10, 11, 12
VEC_ROWS = 16


def regroup(pieces, depth):
    out = None
    for u, (tile, start) in enumerate(pieces):
        shift = (u * depth - start) % LANES
        moved = pltpu.roll(tile, shift, 1) if shift else tile
        lane = lax.broadcasted_iota(jnp.int32, moved.shape, 1)
        out = moved if out is None else jnp.where(lane // depth == u, moved, out)
    return out


def tile_of(at):
    return slice(at // LANES * LANES, at // LANES * LANES + LANES)


def pack(packed, w_qkv, w_out, w_up, w_down):
    depth = w_qkv.shape[0]
    for slab in range(3):
        packed[slab] = w_qkv[:, slab * D : (slab + 1) * D].astype(BF)
    packed[3] = w_out[...].astype(BF)
    each = LANES // depth
    for j in range(4):
        packed[DOWN + 2 * j] = w_down[j * depth : (j + 1) * depth].astype(BF)
        for t in range(D // LANES):
            starts = [4 * depth * (t * each + u) + depth * j for u in range(each)]
            pieces = [(w_up[:, tile_of(at)], at % LANES) for at in starts]
            packed[UP + 2 * j, :, t * LANES : (t + 1) * LANES] = regroup(pieces, depth).astype(BF)


def unpack_vectors(vec_full, rows_out, bias, depth):
    hi_count = vec_full.shape[1]
    each = LANES // depth

    def of_shard(shard):
        return vec_full[0, shard // 4, shard // 2 % 2, shard % 2].astype(F32)

    def join(pieces):
        lane = lax.broadcasted_iota(jnp.int32, pieces[0].shape, 1)
        out = pieces[0]
        for u in range(1, each):
            out = jnp.where(lane // depth == u, pieces[u], out)
        return out

    for t in range(D // LANES):
        tile = slice(t * LANES, (t + 1) * LANES)
        rows_out[:, tile] = join([of_shard(t * each + u) for u in range(each)])
        for j in range(3):
            chunks = [(j * D + t * LANES) // depth + u for u in range(each)]
            bias[j : j + 1, tile] = join([of_shard(m // 3)[m % 3 : m % 3 + 1] for m in chunks])


def gelu_parts(hidden):
    gauss = jnp.exp(hidden * hidden * -0.5)
    t = 1.0 / (1.0 + (ERFC_P * math.sqrt(0.5)) * jnp.abs(hidden))
    poly = jnp.full_like(t, ERFC_Q[-1])
    for coefficient in ERFC_Q[-2::-1]:
        poly = poly * t + coefficient
    tail = 0.5 * t * poly * gauss
    cdf = jnp.where(hidden >= 0, 1.0 - tail, tail)
    return hidden * cdf, cdf + hidden * gauss * (1.0 / math.sqrt(2.0 * math.pi))


def forward_kernel(
    hi_count,
    w_qkv,
    w_out,
    w_up,
    w_down,
    vec,
    tokens,
    cotangent,
    q_doc,
    cosine,
    sine,
    full,
    q_all,
    k_all,
    v_all,
    q_ext_all,
    active_all,
    slope_all,
    x_all,
    k_doc,
    context,
    first_low,
    normed_out,
    inv_out,
    result,
    d_second,
    d_ffn,
    sums,
    vectors,
    packed,
    vec_full,
    x_peer,
    slots,
    q_buf,
    k_buf,
    v_buf,
    ext_buf,
    first,
    total,
    act_buf,
    slope_buf,
    bias,
    local_sem,
    load_sem,
    flush_sem,
    t_sem,
    *sems,
):
    rows = tokens.shape[0]
    depth = w_qkv.shape[0]
    rep = lax.axis_index("rep")
    gather = Gather(hi_count, packed, full, sems[:10])
    small = Gather(hi_count, vec, vec_full, sems[10:], swap=0)
    lane_doc = lax.broadcasted_iota(jnp.int32, (rows, LANES), 1)
    other = jnp.where(q_doc[...] > 0.5, 0.0, MASKED)
    other = jnp.where(lane_doc < 61, other, jnp.where(lane_doc < 64, 1.0, 0.0))
    k_doc[:rows] = other.astype(BF)
    pack(packed, w_qkv, w_out, w_up, w_down)
    near_barrier(hi_count)
    peer = {"rep": 1 - rep}
    token_copy = remote(tokens, x_peer, t_sem.at[0], t_sem.at[1], peer)
    doc_copy = remote(k_doc.at[:rows], k_doc.at[rows:], t_sem.at[2], t_sem.at[3], peer)
    copies = [small.own_copy(local_sem.at[0]), gather.own_copy(local_sem.at[1])]
    for copy in copies:
        copy.start()
    doc_copy.start()
    token_copy.start()
    for copy in copies:
        copy.wait()
    warm = gather.lag + 1
    for t in range(warm):
        small.tick(t)
        gather.tick(t)
    unpack_vectors(vec_full, vectors, bias, depth)
    doc_copy.wait()
    token_copy.wait()
    x_copies = [
        pltpu.make_async_copy(tokens, x_all.at[:rows], local_sem.at[0]),
        pltpu.make_async_copy(x_peer, x_all.at[rows:], local_sem.at[1]),
    ]
    for copy in x_copies:
        copy.start()
    ready = 3 * gather.parts + gather.lag

    @pl.loop(warm, ready)
    def _(t):
        gather.tick(t)

    def load_whole(slab, slot):
        return pltpu.make_async_copy(full.at[slab], slots.at[slot], load_sem.at[slot])

    for slab in range(3):
        load_whole(slab, slab).start()
    for slab in range(3):
        load_whole(slab, slab).wait()

    def weight(slot, columns):
        return slots[slot, :, :, :, :, columns].reshape(D, -1)

    own_rows = pl.ds(pl.multiple_of(rep * rows, rows), rows)
    peer_rows = pl.ds(pl.multiple_of((1 - rep) * rows, rows), rows)

    def rope(a, table_rows):
        cos_part, sin_part = cosine[table_rows, :], sine[table_rows, :]
        cos_part = jnp.concatenate([cos_part, cos_part], axis=1)
        sin_part = jnp.concatenate([sin_part, sin_part], axis=1)
        return a * cos_part + swap_halves(a) * sin_part

    def flushes(i):
        return [
            pltpu.make_async_copy(q_buf.at[i], q_all.at[i], flush_sem.at[0, i]),
            pltpu.make_async_copy(k_buf.at[i], k_all.at[i], flush_sem.at[1, i]),
            pltpu.make_async_copy(v_buf.at[i], v_all.at[i], flush_sem.at[2, i]),
            pltpu.make_async_copy(
                ext_buf.at[pl.ds(4 * i, 4)], q_ext_all.at[pl.ds(4 * i, 4)], flush_sem.at[3, i]
            ),
        ]

    ones = jnp.ones((2 * rows, LANES), BF)
    piece = 256

    @pl.loop(0, HEADS // 4)
    def _(i):
        columns = pl.ds(pl.multiple_of(i * QUAD, QUAD), QUAD)
        own_x, peer_x = tokens[...], x_peer[...]
        w = weight(0, columns)
        q_rows = rope(dot(own_x, w) + bias[0:1, columns], own_rows) * HEAD_DIM**-0.5
        q_buf[i] = q_rows.astype(BF)
        w = weight(1, columns)
        k_buf[i, :rows] = rope(dot(own_x, w) + bias[1:2, columns], own_rows).astype(BF)
        k_buf[i, rows:] = rope(dot(peer_x, w) + bias[1:2, columns], peer_rows).astype(BF)
        w = weight(2, columns)
        v_buf[i, :rows] = (dot(own_x, w) + bias[2:3, columns]).astype(BF)
        v_buf[i, rows:] = (dot(peer_x, w) + bias[2:3, columns]).astype(BF)
        for pair in range(2):
            gather.tick(ready + 2 * i + pair)
            lanes = slice(pair * LANES, (pair + 1) * LANES)
            keys = jnp.concatenate([k_buf[i, :, lanes], k_doc[...]], axis=1)
            values = jnp.concatenate([v_buf[i, :, lanes], ones], axis=1)
            for start in range(0, rows, piece):
                part = slice(start, start + piece)
                q_pair = q_buf[i, part, lanes]
                lane = lax.broadcasted_iota(jnp.int32, q_pair.shape, 1)
                doc_q = q_doc[part, :]
                mixed = []
                for head in range(2):
                    in_head = (lane // HEAD_DIM) == head
                    queries = jnp.concatenate([jnp.where(in_head, q_pair, 0), doc_q], axis=1)
                    scores = dot_nt(queries, keys)
                    row_max = jnp.max(scores, axis=1, keepdims=True)
                    prob = jnp.exp(scores - row_max).astype(BF)
                    both = dot(prob, values)
                    row_sum = both[:, LANES:]
                    mixed.append(both[:, :LANES] / row_sum)
                    hi, mid, low = split3(-(row_max + jnp.log(row_sum)))
                    ext = jnp.where(lane == 61, hi, doc_q)
                    ext = jnp.where(lane == 62, mid, ext)
                    ext = jnp.where(lane == 63, low, ext)
                    ext_buf[4 * i + pair * 2 + head, part, :] = ext
                pair_lanes = pl.ds(pl.multiple_of(i * QUAD + pair * LANES, LANES), LANES)
                context[part, pair_lanes] = jnp.where(lane < HEAD_DIM, mixed[0], mixed[1]).astype(BF)
        for copy in flushes(i):
            copy.start()

    done = ready + HEADS // 2

    def vector(row):
        return vectors[row : row + 1, :]

    load_whole(3, 3).start()
    for slot in range(2):
        load_whole(UP + slot, slot).start()
    load_whole(3, 3).wait()
    attn = dot(context[...], weight(3, slice(None))) + vector(B_OUT)
    normed, inv_std = normed_rows(tokens[...].astype(F32) + attn)
    first[...] = normed * vector(GAIN_ONE) + vector(SHIFT_ONE)
    first_low[...] = first[...].astype(BF)
    normed_out[...] = normed
    inv_out[...] = jnp.broadcast_to(inv_std, inv_out.shape)
    total[...] = first[...] + vector(B_DOWN)

    def keeps(j, half):
        return [
            pltpu.make_async_copy(
                act_buf.at[half], active_all.at[2 * j + half], flush_sem.at[4, 2 * half]
            ),
            pltpu.make_async_copy(
                slope_buf.at[half], slope_all.at[2 * j + half], flush_sem.at[4, 2 * half + 1]
            ),
        ]

    @pl.loop(0, 4)
    def _(j):
        base = lax.rem(j, 2) * 2

        for slot in range(2):
            load_whole(UP + 2 * j + slot, base + slot).wait()
        for half in range(2):
            @pl.when(j > 0)
            def _():
                for copy in keeps(j - 1, half):
                    copy.wait()

            columns = slice(half * HALF, (half + 1) * HALF)
            hidden = dot(first_low[...], weight(base, columns)) + vectors[pl.ds(B_UP + j, 1), columns]
            act, slope = gelu_parts(hidden)
            act_buf[half] = act.astype(BF)
            slope_buf[half] = slope.astype(BF)
            down = slots[base + 1, half * (hi_count // 2) : (half + 1) * (hi_count // 2)].reshape(HALF, D)
            total[...] += dot(act_buf[half], down)
            for copy in keeps(j, half):
                copy.start()
            for step in range(2):
                t = 6 * gather.parts + gather.lag + 2 * gather.parts * j + gather.parts * half + step
                if step < gather.parts:
                    pl.when(t >= done)(lambda: gather.tick(t))

        @pl.when(j < 3)
        def _():
            for slot in range(2):
                load_whole(UP + 2 * j + 2 + slot, 2 - base + slot).start()

    for half in range(2):
        for copy in keeps(3, half):
            copy.wait()
    gain = vector(GAIN_TWO)
    normed, inv_std = normed_rows(total[...])
    result[...] = (normed * gain + vector(SHIFT_TWO)).astype(BF)
    up = cotangent[...].astype(F32)
    sums[1:2] = column_sum(up * normed)
    sums[2:3] = column_sum(up)
    grad = norm_back(up, normed, inv_std, gain)
    d_second[...] = grad
    low = grad.astype(BF)
    d_ffn[...] = low
    sums[0:1] = column_sum(low.astype(F32))
    for copy in x_copies:
        copy.wait()
    small.drain()
    gather.drain()

    @pl.loop(0, HEADS // 4)
    def _(i):
        for copy in flushes(i):
            copy.wait()


def forward(hi_count, weights, vec, tokens, cotangent, q_doc, cosine, sine):
    rows = tokens.shape[0]
    depth = weights[0].shape[0]
    anywhere = pl.BlockSpec(memory_space=pl.ANY)
    vmem = pl.BlockSpec(memory_space=pltpu.VMEM)
    dma = pltpu.SemaphoreType.DMA
    quads = HEADS // 4
    shape = jax.ShapeDtypeStruct
    blocks = (hi_count, 2, 2, depth, D)
    return pl.pallas_call(
        functools.partial(forward_kernel, hi_count),
        out_shape=(
            shape((SLABS,) + blocks, BF),
            shape((quads, rows, QUAD), BF),
            shape((quads, 2 * rows, QUAD), BF),
            shape((quads, 2 * rows, QUAD), BF),
            shape((HEADS, rows, LANES), BF),
            shape((8, rows, HALF), BF),
            shape((8, rows, HALF), BF),
            shape((2 * rows, D), BF),
            shape((2 * rows, LANES), BF),
            shape((rows, D), BF),
            shape((rows, D), BF),
            shape((rows, D), F32),
            shape((rows, LANES), F32),
            shape((rows, D), BF),
            shape((rows, D), F32),
            shape((rows, D), BF),
            shape((3, D), F32),
            shape((VEC_ROWS, D), F32),
        ),
        in_specs=[vmem] * 10,
        out_specs=(anywhere,) * 8 + (vmem,) * 10,
        scratch_shapes=[
            pltpu.VMEM((SLABS, depth, D), BF),
            pltpu.VMEM((1, hi_count, 2, 2) + vec.shape[1:], BF),
            pltpu.VMEM((rows, D), BF),
            pltpu.VMEM((4,) + blocks, BF),
            pltpu.VMEM((quads, rows, QUAD), BF),
            pltpu.VMEM((quads, 2 * rows, QUAD), BF),
            pltpu.VMEM((quads, 2 * rows, QUAD), BF),
            pltpu.VMEM((HEADS, rows, LANES), BF),
            pltpu.VMEM((rows, D), F32),
            pltpu.VMEM((rows, D), F32),
            pltpu.VMEM((2, rows, HALF), BF),
            pltpu.VMEM((2, rows, HALF), BF),
            pltpu.VMEM((3, D), F32),
            dma((2,)),
            dma((4,)),
            dma((5, quads)),
            dma((4,)),
        ]
        + Gather.scratch(hi_count, SLABS, depth)
        + Gather.scratch(hi_count, 1, vec.shape[1], swap=0),
        compiler_params=pltpu.CompilerParams(
            collective_id=0, has_side_effects=True, vmem_limit_bytes=VMEM
        ),
        name="forward",
    )(*weights, vec, tokens, cotangent, q_doc, cosine, sine)


RING = 8


class Scatter:
    stages = (0, 2, 4, 6, 8)

    def __init__(self, hi_count, depth, grads, from_core, bufs, sems):
        self.hi_count, self.depth = hi_count, depth
        self.grads, self.from_core = grads, from_core
        self.held, self.staged, self.from_x, self.from_y, self.from_z, self.own, self.other = bufs
        (self.load_sem, self.c_send, self.c_recv, self.x_send, self.x_recv, self.y_send, self.y_recv,
         self.z_send, self.z_recv, self.f_send, self.f_recv) = sems
        self.hi, self.mid, self.core, self.rep = place(hi_count)
        self.parts = Gather.parts_of(depth, SWAP)
        self.rows = depth // self.parts
        self.count = SLABS * self.parts
        self.lag = self.stages[-1]
        self.width = D - SWAP

    @staticmethod
    def scratch(hi_count, depth):
        parts = Gather.parts_of(depth, SWAP)
        count, rows = SLABS * parts, depth // parts
        dma = pltpu.SemaphoreType.DMA
        bufs = [
            pltpu.VMEM((RING, hi_count, 2, rows, D), BF),
            pltpu.VMEM((hi_count, 2, rows, D), BF),
            pltpu.VMEM((count, hi_count, 2, rows, SWAP), BF),
            pltpu.VMEM((count, hi_count, rows, D - SWAP), BF),
            pltpu.VMEM((count, hi_count - 1, rows, D - SWAP), BF),
            pltpu.VMEM((count, rows, D), BF),
            pltpu.VMEM((count, rows, D), BF),
        ]
        sems = [dma((2,))] + [dma((count,))] * 6 + [dma((count, hi_count - 1))] * 2 + [dma((count,))] * 2
        return bufs, sems

    def columns(self, which):
        return pl.ds(pl.multiple_of(which * SWAP, LANES), self.width)

    def only(self, which):
        return pl.ds(pl.multiple_of(which * self.width, LANES), SWAP)

    def block(self, chunk, which):
        start = (chunk % self.parts) * self.rows
        if not isinstance(start, int):
            start = pl.multiple_of(start, self.rows)
        return self.grads.at[chunk // self.parts, :, :, which, pl.ds(start, self.rows)]

    def c_copy(self, chunk):
        return remote(
            self.block(chunk, 1 - self.core),
            self.from_core.at[chunk],
            self.c_send.at[chunk],
            self.c_recv.at[chunk],
            shard_of(self.hi, self.mid, 1 - self.core),
        )

    def loads(self, chunk):
        return [
            pltpu.make_async_copy(
                self.block(chunk, self.core), self.held.at[chunk % RING], self.load_sem.at[0]
            ),
            pltpu.make_async_copy(self.from_core.at[chunk], self.staged, self.load_sem.at[1]),
        ]

    def x_copy(self, chunk):
        return remote(
            self.held.at[chunk % RING, :, :, :, self.only(1 - self.rep)],
            self.from_x.at[chunk],
            self.x_send.at[chunk],
            self.x_recv.at[chunk],
            {"rep": 1 - self.rep},
        )

    def y_copy(self, chunk):
        return remote(
            self.held.at[chunk % RING, :, 1 - self.mid, :, self.columns(self.rep)],
            self.from_y.at[chunk],
            self.y_send.at[chunk],
            self.y_recv.at[chunk],
            shard_of(self.hi, 1 - self.mid, self.core),
        )

    def z_copy(self, chunk, m):
        there = (self.hi + m) % self.hi_count
        return remote(
            self.held.at[chunk % RING, there, self.mid, :, self.columns(self.rep)],
            self.from_z.at[chunk, m - 1],
            self.z_send.at[chunk, m - 1],
            self.z_recv.at[chunk, m - 1],
            shard_of(there, self.mid, self.core),
        )

    def f_copy(self, chunk, landed):
        columns = self.columns(1 - self.rep if landed else self.rep)
        source = self.other if landed else self.own
        return remote(
            source.at[chunk, :, columns],
            self.other.at[chunk, :, columns],
            self.f_send.at[chunk],
            self.f_recv.at[chunk],
            {"rep": 1 - self.rep},
        )

    def hand_over(self, slab):
        for part in range(self.parts):
            self.c_copy(slab * self.parts + part).start()

    def free(self, chunk):
        self.x_copy(chunk).wait_send()
        self.y_copy(chunk).wait_send()
        for m in range(1, self.hi_count):
            self.z_copy(chunk, m).wait_send()

    def tick(self, t):
        def stage(number, act):
            chunk = t - self.stages[number]
            if isinstance(chunk, int):
                if 0 <= chunk < self.count:
                    act(chunk)
            else:
                pl.when((chunk >= 0) & (chunk < self.count))(lambda: act(chunk))

        def begin(chunk):
            self.c_copy(chunk).wait_recv()
            if isinstance(chunk, int):
                if chunk >= RING:
                    self.free(chunk - RING)
            else:
                pl.when(chunk >= RING)(lambda: self.free(chunk - RING))
            for copy in self.loads(chunk):
                copy.start()

        def add_core(chunk):
            for copy in self.loads(chunk):
                copy.wait()
            slot = chunk % RING

            @pl.loop(0, self.hi_count)
            def _(h):
                for m in range(2):
                    self.held[slot, h, m] = (
                        self.held[slot, h, m].astype(F32) + self.staged[h, m].astype(F32)
                    ).astype(BF)

            self.x_copy(chunk).start()

        def add_x(chunk):
            self.x_copy(chunk).wait_recv()
            slot, columns = chunk % RING, self.only(self.rep)

            @pl.loop(0, self.hi_count)
            def _(h):
                for m in range(2):
                    self.held[slot, h, m, :, columns] = (
                        self.held[slot, h, m, :, columns].astype(F32)
                        + self.from_x[chunk, h, m].astype(F32)
                    ).astype(BF)

            self.y_copy(chunk).start()

        def add_y(chunk):
            self.y_copy(chunk).wait_recv()
            slot, columns = chunk % RING, self.columns(self.rep)

            @pl.loop(0, self.hi_count)
            def _(h):
                self.held[slot, h, self.mid, :, columns] = (
                    self.held[slot, h, self.mid, :, columns].astype(F32)
                    + self.from_y[chunk, h].astype(F32)
                ).astype(BF)

            for m in range(1, self.hi_count):
                self.z_copy(chunk, m).start()

        def add_z(chunk):
            columns = self.columns(self.rep)
            value = self.held[chunk % RING, self.hi, self.mid, :, columns].astype(F32)
            for m in range(1, self.hi_count):
                self.z_copy(chunk, m).wait_recv()
                value += self.from_z[chunk, m - 1].astype(F32)
            self.own[chunk, :, columns] = value.astype(BF)
            self.f_copy(chunk, False).start()

        stage(0, begin)
        stage(1, add_x)
        stage(2, add_y)
        stage(3, add_z)
        stage(4, lambda chunk: self.f_copy(chunk, True).wait_recv())
        stage(0, add_core)

    def drain(self):
        @pl.loop(0, self.count)
        def _(chunk):
            self.c_copy(chunk).wait_send()
            self.f_copy(chunk, False).wait_send()

        for chunk in range(self.count - RING, self.count):
            self.free(chunk)

    def whole(self, slab, columns):
        at = [slab * self.parts + part for part in range(self.parts)]
        parts = [self.own[c, :, columns].astype(F32) + self.other[c, :, columns].astype(F32) for c in at]
        return parts[0] if self.parts == 1 else jnp.concatenate(parts, axis=0)


class VectorScatter:
    def __init__(self, hi_count, bufs, sems):
        self.hi_count = hi_count
        self.mine, self.from_core, self.from_y, self.from_z, self.own, self.other = bufs
        (self.c_send, self.c_recv, self.y_send, self.y_recv, self.z_send, self.z_recv, self.f_send,
         self.f_recv) = sems
        self.hi, self.mid, self.core, self.rep = place(hi_count)

    @staticmethod
    def scratch(hi_count):
        tile = (VEC_ROWS, LANES)
        dma = pltpu.SemaphoreType.DMA
        bufs = [
            pltpu.VMEM((hi_count, 2, 2) + tile, F32),
            pltpu.VMEM((hi_count, 2) + tile, F32),
            pltpu.VMEM((hi_count,) + tile, F32),
            pltpu.VMEM((hi_count - 1,) + tile, F32),
            pltpu.VMEM(tile, F32),
            pltpu.VMEM(tile, F32),
        ]
        return bufs, [dma((1,))] * 4 + [dma((hi_count - 1,))] * 2 + [dma((1,))] * 2

    def c_copy(self):
        device = shard_of(self.hi, self.mid, 1 - self.core)
        source = self.mine.at[:, :, 1 - self.core]
        return remote(source, self.from_core, self.c_send.at[0], self.c_recv.at[0], device)

    def y_copy(self):
        device = shard_of(self.hi, 1 - self.mid, self.core)
        source = self.mine.at[:, 1 - self.mid, self.core]
        return remote(source, self.from_y, self.y_send.at[0], self.y_recv.at[0], device)

    def z_copy(self, m):
        there = (self.hi + m) % self.hi_count
        source = self.mine.at[there, self.mid, self.core]
        sems = (self.z_send.at[m - 1], self.z_recv.at[m - 1])
        return remote(source, self.from_z.at[m - 1], *sems, shard_of(there, self.mid, self.core))

    def f_copy(self):
        return remote(self.own, self.other, self.f_send.at[0], self.f_recv.at[0], {"rep": 1 - self.rep})

    def step(self, number):
        if number == 0:
            self.c_copy().start()
        elif number == 1:
            self.c_copy().wait_recv()
            self.mine[:, :, self.core] = self.mine[:, :, self.core] + self.from_core[...]
            self.y_copy().start()
        elif number == 2:
            self.y_copy().wait_recv()
            self.mine[:, self.mid, self.core] = self.mine[:, self.mid, self.core] + self.from_y[...]
            for m in range(1, self.hi_count):
                self.z_copy(m).start()
        elif number == 3:
            total = self.mine[self.hi, self.mid, self.core]
            for m in range(1, self.hi_count):
                self.z_copy(m).wait_recv()
                total += self.from_z[m - 1]
            self.own[...] = total
            self.f_copy().start()
        else:
            self.f_copy().wait()
            self.c_copy().wait_send()
            self.y_copy().wait_send()
            for m in range(1, self.hi_count):
                self.z_copy(m).wait_send()


def spread_vectors(mine, rows, bias, depth):
    hi_count = mine.shape[0]
    for shard in range(4 * hi_count):
        at = shard // 4, shard // 2 % 2, shard % 2

        def piece(ref, some, start):
            tile = ref[some, tile_of(start)]
            shift = -start % LANES
            return pltpu.roll(tile, shift, 1) if shift else tile

        mine[at] = piece(rows, slice(None), shard * depth)
        for t in range(3):
            start = (3 * shard + t) * depth
            slab = start // D
            mine[at + (slice(t, t + 1),)] = piece(bias, slice(slab, slab + 1), start % D)


def backward_kernel(
    hi_count,
    full,
    d_ffn_in,
    d_second,
    first_in,
    normed_in,
    q_all,
    k_all,
    v_all,
    q_ext_all,
    active_all,
    slope_all,
    x_all,
    inv_std,
    context,
    k_doc,
    vectors,
    sums_two,
    cosine,
    sine,
    grads,
    from_core,
    input_grad,
    g_qkv,
    g_out,
    g_up,
    g_down,
    g_vec,
    down_buf,
    up_buf,
    d_context,
    peer_part,
    peer_sum,
    rows_grad,
    bias_grad,
    load_sem,
    flush_sem,
    w_sem,
    p_sem,
    *rest,
):
    rows = context.shape[0]
    depth = g_qkv.shape[0]
    scatter = Scatter(hi_count, depth, grads, from_core, rest[:7], rest[7:18])
    small = VectorScatter(hi_count, rest[18:24], rest[24:])
    hi, mid, core, rep = place(hi_count)
    scatter.own[...] = jnp.zeros_like(scatter.own)
    scatter.other[...] = jnp.zeros_like(scatter.other)
    rows_grad[...] = jnp.zeros_like(rows_grad)
    rows_grad[B_DOWN : B_DOWN + 3] = sums_two[...]
    entry_barrier(hi_count, hi, mid, core, rep)
    upper = hi_count // 2
    own_rows = pl.ds(pl.multiple_of(rep * rows, rows), rows)
    peer_rows = pl.ds(pl.multiple_of((1 - rep) * rows, rows), rows)

    def flush_rows(slab, half):
        return pltpu.make_async_copy(
            down_buf.at[half], grads.at[slab, pl.ds(half * upper, upper)], flush_sem.at[half]
        )

    def flush_columns(slab, half):
        columns = pl.ds(half * HALF, HALF)
        return pltpu.make_async_copy(
            up_buf.at[half], grads.at[slab, :, :, :, :, columns], flush_sem.at[2 + half]
        )

    def ffn_phase(slots, act, slope, d_ffn, first, normed):
        def weights(j, base):
            return [
                pltpu.make_async_copy(full.at[UP + 2 * j + s], slots.at[base + s], w_sem.at[base + s])
                for s in range(2)
            ]

        def kept(j, half):
            return [
                pltpu.make_async_copy(active_all.at[2 * j + half], act.at[half], load_sem.at[2 * half]),
                pltpu.make_async_copy(slope_all.at[2 * j + half], slope.at[half], load_sem.at[2 * half + 1]),
            ]

        others = [
            pltpu.make_async_copy(d_ffn_in, d_ffn, p_sem.at[0]),
            pltpu.make_async_copy(first_in, first, p_sem.at[1]),
            pltpu.make_async_copy(d_second, input_grad, p_sem.at[2]),
            pltpu.make_async_copy(normed_in, normed, p_sem.at[3]),
        ]
        for copy in others[:1] + weights(0, 0) + kept(0, 0) + kept(0, 1) + others[1:]:
            copy.start()
        for copy in others:
            copy.wait()

        @pl.loop(0, 4)
        def _(j):
            base = lax.rem(j, 2) * 2
            for copy in weights(j, base):
                copy.wait()

            @pl.when(j < 3)
            def _():
                for copy in weights(j + 1, 2 - base):
                    copy.start()

            for half in range(2):
                for copy in kept(j, half):
                    copy.wait()
                low = d_ffn[...]
                down = slots[base + 1, half * upper : (half + 1) * upper].reshape(HALF, D)
                d_hidden = (dot_nt(low, down) * slope[half].astype(F32)).astype(BF)
                columns = slice(half * HALF, (half + 1) * HALF)
                rows_grad[pl.ds(B_UP + j, 1), columns] = column_sum(d_hidden.astype(F32))
                g_rows = dot_tn(act[half], low)
                g_columns = dot_tn(first[...], d_hidden)

                @pl.when(j < 3)
                def _():
                    for copy in kept(j + 1, half):
                        copy.start()

                @pl.when(j > 0)
                def _():
                    if half == 0:
                        for h in range(2):
                            flush_rows(2 * j - 2, h).wait()
                            flush_columns(2 * j - 1, h).wait()
                        scatter.hand_over(2 * j - 2)
                        scatter.hand_over(2 * j - 1)

                down_buf[half] = g_rows.astype(BF).reshape(down_buf.shape[1:])
                up_buf[half] = g_columns.astype(BF).reshape(up_buf.shape[1:])
                flush_rows(2 * j, half).start()
                flush_columns(2 * j + 1, half).start()
                up = slots[base, :, :, :, :, columns].reshape(D, HALF)
                input_grad[...] += dot_nt(d_hidden, up)
                t = scatter.parts * (j - 1) + half
                if half < scatter.parts:
                    pl.when(t >= 0)(lambda: scatter.tick(t))

        w_out = pltpu.make_async_copy(full.at[3], slots.at[0], w_sem.at[0])
        w_out.start()
        for half in range(2):
            flush_rows(6, half).wait()
            flush_columns(7, half).wait()
        scatter.hand_over(6)
        scatter.hand_over(7)
        up = input_grad[...]
        normed_rows_ = normed[...]
        rows_grad[GAIN_ONE : GAIN_ONE + 1] = column_sum(up * normed_rows_)
        rows_grad[SHIFT_ONE : SHIFT_ONE + 1] = column_sum(up)
        grad = norm_back(up, normed_rows_, inv_std[:, 0:1], vectors[GAIN_ONE : GAIN_ONE + 1])
        input_grad[...] = grad
        d_attn = d_ffn
        d_attn[...] = grad.astype(BF)
        rows_grad[B_OUT : B_OUT + 1] = column_sum(d_attn[...].astype(F32))
        scatter.tick(3 * scatter.parts)
        w_out.wait()
        for half in range(2):
            columns = slice(half * HALF, (half + 1) * HALF)
            g_rows = dot_tn(context[:, columns], d_attn[...])
            down_buf[half] = g_rows.astype(BF).reshape(down_buf.shape[1:])
            flush_rows(8, half).start()
        d_context[...] = dot_nt(d_attn[...], slots[0].reshape(D, D)).astype(BF)
        for half in range(2):
            flush_rows(8, half).wait()
        scatter.hand_over(8)

    blocks = (hi_count, 2, 2, depth, D)
    pl.run_scoped(
        ffn_phase,
        pltpu.VMEM((4,) + blocks, BF),
        pltpu.VMEM((2, rows, HALF), BF),
        pltpu.VMEM((2, rows, HALF), BF),
        pltpu.VMEM((rows, D), BF),
        pltpu.VMEM((rows, D), BF),
        pltpu.VMEM((rows, D), F32),
    )
    early = 3 * scatter.parts + 1

    at = [min(early + HEADS // 2, 9 * scatter.parts)]

    def advance(handed):
        if at[0] < (9 + handed) * scatter.parts:
            scatter.tick(at[0])
            at[0] += 1

    def attention_phase(slots, q_in, k_in, v_in, ext_in, d_q, d_k, d_v, x):
        def quad(i, slot):
            return [
                pltpu.make_async_copy(q_all.at[i], q_in.at[slot], load_sem.at[slot]),
                pltpu.make_async_copy(k_all.at[i], k_in.at[slot], load_sem.at[2 + slot]),
                pltpu.make_async_copy(v_all.at[i], v_in.at[slot], load_sem.at[4 + slot]),
                pltpu.make_async_copy(q_ext_all.at[pl.ds(4 * i, 4)], ext_in.at[slot], load_sem.at[6 + slot]),
            ]

        weights = [pltpu.make_async_copy(full.at[s], slots.at[s], w_sem.at[s]) for s in range(3)]
        x_copy = pltpu.make_async_copy(x_all, x, w_sem.at[3])
        for copy in quad(0, 0) + weights + [x_copy]:
            copy.start()
        doc_k = k_doc[...]
        piece = 256

        def rope_back(a, table_rows):
            return a * cosine[table_rows, :] + swap_halves(a * sine[table_rows, :])

        @pl.loop(0, HEADS // 4)
        def _(i):
            slot = lax.rem(i, 2)
            for copy in quad(i, slot):
                copy.wait()

            @pl.when(i < HEADS // 4 - 1)
            def _():
                for copy in quad(i + 1, 1 - slot):
                    copy.start()

            for pair in range(2):
                lanes = slice(pair * LANES, (pair + 1) * LANES)
                wide = pl.ds(pl.multiple_of(i * QUAD + pair * LANES, LANES), LANES)
                k_pair, v_pair = k_in[slot, :, lanes], v_in[slot, :, lanes]
                k_lane = lax.broadcasted_iota(jnp.int32, k_pair.shape, 1)
                keys = jnp.concatenate([k_pair, doc_k], axis=1)
                minus = jnp.where(k_lane < 3, -1.0, 0.0).astype(BF)
                values = jnp.concatenate([v_pair, minus], axis=1)
                dk = dv = None
                for start in range(0, rows, piece):
                    part = slice(start, start + piece)
                    q_pair, g_pair = q_in[slot, part, lanes], d_context[part, wide]
                    lane = lax.broadcasted_iota(jnp.int32, q_pair.shape, 1)
                    product = g_pair.astype(F32) * context[part, wide].astype(F32)
                    dq = None
                    for head in range(2):
                        in_head = (lane // HEAD_DIM) == head
                        q_head = jnp.where(in_head, q_pair, 0)
                        g_head = jnp.where(in_head, g_pair, 0)
                        inner = jnp.sum(jnp.where(in_head, product, 0.0), axis=1, keepdims=True)
                        top, middle, low = split3(jnp.broadcast_to(inner, q_pair.shape))
                        g_ext = jnp.where(lane == 0, top, jnp.where(lane == 1, middle, low))
                        g_ext = jnp.where(lane < 3, g_ext, 0)
                        q_wide = jnp.concatenate([q_head, ext_in[slot, pair * 2 + head, part, :]], axis=1)
                        prob = jnp.exp(dot_nt(keys, q_wide))
                        d_prob = dot_nt(values, jnp.concatenate([g_head, g_ext], axis=1))
                        d_score = (prob * d_prob).astype(BF)
                        dv_part = dot(prob.astype(BF), g_head)
                        dk_part = dot(d_score, q_head)
                        k_head = jnp.where((k_lane // HEAD_DIM) == head, k_pair, 0)
                        dq_part = dot_tn(d_score, k_head)
                        dv = dv_part if dv is None else dv + dv_part
                        dk = dk_part if dk is None else dk + dk_part
                        dq = dq_part if dq is None else dq + dq_part
                    table_rows = pl.ds(pl.multiple_of(rep * rows + start, piece), piece)
                    d_q[part, wide] = rope_back(dq * HEAD_DIM**-0.5, table_rows).astype(BF)
                d_k[:rows, wide] = rope_back(dk[:rows], own_rows).astype(BF)
                d_k[rows:, wide] = rope_back(dk[rows:], peer_rows).astype(BF)
                d_v[:, wide] = dv.astype(BF)
                t = early + 2 * i + pair
                pl.when(t < 9 * scatter.parts)(lambda: scatter.tick(t))

        for copy in weights + [x_copy]:
            copy.wait()
        def slab_grad(s, count, d_rows):
            for half in range(2):
                columns = slice(half * HALF, (half + 1) * HALF)
                if s > 0:
                    flush_columns(8 + s, half).wait()
                g_columns = dot_tn(x[:count], d_rows[:, columns])
                up_buf[half] = g_columns.astype(BF).reshape(up_buf.shape[1:])
                flush_columns(9 + s, half).start()
            if s > 0:
                scatter.hand_over(8 + s)
            bias_grad[s : s + 1] = column_sum(d_rows[...].astype(F32))

        slab_grad(0, rows, d_q)
        advance(0)
        slab_grad(1, 2 * rows, d_k)
        advance(1)
        slab_grad(2, 2 * rows, d_v)
        advance(2)
        w_k, w_v = slots[1].reshape(D, D), slots[2].reshape(D, D)
        peer_part[...] = (dot_nt(d_k[rows:], w_k) + dot_nt(d_v[rows:], w_v)).astype(BF)
        peer_copy = remote(peer_part, peer_sum, p_sem.at[4], p_sem.at[5], {"rep": 1 - rep})
        peer_copy.start()
        for half in range(2):
            flush_columns(11, half).wait()
        scatter.hand_over(11)
        advance(3)
        spread_vectors(small.mine, rows_grad, bias_grad, depth)
        small.step(0)
        advance(3)
        small.step(1)
        input_grad[...] += dot_nt(d_q[...], slots[0].reshape(D, D))
        advance(3)
        input_grad[...] += dot_nt(d_k[:rows], w_k)
        advance(3)
        small.step(2)
        input_grad[...] += dot_nt(d_v[:rows], w_v)
        peer_copy.wait()
        input_grad[...] += peer_sum[...].astype(F32)

    pl.run_scoped(
        attention_phase,
        pltpu.VMEM((3,) + blocks, BF),
        pltpu.VMEM((2, rows, QUAD), BF),
        pltpu.VMEM((2, 2 * rows, QUAD), BF),
        pltpu.VMEM((2, 2 * rows, QUAD), BF),
        pltpu.VMEM((2, 4, rows, LANES), BF),
        pltpu.VMEM((rows, D), BF),
        pltpu.VMEM((2 * rows, D), BF),
        pltpu.VMEM((2 * rows, D), BF),
        pltpu.VMEM((2 * rows, D), BF),
    )

    @pl.loop(at[0], scatter.count + scatter.lag)
    def _(t):
        scatter.tick(t)

    small.step(3)
    for s in range(3):
        g_qkv[:, s * D : (s + 1) * D] = scatter.whole(9 + s, slice(None))
    g_out[...] = scatter.whole(8, slice(None))
    each = LANES // depth
    for j in range(4):
        g_down[j * depth : (j + 1) * depth] = scatter.whole(2 * j, slice(None))
    for t in range(FF // LANES):
        pieces = []
        for u in range(each):
            shard, j = divmod(t * each + u, 4)
            pieces.append((scatter.whole(2 * j + 1, tile_of(shard * depth)), shard * depth % LANES))
        g_up[:, t * LANES : (t + 1) * LANES] = regroup(pieces, depth)
    small.step(4)
    g_vec[...] = small.own[...] + small.other[...]
    scatter.drain()


def backward(hi_count, full, arrays, kept):
    context, depth = kept[1], full.shape[4]
    rows = context.shape[0]
    anywhere = pl.BlockSpec(memory_space=pl.ANY)
    vmem = pl.BlockSpec(memory_space=pltpu.VMEM)
    dma = pltpu.SemaphoreType.DMA
    shape = jax.ShapeDtypeStruct
    blocks = (hi_count, 2, 2, depth)
    parts = Gather.parts_of(depth, SWAP)
    bufs, sems = Scatter.scratch(hi_count, depth)
    small_bufs, small_sems = VectorScatter.scratch(hi_count)
    return pl.pallas_call(
        functools.partial(backward_kernel, hi_count),
        out_shape=(
            shape((SLABS,) + blocks + (D,), BF),
            shape((SLABS * parts, hi_count, 2, depth // parts, D), BF),
            shape((rows, D), F32),
            shape((depth, 3 * D), F32),
            shape((depth, D), F32),
            shape((depth, FF), F32),
            shape((4 * depth, D), F32),
            shape((VEC_ROWS, LANES), F32),
        ),
        in_specs=[anywhere] * (1 + len(arrays)) + [vmem] * len(kept),
        out_specs=(anywhere,) * 2 + (vmem,) * 6,
        scratch_shapes=[
            pltpu.VMEM((2, hi_count // 2, 2, 2, depth, D), BF),
            pltpu.VMEM((2,) + blocks + (HALF,), BF),
            pltpu.VMEM((rows, D), BF),
            pltpu.VMEM((rows, D), BF),
            pltpu.VMEM((rows, D), BF),
            pltpu.VMEM((VEC_ROWS, D), F32),
            pltpu.VMEM((3, D), F32),
            dma((8,)),
            dma((4,)),
            dma((4,)),
            dma((6,)),
        ]
        + bufs
        + sems
        + small_bufs
        + small_sems,
        compiler_params=pltpu.CompilerParams(
            collective_id=1, has_side_effects=True, vmem_limit_bytes=VMEM
        ),
        name="backward",
    )(full, *arrays, *kept)


def rope_tables(count):
    position = np.arange(count, dtype=np.float32)
    frequency = np.exp(np.arange(HEAD_DIM // 2, dtype=np.float32) * np.float32(-2.0 * math.log(10000.0) / HEAD_DIM))
    angles = position[:, None] * frequency[None, :].astype(np.float32)
    cosine, sine = np.cos(angles).astype(np.float32), np.sin(angles).astype(np.float32)
    return (
        jnp.asarray(np.concatenate([cosine] * 4, axis=1)),
        jnp.asarray(np.concatenate([-sine, sine, -sine, sine], axis=1)),
    )


def local(
    tokens,
    segments,
    cotangent,
    w_qkv,
    b_qkv,
    w_out,
    b_out,
    gain_one,
    shift_one,
    w_up,
    b_up,
    w_down,
    b_down,
    gain_two,
    shift_two,
):
    rows = tokens.shape[0]
    shards = lax.axis_size("shard")
    hi_count = shards // 4
    depth = D // shards
    small = (b_qkv, b_out, gain_one, shift_one, b_up, b_down, gain_two, shift_two)
    widths = [a.shape[0] for a in small]
    vec = jnp.concatenate(small).astype(BF).reshape(-1, depth)
    vec = jnp.tile(jnp.pad(vec, ((0, VEC_ROWS - vec.shape[0]), (0, 0))), (1, LANES // depth))
    lane = jnp.arange(LANES, dtype=jnp.int32)[None, :]
    q_doc = (segments[:, None] == lane).astype(BF)
    cosine, sine = rope_tables(2 * rows)
    (
        full, q, k, v, q_ext, active, slope, x_all, k_doc, context, first, normed, inv_std, result,
        d_second, d_ffn, sums_two, vectors,
    ) = forward(hi_count, (w_qkv, w_out, w_up, w_down), vec[None], tokens, cotangent, q_doc, cosine, sine)
    _, _, input_grad, g_qkv, g_out, g_up, g_down, g_vec = backward(
        hi_count,
        full,
        (d_ffn, d_second, first, normed, q, k, v, q_ext, active, slope, x_all),
        (inv_std, context, k_doc, vectors, sums_two, cosine, sine),
    )
    outs = []
    at = 0
    for width in widths:
        count = width // depth
        outs.append(g_vec[at : at + count, :depth].reshape(width))
        at += count
    return (
        result,
        input_grad,
        g_qkv,
        outs[0],
        g_out,
        outs[1],
        outs[2],
        outs[3],
        g_up,
        outs[4],
        g_down,
        outs[5],
        outs[6],
        outs[7],
    )


def solution(mesh):
    act = P(("shard", "rep"), None)
    matrix = P("shard", None)
    vector = P("shard")
    params = (matrix, vector, matrix, vector, vector, vector, matrix, vector, matrix, vector, vector, vector)
    return jax.shard_map(
        local,
        mesh=mesh,
        in_specs=(act, P(("shard", "rep")), act) + params,
        out_specs=(act, act) + params,
        check_vma=False,
    )
```

```python
import functools
import math

import jax
import jax.numpy as jnp
import numpy as np
from jax import lax
from jax.experimental import pallas as pl
from jax.experimental.pallas import tpu as pltpu
from jax.sharding import PartitionSpec as P

D = 1024
HEADS = 16
HEAD_DIM = 64
FF = 4096
SLABS = 12
LANES = 128
MASKED = -1e30
MESH = pl.DeviceIdType.MESH
VMEM = 60 * 1024 * 1024
BF = jnp.bfloat16
F32 = jnp.float32

ERFC_P = 0.33
ERFC_Q = (
    0.1863661,
    0.182837329,
    0.20192357,
    0.0450108379,
    0.412542064,
    -0.355440048,
    0.462689118,
    -0.135929052,
)


def dot(a, b):
    return lax.dot_general(a, b, (((1,), (0,)), ((), ())), preferred_element_type=F32)


def dot_nt(a, b):
    return lax.dot_general(a, b, (((1,), (1,)), ((), ())), preferred_element_type=F32)


def dot_tn(a, b):
    return lax.dot_general(a, b, (((0,), (0,)), ((), ())), preferred_element_type=F32)


def swap_halves(a):
    width = a.shape[1]
    lane = lax.broadcasted_iota(jnp.int32, a.shape, 1) % HEAD_DIM
    return jnp.where(
        lane < HEAD_DIM // 2,
        pltpu.roll(a, width - HEAD_DIM // 2, 1),
        pltpu.roll(a, HEAD_DIM // 2, 1),
    )


def split3(a):
    hi = a.astype(BF)
    rest = a - hi.astype(F32)
    mid = rest.astype(BF)
    low = (rest - mid.astype(F32)).astype(BF)
    return hi, mid, low


def remote(src, dst, send, recv, device):
    return pltpu.make_async_remote_copy(
        src_ref=src, dst_ref=dst, send_sem=send, recv_sem=recv, device_id=device, device_id_type=MESH
    )


def place(hi_count):
    index = lax.axis_index("shard")
    return index // 4, (index // 2) % 2, index % 2, lax.axis_index("rep")


def shard_of(hi, mid, core):
    return {"shard": hi * 4 + mid * 2 + core}


def entry_barrier(hi_count, hi, mid, core, rep):
    barrier = pltpu.get_barrier_semaphore()
    for m in range(1, hi_count):
        pl.semaphore_signal(
            barrier, inc=1, device_id=shard_of((hi + m) % hi_count, mid, core), device_id_type=MESH
        )
    pl.semaphore_signal(barrier, inc=1, device_id=shard_of(hi, 1 - mid, core), device_id_type=MESH)
    pl.semaphore_signal(barrier, inc=1, device_id=shard_of(hi, mid, 1 - core), device_id_type=MESH)
    pl.semaphore_signal(barrier, inc=1, device_id={"rep": 1 - rep}, device_id_type=MESH)
    pl.semaphore_wait(barrier, hi_count + 2)


SWAP = 256
PARTS = 2


def normed_rows(residual):
    mean_val = jnp.mean(residual, axis=-1, keepdims=True)
    centred = residual - mean_val
    variance = jnp.mean(centred * centred, axis=-1, keepdims=True)
    inv_std = lax.rsqrt(variance + 1e-05)
    return centred * inv_std, inv_std


def norm_back(upstream, normed, inv_std, gain_vec):
    scaled = upstream * gain_vec
    return inv_std * (
        scaled
        - jnp.mean(scaled, axis=-1, keepdims=True)
        - normed * jnp.mean(scaled * normed, axis=-1, keepdims=True)
    )


def column_sum(a):
    return jnp.sum(a, axis=0, keepdims=True)


class Gather:
    def __init__(self, hi_count, packed, full, sems, swap=SWAP):
        self.hi_count = hi_count
        self.packed, self.full = packed, full
        (self.up_send, self.up_recv, self.down_send, self.down_recv, self.y_send, self.y_recv,
         self.x_send, self.x_recv, self.c_send, self.c_recv) = sems
        self.hi, self.mid, self.core, self.rep = place(hi_count)
        slabs, self.depth, width = packed.shape
        self.parts = self.parts_of(self.depth, swap)
        self.rows = self.depth // self.parts
        self.count = slabs * self.parts
        self.swap = swap
        self.mine = slice(None)
        if swap:
            self.mine = pl.ds(pl.multiple_of(self.rep * swap, LANES), width - swap)

    @staticmethod
    def parts_of(depth, swap):
        return PARTS if swap and depth % (16 * PARTS) == 0 else 1

    @staticmethod
    def scratch(hi_count, slabs, depth, swap=SWAP):
        count = slabs * Gather.parts_of(depth, swap)
        dma = pltpu.SemaphoreType.DMA
        hops = dma((count, hi_count - 1))
        return [hops] * 4 + [dma((count,))] * 4 + [dma((count, 2))] * 2

    def only(self, which):
        return pl.ds(pl.multiple_of(which * (D - self.swap), LANES), self.swap)

    def spot(self, chunk):
        start = (chunk % self.parts) * self.rows
        if not isinstance(start, int):
            start = pl.multiple_of(start, self.rows)
        return chunk // self.parts, pl.ds(start, self.rows)

    def hop(self, chunk, distance, up):
        slab, rows = self.spot(chunk)
        origin = self.hi - distance if up else self.hi + distance
        block = self.full.at[slab, origin, self.mid, self.core, rows, self.mine]
        source = self.packed.at[slab, rows, self.mine] if distance == 0 else block
        send, recv = (self.up_send, self.up_recv) if up else (self.down_send, self.down_recv)
        device = shard_of(self.hi + 1 if up else self.hi - 1, self.mid, self.core)
        return remote(source, block, send.at[chunk, distance], recv.at[chunk, distance], device)

    def landed_hop(self, chunk, distance, up):
        slab, rows = self.spot(chunk)
        origin = self.hi - distance - 1 if up else self.hi + distance + 1
        block = self.full.at[slab, origin, self.mid, self.core, rows, self.mine]
        send, recv = (self.up_send, self.up_recv) if up else (self.down_send, self.down_recv)
        device = shard_of(self.hi, self.mid, self.core)
        return remote(block, block, send.at[chunk, distance], recv.at[chunk, distance], device)

    def sends(self, distance, up):
        if up:
            return (self.hi - distance >= 0) & (self.hi + 1 < self.hi_count)
        return (self.hi + distance < self.hi_count) & (self.hi - 1 >= 0)

    def lands(self, distance, up):
        if up:
            return self.hi - distance - 1 >= 0
        return self.hi + distance + 1 < self.hi_count

    def y_copy(self, chunk, landed):
        slab, rows = self.spot(chunk)
        which = 1 - self.mid if landed else self.mid
        block = self.full.at[slab, :, which, self.core, rows, self.mine]
        device = shard_of(self.hi, 1 - self.mid, self.core)
        return remote(block, block, self.y_send.at[chunk], self.y_recv.at[chunk], device)

    def x_copy(self, chunk, landed):
        slab, rows = self.spot(chunk)
        columns = self.only(1 - self.rep if landed else self.rep)
        block = self.full.at[slab, :, :, self.core, rows, columns]
        return remote(block, block, self.x_send.at[chunk], self.x_recv.at[chunk], {"rep": 1 - self.rep})

    def c_copy(self, chunk, part, landed):
        slab, rows = self.spot(chunk)
        which = 1 - self.core if landed else self.core
        columns = self.mine if part == 0 else self.only(1 - self.rep)
        block = self.full.at[slab, :, :, which, rows, columns]
        device = shard_of(self.hi, self.mid, 1 - self.core)
        return remote(block, block, self.c_send.at[chunk, part], self.c_recv.at[chunk, part], device)

    @property
    def lag(self):
        return 2 * self.hi_count + 4

    def own_copy(self, sem):
        target = self.full.at[:, self.hi, self.mid, self.core, :, self.mine]
        return pltpu.make_async_copy(self.packed.at[:, :, self.mine], target, sem)

    def tick(self, t):
        def stage(offset, act):
            if not isinstance(t, int):
                chunk = t - offset
                pl.when((chunk >= 0) & (chunk < self.count))(lambda: act(chunk))
            elif 0 <= t - offset < self.count:
                act(t - offset)

        def own(chunk):
            for up in (True, False):
                pl.when(self.sends(0, up))(lambda: self.hop(chunk, 0, up).start())

        def forward(distance, chunk):
            for up in (True, False):
                pl.when(self.lands(distance - 1, up))(
                    lambda: self.landed_hop(chunk, distance - 1, up).wait_recv()
                )
                if distance < self.hi_count - 1:
                    pl.when(self.sends(distance, up))(lambda: self.hop(chunk, distance, up).start())
            if distance == self.hi_count - 1:
                self.y_copy(chunk, False).start()

        def after_y(chunk):
            self.y_copy(chunk, True).wait_recv()
            if self.swap:
                self.x_copy(chunk, False).start()
            self.c_copy(chunk, 0, False).start()

        def after_x(chunk):
            if self.swap:
                self.x_copy(chunk, True).wait_recv()
                self.c_copy(chunk, 1, False).start()

        def after_c(chunk):
            for part in range(2 if self.swap else 1):
                self.c_copy(chunk, part, True).wait_recv()

        stage(0, own)
        for distance in range(1, self.hi_count):
            stage(2 * distance, functools.partial(forward, distance))
        stage(2 * self.hi_count, after_y)
        stage(2 * self.hi_count + 2, after_x)
        stage(2 * self.hi_count + 4, after_c)

    def drain(self):
        @pl.loop(0, self.count)
        def _(chunk):
            for distance in range(self.hi_count - 1):
                for up in (True, False):
                    pl.when(self.sends(distance, up))(
                        lambda: self.hop(chunk, distance, up).wait_send()
                    )
            self.y_copy(chunk, False).wait_send()
            if self.swap:
                self.x_copy(chunk, False).wait_send()
            for part in range(2 if self.swap else 1):
                self.c_copy(chunk, part, False).wait_send()


def near_barrier(hi_count):
    hi, mid, core, rep = place(hi_count)
    barrier = pltpu.get_barrier_semaphore()

    def greet(device):
        pl.semaphore_signal(barrier, inc=1, device_id=device, device_id_type=MESH)

    pl.when(hi + 1 < hi_count)(lambda: greet(shard_of(hi + 1, mid, core)))
    pl.when(hi - 1 >= 0)(lambda: greet(shard_of(hi - 1, mid, core)))
    greet(shard_of(hi, 1 - mid, core))
    greet(shard_of(hi, mid, 1 - core))
    greet({"rep": 1 - rep})
    first, last = hi == 0, hi == hi_count - 1
    pl.semaphore_wait(barrier, 5 - first.astype(jnp.int32) - last.astype(jnp.int32))


UP, DOWN = 4, 5
HALF = D // 2
QUAD = 4 * HEAD_DIM
B_OUT, GAIN_ONE, SHIFT_ONE, B_UP, B_DOWN, GAIN_TWO, SHIFT_TWO = 3, 4, 5, 6, 10, 11, 12
VEC_ROWS = 16


def regroup(pieces, depth):
    out = None
    for u, (tile, start) in enumerate(pieces):
        shift = (u * depth - start) % LANES
        moved = pltpu.roll(tile, shift, 1) if shift else tile
        lane = lax.broadcasted_iota(jnp.int32, moved.shape, 1)
        out = moved if out is None else jnp.where(lane // depth == u, moved, out)
    return out


def tile_of(at):
    return slice(at // LANES * LANES, at // LANES * LANES + LANES)


def pack(packed, w_qkv, w_out, w_up, w_down):
    depth = w_qkv.shape[0]
    for slab in range(3):
        packed[slab] = w_qkv[:, slab * D : (slab + 1) * D].astype(BF)
    packed[3] = w_out[...].astype(BF)
    each = LANES // depth
    for j in range(4):
        packed[DOWN + 2 * j] = w_down[j * depth : (j + 1) * depth].astype(BF)
        for t in range(D // LANES):
            starts = [4 * depth * (t * each + u) + depth * j for u in range(each)]
            pieces = [(w_up[:, tile_of(at)], at % LANES) for at in starts]
            packed[UP + 2 * j, :, t * LANES : (t + 1) * LANES] = regroup(pieces, depth).astype(BF)


def unpack_vectors(vec_full, rows_out, bias, depth):
    hi_count = vec_full.shape[1]
    each = LANES // depth

    def of_shard(shard):
        return vec_full[0, shard // 4, shard // 2 % 2, shard % 2].astype(BF).astype(F32)

    def join(pieces):
        lane = lax.broadcasted_iota(jnp.int32, pieces[0].shape, 1)
        out = pieces[0]
        for u in range(1, each):
            out = jnp.where(lane // depth == u, pieces[u], out)
        return out

    for t in range(D // LANES):
        tile = slice(t * LANES, (t + 1) * LANES)
        rows_out[:, tile] = join([of_shard(t * each + u) for u in range(each)])
        for j in range(3):
            chunks = [(j * D + t * LANES) // depth + u for u in range(each)]
            bias[j : j + 1, tile] = join([of_shard(m // 3)[m % 3 : m % 3 + 1] for m in chunks])


def gelu_parts(hidden):
    gauss = jnp.exp(hidden * hidden * -0.5)
    t = 1.0 / (1.0 + (ERFC_P * math.sqrt(0.5)) * jnp.abs(hidden))
    poly = jnp.full_like(t, ERFC_Q[-1])
    for coefficient in ERFC_Q[-2::-1]:
        poly = poly * t + coefficient
    tail = 0.5 * t * poly * gauss
    cdf = jnp.where(hidden >= 0, 1.0 - tail, tail)
    return hidden * cdf, cdf + hidden * gauss * (1.0 / math.sqrt(2.0 * math.pi))


def forward_kernel(
    hi_count,
    w_qkv,
    w_out,
    w_up,
    w_down,
    vec,
    tokens,
    cotangent,
    q_doc,
    cosine,
    sine,
    full,
    q_all,
    k_all,
    v_all,
    q_ext_all,
    active_all,
    slope_all,
    x_all,
    k_doc,
    context,
    first_turned,
    normed_out,
    inv_out,
    result,
    d_second,
    d_ffn,
    sums,
    vectors,
    packed,
    vec_full,
    x_peer,
    slots,
    q_buf,
    k_buf,
    v_buf,
    ext_buf,
    first,
    first_low,
    turned,
    total,
    act_buf,
    slope_buf,
    bias,
    local_sem,
    load_sem,
    flush_sem,
    t_sem,
    *sems,
):
    rows = tokens.shape[0]
    depth = w_qkv.shape[0]
    rep = lax.axis_index("rep")
    gather = Gather(hi_count, packed, full, sems[:10])
    small = Gather(hi_count, vec, vec_full, sems[10:], swap=0)
    lane_doc = lax.broadcasted_iota(jnp.int32, (rows, LANES), 1)
    other = jnp.where(q_doc[...] > 0.5, 0.0, MASKED)
    other = jnp.where(lane_doc < 61, other, jnp.where(lane_doc < 64, 1.0, 0.0))
    k_doc[:rows] = other.astype(BF)
    pack(packed, w_qkv, w_out, w_up, w_down)
    near_barrier(hi_count)
    peer = {"rep": 1 - rep}
    token_copy = remote(tokens, x_peer, t_sem.at[0], t_sem.at[1], peer)
    doc_copy = remote(k_doc.at[:rows], k_doc.at[rows:], t_sem.at[2], t_sem.at[3], peer)
    copies = [small.own_copy(local_sem.at[0]), gather.own_copy(local_sem.at[1])]
    for copy in copies:
        copy.start()
    doc_copy.start()
    token_copy.start()
    for copy in copies:
        copy.wait()
    warm = gather.lag + 1
    for t in range(warm):
        small.tick(t)
        gather.tick(t)
    unpack_vectors(vec_full, vectors, bias, depth)
    doc_copy.wait()
    token_copy.wait()
    turned[:, :rows] = tokens[...].T
    turned[:, rows:] = x_peer[...].T
    x_copy = pltpu.make_async_copy(turned, x_all, local_sem.at[0])
    x_copy.start()
    ready = 3 * gather.parts + gather.lag

    @pl.loop(warm, ready)
    def _(t):
        gather.tick(t)

    def load_whole(slab, slot):
        return pltpu.make_async_copy(full.at[slab], slots.at[slot], load_sem.at[slot])

    for slab in range(3):
        load_whole(slab, slab).start()
    for slab in range(3):
        load_whole(slab, slab).wait()

    def weight(slot, columns):
        return slots[slot, :, :, :, :, columns].reshape(D, -1)

    own_rows = pl.ds(pl.multiple_of(rep * rows, rows), rows)
    peer_rows = pl.ds(pl.multiple_of((1 - rep) * rows, rows), rows)

    def rope(a, table_rows):
        cos_part, sin_part = cosine[table_rows, :], sine[table_rows, :]
        cos_part = jnp.concatenate([cos_part, cos_part], axis=1)
        sin_part = jnp.concatenate([sin_part, sin_part], axis=1)
        return a * cos_part + swap_halves(a) * sin_part

    def flushes(i):
        return [
            pltpu.make_async_copy(q_buf.at[i], q_all.at[i], flush_sem.at[0, i]),
            pltpu.make_async_copy(k_buf.at[i], k_all.at[i], flush_sem.at[1, i]),
            pltpu.make_async_copy(v_buf.at[i], v_all.at[i], flush_sem.at[2, i]),
            pltpu.make_async_copy(
                ext_buf.at[pl.ds(4 * i, 4)], q_ext_all.at[pl.ds(4 * i, 4)], flush_sem.at[3, i]
            ),
        ]

    ones = jnp.ones((2 * rows, LANES), BF)
    piece = 256

    @pl.loop(0, HEADS // 4)
    def _(i):
        columns = pl.ds(pl.multiple_of(i * QUAD, QUAD), QUAD)
        own_x, peer_x = tokens[...], x_peer[...]
        w = weight(0, columns)
        q_rows = rope(dot(own_x, w) + bias[0:1, columns], own_rows) * HEAD_DIM**-0.5
        q_buf[i] = q_rows.astype(BF)
        w = weight(1, columns)
        k_buf[i, :rows] = rope(dot(own_x, w) + bias[1:2, columns], own_rows).astype(BF)
        k_buf[i, rows:] = rope(dot(peer_x, w) + bias[1:2, columns], peer_rows).astype(BF)
        w = weight(2, columns)
        v_buf[i, :rows] = (dot(own_x, w) + bias[2:3, columns]).astype(BF)
        v_buf[i, rows:] = (dot(peer_x, w) + bias[2:3, columns]).astype(BF)
        for pair in range(2):
            gather.tick(ready + 2 * i + pair)
            lanes = slice(pair * LANES, (pair + 1) * LANES)
            keys = jnp.concatenate([k_buf[i, :, lanes], k_doc[...]], axis=1)
            values = jnp.concatenate([v_buf[i, :, lanes], ones], axis=1)
            for start in range(0, rows, piece):
                part = slice(start, start + piece)
                q_pair = q_buf[i, part, lanes]
                lane = lax.broadcasted_iota(jnp.int32, q_pair.shape, 1)
                doc_q = q_doc[part, :]
                mixed = []
                for head in range(2):
                    in_head = (lane // HEAD_DIM) == head
                    queries = jnp.concatenate([jnp.where(in_head, q_pair, 0), doc_q], axis=1)
                    scores = dot_nt(queries, keys)
                    row_max = jnp.max(scores, axis=1, keepdims=True)
                    prob = jnp.exp(scores - row_max).astype(BF)
                    both = dot(prob, values)
                    row_sum = both[:, LANES:]
                    mixed.append(both[:, :LANES] / row_sum)
                    hi, mid, low = split3(-(row_max + jnp.log(row_sum)))
                    ext = jnp.where(lane == 61, hi, doc_q)
                    ext = jnp.where(lane == 62, mid, ext)
                    ext = jnp.where(lane == 63, low, ext)
                    ext_buf[4 * i + pair * 2 + head, part, :] = ext
                pair_lanes = pl.ds(pl.multiple_of(i * QUAD + pair * LANES, LANES), LANES)
                context[part, pair_lanes] = jnp.where(lane < HEAD_DIM, mixed[0], mixed[1]).astype(BF)
        for copy in flushes(i):
            copy.start()

    done = ready + HEADS // 2

    def vector(row):
        return vectors[row : row + 1, :]

    load_whole(3, 3).start()
    for slot in range(2):
        load_whole(UP + slot, slot).start()
    load_whole(3, 3).wait()
    attn = dot(context[...], weight(3, slice(None))) + vector(B_OUT)
    normed, inv_std = normed_rows(tokens[...].astype(F32) + attn)
    first[...] = normed * vector(GAIN_ONE) + vector(SHIFT_ONE)
    first_low[...] = first[...].astype(BF)
    first_turned[...] = first_low[...].T
    normed_out[...] = normed
    inv_out[...] = jnp.broadcast_to(inv_std, inv_out.shape)
    total[...] = first[...] + vector(B_DOWN)

    def keeps(j, half):
        return [
            pltpu.make_async_copy(
                act_buf.at[half], active_all.at[2 * j + half], flush_sem.at[4, 2 * half]
            ),
            pltpu.make_async_copy(
                slope_buf.at[half], slope_all.at[2 * j + half], flush_sem.at[4, 2 * half + 1]
            ),
        ]

    @pl.loop(0, 4)
    def _(j):
        base = lax.rem(j, 2) * 2

        for slot in range(2):
            load_whole(UP + 2 * j + slot, base + slot).wait()
        for half in range(2):
            @pl.when(j > 0)
            def _():
                for copy in keeps(j - 1, half):
                    copy.wait()

            columns = slice(half * HALF, (half + 1) * HALF)
            hidden = dot(first_low[...], weight(base, columns)) + vectors[pl.ds(B_UP + j, 1), columns]
            act, slope = gelu_parts(hidden)
            act = act.astype(BF)
            act_buf[half] = act.T
            slope_buf[half] = slope.astype(BF)
            down = slots[base + 1, half * (hi_count // 2) : (half + 1) * (hi_count // 2)].reshape(HALF, D)
            total[...] += dot(act, down)
            for copy in keeps(j, half):
                copy.start()
            for step in range(2):
                t = 6 * gather.parts + gather.lag + 2 * gather.parts * j + gather.parts * half + step
                if step < gather.parts:
                    pl.when(t >= done)(lambda: gather.tick(t))

        @pl.when(j < 3)
        def _():
            for slot in range(2):
                load_whole(UP + 2 * j + 2 + slot, 2 - base + slot).start()

    for half in range(2):
        for copy in keeps(3, half):
            copy.wait()
    gain = vector(GAIN_TWO)
    normed, inv_std = normed_rows(total[...])
    result[...] = (normed * gain + vector(SHIFT_TWO)).astype(BF)
    up = cotangent[...].astype(F32)
    sums[1:2] = column_sum(up * normed)
    sums[2:3] = column_sum(up)
    grad = norm_back(up, normed, inv_std, gain)
    d_second[...] = grad
    low = grad.astype(BF)
    d_ffn[...] = low
    sums[0:1] = column_sum(low.astype(F32))
    x_copy.wait()
    small.drain()
    gather.drain()

    @pl.loop(0, HEADS // 4)
    def _(i):
        for copy in flushes(i):
            copy.wait()


def forward(hi_count, weights, vec, tokens, cotangent, q_doc, cosine, sine):
    rows = tokens.shape[0]
    depth = weights[0].shape[0]
    anywhere = pl.BlockSpec(memory_space=pl.ANY)
    vmem = pl.BlockSpec(memory_space=pltpu.VMEM)
    dma = pltpu.SemaphoreType.DMA
    quads = HEADS // 4
    shape = jax.ShapeDtypeStruct
    blocks = (hi_count, 2, 2, depth, D)
    return pl.pallas_call(
        functools.partial(forward_kernel, hi_count),
        out_shape=(
            shape((SLABS,) + blocks, BF),
            shape((quads, rows, QUAD), BF),
            shape((quads, 2 * rows, QUAD), BF),
            shape((quads, 2 * rows, QUAD), BF),
            shape((HEADS, rows, LANES), BF),
            shape((8, HALF, rows), BF),
            shape((8, rows, HALF), BF),
            shape((D, 2 * rows), BF),
            shape((2 * rows, LANES), BF),
            shape((rows, D), BF),
            shape((D, rows), BF),
            shape((rows, D), F32),
            shape((rows, LANES), F32),
            shape((rows, D), BF),
            shape((rows, D), F32),
            shape((rows, D), BF),
            shape((3, D), F32),
            shape((VEC_ROWS, D), F32),
        ),
        in_specs=[vmem] * 10,
        out_specs=(anywhere,) * 8 + (vmem,) * 10,
        scratch_shapes=[
            pltpu.VMEM((SLABS, depth, D), BF),
            pltpu.VMEM((1, hi_count, 2, 2) + vec.shape[1:], F32),
            pltpu.VMEM((rows, D), BF),
            pltpu.VMEM((4,) + blocks, BF),
            pltpu.VMEM((quads, rows, QUAD), BF),
            pltpu.VMEM((quads, 2 * rows, QUAD), BF),
            pltpu.VMEM((quads, 2 * rows, QUAD), BF),
            pltpu.VMEM((HEADS, rows, LANES), BF),
            pltpu.VMEM((rows, D), F32),
            pltpu.VMEM((rows, D), BF),
            pltpu.VMEM((D, 2 * rows), BF),
            pltpu.VMEM((rows, D), F32),
            pltpu.VMEM((2, HALF, rows), BF),
            pltpu.VMEM((2, rows, HALF), BF),
            pltpu.VMEM((3, D), F32),
            dma((2,)),
            dma((4,)),
            dma((5, quads)),
            dma((4,)),
        ]
        + Gather.scratch(hi_count, SLABS, depth)
        + Gather.scratch(hi_count, 1, vec.shape[1], swap=0),
        compiler_params=pltpu.CompilerParams(
            collective_id=0, has_side_effects=True, vmem_limit_bytes=VMEM
        ),
        name="forward",
    )(*weights, vec, tokens, cotangent, q_doc, cosine, sine)


RING = 8
EARLY = 9


class Scatter:
    stages = (0, 2, 4, 6, 8)

    def __init__(self, hi_count, depth, grads, from_core, bufs, sems):
        self.hi_count, self.depth = hi_count, depth
        self.grads, self.from_core = grads, from_core
        (self.held, self.staged, self.from_x, self.from_y, self.from_z, self.late_y, self.late_z,
         self.own, self.other) = bufs
        (self.load_sem, self.c_send, self.c_recv, self.x_send, self.x_recv, self.y_send, self.y_recv,
         self.z_send, self.z_recv, self.f_send, self.f_recv) = sems
        self.hi, self.mid, self.core, self.rep = place(hi_count)
        self.parts = Gather.parts_of(depth, SWAP)
        self.rows = depth // self.parts
        self.count = SLABS * self.parts
        self.lag = self.stages[-1]
        self.early = EARLY * self.parts

    @staticmethod
    def scratch(hi_count, depth):
        parts = Gather.parts_of(depth, SWAP)
        count, early, rows = SLABS * parts, EARLY * parts, depth // parts
        dma = pltpu.SemaphoreType.DMA
        bufs = [
            pltpu.VMEM((RING, hi_count, 2, rows, D), BF),
            pltpu.VMEM((hi_count, 2, rows, D), BF),
            pltpu.VMEM((early, hi_count, 2, rows, SWAP), BF),
            pltpu.VMEM((early, hi_count, rows, D - SWAP), BF),
            pltpu.VMEM((early, hi_count - 1, rows, D - SWAP), BF),
            pltpu.VMEM((count - early, hi_count, rows, D), BF),
            pltpu.VMEM((count - early, hi_count - 1, rows, D), BF),
            pltpu.VMEM((count, rows, D), BF),
            pltpu.VMEM((count, rows, D), BF),
        ]
        sems = [dma((2,))] + [dma((count,))] * 6 + [dma((count, hi_count - 1))] * 2 + [dma((count,))] * 2
        return bufs, sems

    def late(self, chunk):
        return isinstance(chunk, int) and chunk >= self.early

    def columns(self, chunk, which):
        if self.late(chunk):
            return slice(None)
        return pl.ds(pl.multiple_of(which * SWAP, LANES), D - SWAP)

    def only(self, which):
        return pl.ds(pl.multiple_of(which * (D - SWAP), LANES), SWAP)

    def y_land(self, chunk):
        return self.late_y.at[chunk - self.early] if self.late(chunk) else self.from_y.at[chunk]

    def z_land(self, chunk, m):
        if self.late(chunk):
            return self.late_z.at[chunk - self.early, m - 1]
        return self.from_z.at[chunk, m - 1]

    def block(self, chunk, which):
        start = (chunk % self.parts) * self.rows
        if not isinstance(start, int):
            start = pl.multiple_of(start, self.rows)
        return self.grads.at[chunk // self.parts, :, :, which, pl.ds(start, self.rows)]

    def c_copy(self, chunk):
        return remote(
            self.block(chunk, 1 - self.core),
            self.from_core.at[chunk],
            self.c_send.at[chunk],
            self.c_recv.at[chunk],
            shard_of(self.hi, self.mid, 1 - self.core),
        )

    def loads(self, chunk):
        return [
            pltpu.make_async_copy(
                self.block(chunk, self.core), self.held.at[chunk % RING], self.load_sem.at[0]
            ),
            pltpu.make_async_copy(self.from_core.at[chunk], self.staged, self.load_sem.at[1]),
        ]

    def x_copy(self, chunk):
        return remote(
            self.held.at[chunk % RING, :, :, :, self.only(1 - self.rep)],
            self.from_x.at[chunk],
            self.x_send.at[chunk],
            self.x_recv.at[chunk],
            {"rep": 1 - self.rep},
        )

    def y_copy(self, chunk):
        return remote(
            self.held.at[chunk % RING, :, 1 - self.mid, :, self.columns(chunk, self.rep)],
            self.y_land(chunk),
            self.y_send.at[chunk],
            self.y_recv.at[chunk],
            shard_of(self.hi, 1 - self.mid, self.core),
        )

    def z_copy(self, chunk, m):
        there = (self.hi + m) % self.hi_count
        return remote(
            self.held.at[chunk % RING, there, self.mid, :, self.columns(chunk, self.rep)],
            self.z_land(chunk, m),
            self.z_send.at[chunk, m - 1],
            self.z_recv.at[chunk, m - 1],
            shard_of(there, self.mid, self.core),
        )

    def f_copy(self, chunk, landed):
        columns = self.columns(chunk, 1 - self.rep if landed else self.rep)
        source = self.other if landed else self.own
        return remote(
            source.at[chunk, :, columns],
            self.other.at[chunk, :, columns],
            self.f_send.at[chunk],
            self.f_recv.at[chunk],
            {"rep": 1 - self.rep},
        )

    def hand_over(self, slab):
        for part in range(self.parts):
            self.c_copy(slab * self.parts + part).start()

    def free(self, chunk):
        if not self.late(chunk):
            self.x_copy(chunk).wait_send()
        self.y_copy(chunk).wait_send()
        for m in range(1, self.hi_count):
            self.z_copy(chunk, m).wait_send()

    def tick(self, t):
        def stage(number, act):
            chunk = t - self.stages[number]
            if isinstance(chunk, int):
                if 0 <= chunk < self.early:
                    act(chunk)
                chunk = t - self.stages[max(number - 1, 0)]
                if self.early <= chunk < self.count:
                    act(chunk)
            else:
                pl.when(chunk >= 0)(lambda: act(chunk))

        def begin(chunk):
            self.c_copy(chunk).wait_recv()
            if isinstance(chunk, int):
                if chunk >= RING:
                    self.free(chunk - RING)
            else:
                pl.when(chunk >= RING)(lambda: self.free(chunk - RING))
            for copy in self.loads(chunk):
                copy.start()

        def add_core(chunk):
            for copy in self.loads(chunk):
                copy.wait()
            slot = chunk % RING

            @pl.loop(0, self.hi_count)
            def _(h):
                for m in range(2):
                    self.held[slot, h, m] = self.held[slot, h, m] + self.staged[h, m]

            if self.late(chunk):
                self.y_copy(chunk).start()
            else:
                self.x_copy(chunk).start()

        def add_x(chunk):
            if self.late(chunk):
                return
            self.x_copy(chunk).wait_recv()
            slot, columns = chunk % RING, self.only(self.rep)

            @pl.loop(0, self.hi_count)
            def _(h):
                for m in range(2):
                    self.held[slot, h, m, :, columns] = (
                        self.held[slot, h, m, :, columns] + self.from_x[chunk, h, m]
                    )

            self.y_copy(chunk).start()

        def add_y(chunk):
            self.y_copy(chunk).wait_recv()
            slot, columns = chunk % RING, self.columns(chunk, self.rep)

            @pl.loop(0, self.hi_count)
            def _(h):
                self.held[slot, h, self.mid, :, columns] = (
                    self.held[slot, h, self.mid, :, columns] + self.y_land(chunk)[h]
                )

            for m in range(1, self.hi_count):
                self.z_copy(chunk, m).start()

        def add_z(chunk):
            columns = self.columns(chunk, self.rep)
            value = self.held[chunk % RING, self.hi, self.mid, :, columns].astype(F32)
            for m in range(1, self.hi_count):
                self.z_copy(chunk, m).wait_recv()
                value += self.z_land(chunk, m)[...].astype(F32)
            self.own[chunk, :, columns] = value.astype(BF)
            self.f_copy(chunk, False).start()

        stage(0, begin)
        stage(1, add_x)
        stage(2, add_y)
        stage(3, add_z)
        stage(4, lambda chunk: self.f_copy(chunk, True).wait_recv())
        stage(0, add_core)

    def drain(self):
        def finish(chunk):
            self.c_copy(chunk).wait_send()
            self.f_copy(chunk, False).wait_send()

        pl.loop(0, self.early)(finish)
        for chunk in range(self.early, self.count):
            finish(chunk)
        for chunk in range(self.count - RING, self.count):
            self.free(chunk)

    def whole(self, slab, columns):
        at = [slab * self.parts + part for part in range(self.parts)]
        parts = [self.own[c, :, columns].astype(F32) + self.other[c, :, columns].astype(F32) for c in at]
        return parts[0] if self.parts == 1 else jnp.concatenate(parts, axis=0)


class VectorScatter:
    def __init__(self, hi_count, bufs, sems):
        self.hi_count = hi_count
        self.mine, self.from_core, self.from_y, self.from_z, self.own, self.other = bufs
        (self.c_send, self.c_recv, self.y_send, self.y_recv, self.z_send, self.z_recv, self.f_send,
         self.f_recv) = sems
        self.hi, self.mid, self.core, self.rep = place(hi_count)

    @staticmethod
    def scratch(hi_count):
        tile = (VEC_ROWS, LANES)
        dma = pltpu.SemaphoreType.DMA
        bufs = [
            pltpu.VMEM((hi_count, 2, 2) + tile, F32),
            pltpu.VMEM((hi_count, 2) + tile, F32),
            pltpu.VMEM((hi_count,) + tile, F32),
            pltpu.VMEM((hi_count - 1,) + tile, F32),
            pltpu.VMEM(tile, F32),
            pltpu.VMEM(tile, F32),
        ]
        return bufs, [dma((1,))] * 4 + [dma((hi_count - 1,))] * 2 + [dma((1,))] * 2

    def c_copy(self):
        device = shard_of(self.hi, self.mid, 1 - self.core)
        source = self.mine.at[:, :, 1 - self.core]
        return remote(source, self.from_core, self.c_send.at[0], self.c_recv.at[0], device)

    def y_copy(self):
        device = shard_of(self.hi, 1 - self.mid, self.core)
        source = self.mine.at[:, 1 - self.mid, self.core]
        return remote(source, self.from_y, self.y_send.at[0], self.y_recv.at[0], device)

    def z_copy(self, m):
        there = (self.hi + m) % self.hi_count
        source = self.mine.at[there, self.mid, self.core]
        sems = (self.z_send.at[m - 1], self.z_recv.at[m - 1])
        return remote(source, self.from_z.at[m - 1], *sems, shard_of(there, self.mid, self.core))

    def f_copy(self):
        return remote(self.own, self.other, self.f_send.at[0], self.f_recv.at[0], {"rep": 1 - self.rep})

    def step(self, number):
        if number == 0:
            self.c_copy().start()
        elif number == 1:
            self.c_copy().wait_recv()
            self.mine[:, :, self.core] = self.mine[:, :, self.core] + self.from_core[...]
            self.y_copy().start()
        elif number == 2:
            self.y_copy().wait_recv()
            self.mine[:, self.mid, self.core] = self.mine[:, self.mid, self.core] + self.from_y[...]
            for m in range(1, self.hi_count):
                self.z_copy(m).start()
        elif number == 3:
            total = self.mine[self.hi, self.mid, self.core]
            for m in range(1, self.hi_count):
                self.z_copy(m).wait_recv()
                total += self.from_z[m - 1]
            self.own[...] = total
            self.f_copy().start()
        else:
            self.f_copy().wait()
            self.c_copy().wait_send()
            self.y_copy().wait_send()
            for m in range(1, self.hi_count):
                self.z_copy(m).wait_send()


def spread_vectors(mine, rows, bias, depth):
    hi_count = mine.shape[0]
    for shard in range(4 * hi_count):
        at = shard // 4, shard // 2 % 2, shard % 2

        def piece(ref, some, start):
            tile = ref[some, tile_of(start)]
            shift = -start % LANES
            return pltpu.roll(tile, shift, 1) if shift else tile

        mine[at] = piece(rows, slice(None), shard * depth)
        for t in range(3):
            start = (3 * shard + t) * depth
            slab = start // D
            mine[at + (slice(t, t + 1),)] = piece(bias, slice(slab, slab + 1), start % D)


def backward_kernel(
    hi_count,
    full,
    d_ffn_in,
    d_second,
    first_in,
    normed_in,
    q_all,
    k_all,
    v_all,
    q_ext_all,
    active_all,
    slope_all,
    x_all,
    inv_std,
    context,
    k_doc,
    vectors,
    sums_two,
    cosine,
    sine,
    grads,
    from_core,
    input_grad,
    g_qkv,
    g_out,
    g_up,
    g_down,
    g_vec,
    down_buf,
    up_buf,
    d_context,
    peer_part,
    peer_sum,
    rows_grad,
    bias_grad,
    load_sem,
    flush_sem,
    w_sem,
    p_sem,
    *rest,
):
    rows = context.shape[0]
    depth = g_qkv.shape[0]
    scatter = Scatter(hi_count, depth, grads, from_core, rest[:9], rest[9:20])
    small = VectorScatter(hi_count, rest[20:26], rest[26:])
    hi, mid, core, rep = place(hi_count)
    scatter.own[...] = jnp.zeros_like(scatter.own)
    scatter.other[...] = jnp.zeros_like(scatter.other)
    rows_grad[...] = jnp.zeros_like(rows_grad)
    rows_grad[B_DOWN : B_DOWN + 3] = sums_two[...]
    entry_barrier(hi_count, hi, mid, core, rep)
    upper = hi_count // 2
    own_rows = pl.ds(pl.multiple_of(rep * rows, rows), rows)
    peer_rows = pl.ds(pl.multiple_of((1 - rep) * rows, rows), rows)

    def flush_rows(slab, half):
        return pltpu.make_async_copy(
            down_buf.at[half], grads.at[slab, pl.ds(half * upper, upper)], flush_sem.at[half]
        )

    def flush_columns(slab, half):
        columns = pl.ds(half * HALF, HALF)
        return pltpu.make_async_copy(
            up_buf.at[half], grads.at[slab, :, :, :, :, columns], flush_sem.at[2 + half]
        )

    def ffn_phase(slots, act, slope, d_ffn, first, normed):
        def weights(j, base):
            return [
                pltpu.make_async_copy(full.at[UP + 2 * j + s], slots.at[base + s], w_sem.at[base + s])
                for s in range(2)
            ]

        def kept(j, half):
            return [
                pltpu.make_async_copy(active_all.at[2 * j + half], act.at[half], load_sem.at[2 * half]),
                pltpu.make_async_copy(slope_all.at[2 * j + half], slope.at[half], load_sem.at[2 * half + 1]),
            ]

        others = [
            pltpu.make_async_copy(d_ffn_in, d_ffn, p_sem.at[0]),
            pltpu.make_async_copy(first_in, first, p_sem.at[1]),
            pltpu.make_async_copy(d_second, input_grad, p_sem.at[2]),
            pltpu.make_async_copy(normed_in, normed, p_sem.at[3]),
        ]
        for copy in others[:1] + weights(0, 0) + kept(0, 0) + kept(0, 1) + others[1:]:
            copy.start()
        for copy in others:
            copy.wait()

        @pl.loop(0, 4)
        def _(j):
            base = lax.rem(j, 2) * 2
            for copy in weights(j, base):
                copy.wait()

            @pl.when(j < 3)
            def _():
                for copy in weights(j + 1, 2 - base):
                    copy.start()

            for half in range(2):
                for copy in kept(j, half):
                    copy.wait()
                low = d_ffn[...]
                down = slots[base + 1, half * upper : (half + 1) * upper].reshape(HALF, D)
                d_hidden = (dot_nt(low, down) * slope[half].astype(F32)).astype(BF)
                columns = slice(half * HALF, (half + 1) * HALF)
                rows_grad[pl.ds(B_UP + j, 1), columns] = column_sum(d_hidden.astype(F32))
                g_rows = dot(act[half], low)
                g_columns = dot(first[...], d_hidden)

                @pl.when(j < 3)
                def _():
                    for copy in kept(j + 1, half):
                        copy.start()

                @pl.when(j > 0)
                def _():
                    if half == 0:
                        for h in range(2):
                            flush_rows(2 * j - 2, h).wait()
                            flush_columns(2 * j - 1, h).wait()
                        scatter.hand_over(2 * j - 2)
                        scatter.hand_over(2 * j - 1)

                down_buf[half] = g_rows.astype(BF).reshape(down_buf.shape[1:])
                up_buf[half] = g_columns.astype(BF).reshape(up_buf.shape[1:])
                flush_rows(2 * j, half).start()
                flush_columns(2 * j + 1, half).start()
                up = slots[base, :, :, :, :, columns].reshape(D, HALF)
                input_grad[...] += dot_nt(d_hidden, up)
                t = scatter.parts * (j - 1) + half
                if half < scatter.parts:
                    pl.when(t >= 0)(lambda: scatter.tick(t))

        w_out = pltpu.make_async_copy(full.at[3], slots.at[0], w_sem.at[0])
        w_out.start()
        for half in range(2):
            flush_rows(6, half).wait()
            flush_columns(7, half).wait()
        scatter.hand_over(6)
        scatter.hand_over(7)
        up = input_grad[...]
        normed_rows_ = normed[...]
        rows_grad[GAIN_ONE : GAIN_ONE + 1] = column_sum(up * normed_rows_)
        rows_grad[SHIFT_ONE : SHIFT_ONE + 1] = column_sum(up)
        grad = norm_back(up, normed_rows_, inv_std[:, 0:1], vectors[GAIN_ONE : GAIN_ONE + 1])
        input_grad[...] = grad
        d_attn = d_ffn
        d_attn[...] = grad.astype(BF)
        rows_grad[B_OUT : B_OUT + 1] = column_sum(d_attn[...].astype(F32))
        scatter.tick(3 * scatter.parts)
        w_out.wait()
        for half in range(2):
            columns = slice(half * HALF, (half + 1) * HALF)
            g_rows = dot_tn(context[:, columns], d_attn[...])
            down_buf[half] = g_rows.astype(BF).reshape(down_buf.shape[1:])
            flush_rows(8, half).start()
        d_context[...] = dot_nt(d_attn[...], slots[0].reshape(D, D)).astype(BF)
        for half in range(2):
            flush_rows(8, half).wait()
        scatter.hand_over(8)

    blocks = (hi_count, 2, 2, depth, D)
    pl.run_scoped(
        ffn_phase,
        pltpu.VMEM((4,) + blocks, BF),
        pltpu.VMEM((2, HALF, rows), BF),
        pltpu.VMEM((2, rows, HALF), BF),
        pltpu.VMEM((rows, D), BF),
        pltpu.VMEM((D, rows), BF),
        pltpu.VMEM((rows, D), F32),
    )
    early = 3 * scatter.parts + 1

    at = [min(early + HEADS // 2, 9 * scatter.parts)]

    def advance(handed):
        if at[0] < (9 + handed) * scatter.parts:
            scatter.tick(at[0])
            at[0] += 1

    def attention_phase(slots, q_in, k_in, v_in, ext_in, d_q, d_k, d_v, x):
        def quad(i, slot):
            return [
                pltpu.make_async_copy(q_all.at[i], q_in.at[slot], load_sem.at[slot]),
                pltpu.make_async_copy(k_all.at[i], k_in.at[slot], load_sem.at[2 + slot]),
                pltpu.make_async_copy(v_all.at[i], v_in.at[slot], load_sem.at[4 + slot]),
                pltpu.make_async_copy(q_ext_all.at[pl.ds(4 * i, 4)], ext_in.at[slot], load_sem.at[6 + slot]),
            ]

        weights = [pltpu.make_async_copy(full.at[s], slots.at[s], w_sem.at[s]) for s in range(3)]
        x_copy = pltpu.make_async_copy(x_all, x, w_sem.at[3])
        for copy in quad(0, 0) + weights + [x_copy]:
            copy.start()
        doc_k = k_doc[...]
        piece = 256

        def rope_back(a, table_rows):
            return a * cosine[table_rows, :] + swap_halves(a * sine[table_rows, :])

        @pl.loop(0, HEADS // 4)
        def _(i):
            slot = lax.rem(i, 2)
            for copy in quad(i, slot):
                copy.wait()

            @pl.when(i < HEADS // 4 - 1)
            def _():
                for copy in quad(i + 1, 1 - slot):
                    copy.start()

            for pair in range(2):
                lanes = slice(pair * LANES, (pair + 1) * LANES)
                wide = pl.ds(pl.multiple_of(i * QUAD + pair * LANES, LANES), LANES)
                k_pair, v_pair = k_in[slot, :, lanes], v_in[slot, :, lanes]
                k_lane = lax.broadcasted_iota(jnp.int32, k_pair.shape, 1)
                keys = jnp.concatenate([k_pair, doc_k], axis=1)
                minus = jnp.where(k_lane < 3, -1.0, 0.0).astype(BF)
                values = jnp.concatenate([v_pair, minus], axis=1)
                dk = dv = None
                for start in range(0, rows, piece):
                    part = slice(start, start + piece)
                    q_pair, g_pair = q_in[slot, part, lanes], d_context[part, wide]
                    lane = lax.broadcasted_iota(jnp.int32, q_pair.shape, 1)
                    product = g_pair.astype(F32) * context[part, wide].astype(F32)
                    dq = None
                    for head in range(2):
                        in_head = (lane // HEAD_DIM) == head
                        q_head = jnp.where(in_head, q_pair, 0)
                        g_head = jnp.where(in_head, g_pair, 0)
                        inner = jnp.sum(jnp.where(in_head, product, 0.0), axis=1, keepdims=True)
                        top, middle, low = split3(jnp.broadcast_to(inner, q_pair.shape))
                        g_ext = jnp.where(lane == 0, top, jnp.where(lane == 1, middle, low))
                        g_ext = jnp.where(lane < 3, g_ext, 0)
                        q_wide = jnp.concatenate([q_head, ext_in[slot, pair * 2 + head, part, :]], axis=1)
                        prob = jnp.exp(dot_nt(keys, q_wide))
                        d_prob = dot_nt(values, jnp.concatenate([g_head, g_ext], axis=1))
                        d_score = (prob * d_prob).astype(BF)
                        dv_part = dot(prob.astype(BF), g_head)
                        dk_part = dot(d_score, q_head)
                        k_head = jnp.where((k_lane // HEAD_DIM) == head, k_pair, 0)
                        dq_part = dot_tn(d_score, k_head)
                        dv = dv_part if dv is None else dv + dv_part
                        dk = dk_part if dk is None else dk + dk_part
                        dq = dq_part if dq is None else dq + dq_part
                    table_rows = pl.ds(pl.multiple_of(rep * rows + start, piece), piece)
                    d_q[part, wide] = rope_back(dq * HEAD_DIM**-0.5, table_rows).astype(BF)
                d_k[:rows, wide] = rope_back(dk[:rows], own_rows).astype(BF)
                d_k[rows:, wide] = rope_back(dk[rows:], peer_rows).astype(BF)
                d_v[:, wide] = dv.astype(BF)
                t = early + 2 * i + pair
                pl.when(t < 9 * scatter.parts)(lambda: scatter.tick(t))

        for copy in weights + [x_copy]:
            copy.wait()
        def slab_grad(s, count, d_rows):
            for half in range(2):
                columns = slice(half * HALF, (half + 1) * HALF)
                if s > 0:
                    flush_columns(8 + s, half).wait()
                g_columns = dot(x[:, :count], d_rows[:, columns])
                up_buf[half] = g_columns.astype(BF).reshape(up_buf.shape[1:])
                flush_columns(9 + s, half).start()
            if s > 0:
                scatter.hand_over(8 + s)
            bias_grad[s : s + 1] = column_sum(d_rows[...].astype(F32))

        slab_grad(0, rows, d_q)
        advance(0)
        slab_grad(1, 2 * rows, d_k)
        advance(1)
        slab_grad(2, 2 * rows, d_v)
        advance(2)
        w_k, w_v = slots[1].reshape(D, D), slots[2].reshape(D, D)
        peer_part[...] = (dot_nt(d_k[rows:], w_k) + dot_nt(d_v[rows:], w_v)).astype(BF)
        peer_copy = remote(peer_part, peer_sum, p_sem.at[4], p_sem.at[5], {"rep": 1 - rep})
        peer_copy.start()
        for half in range(2):
            flush_columns(11, half).wait()
        scatter.hand_over(11)
        advance(3)
        spread_vectors(small.mine, rows_grad, bias_grad, depth)
        small.step(0)
        advance(3)
        small.step(1)
        input_grad[...] += dot_nt(d_q[...], slots[0].reshape(D, D))
        advance(3)
        input_grad[...] += dot_nt(d_k[:rows], w_k)
        advance(3)
        small.step(2)
        input_grad[...] += dot_nt(d_v[:rows], w_v)
        peer_copy.wait()
        input_grad[...] += peer_sum[...].astype(F32)

    pl.run_scoped(
        attention_phase,
        pltpu.VMEM((3,) + blocks, BF),
        pltpu.VMEM((2, rows, QUAD), BF),
        pltpu.VMEM((2, 2 * rows, QUAD), BF),
        pltpu.VMEM((2, 2 * rows, QUAD), BF),
        pltpu.VMEM((2, 4, rows, LANES), BF),
        pltpu.VMEM((rows, D), BF),
        pltpu.VMEM((2 * rows, D), BF),
        pltpu.VMEM((2 * rows, D), BF),
        pltpu.VMEM((D, 2 * rows), BF),
    )

    for t in range(at[0], scatter.count + scatter.stages[-2]):
        scatter.tick(t)

    small.step(3)
    for s in range(3):
        g_qkv[:, s * D : (s + 1) * D] = scatter.whole(9 + s, slice(None))
    g_out[...] = scatter.whole(8, slice(None))
    each = LANES // depth
    for j in range(4):
        g_down[j * depth : (j + 1) * depth] = scatter.whole(2 * j, slice(None))
    for t in range(FF // LANES):
        pieces = []
        for u in range(each):
            shard, j = divmod(t * each + u, 4)
            pieces.append((scatter.whole(2 * j + 1, tile_of(shard * depth)), shard * depth % LANES))
        g_up[:, t * LANES : (t + 1) * LANES] = regroup(pieces, depth)
    small.step(4)
    g_vec[...] = small.own[...] + small.other[...]
    scatter.drain()


def backward(hi_count, full, arrays, kept):
    context, depth = kept[1], full.shape[4]
    rows = context.shape[0]
    anywhere = pl.BlockSpec(memory_space=pl.ANY)
    vmem = pl.BlockSpec(memory_space=pltpu.VMEM)
    dma = pltpu.SemaphoreType.DMA
    shape = jax.ShapeDtypeStruct
    blocks = (hi_count, 2, 2, depth)
    parts = Gather.parts_of(depth, SWAP)
    bufs, sems = Scatter.scratch(hi_count, depth)
    small_bufs, small_sems = VectorScatter.scratch(hi_count)
    return pl.pallas_call(
        functools.partial(backward_kernel, hi_count),
        out_shape=(
            shape((SLABS,) + blocks + (D,), BF),
            shape((SLABS * parts, hi_count, 2, depth // parts, D), BF),
            shape((rows, D), F32),
            shape((depth, 3 * D), F32),
            shape((depth, D), F32),
            shape((depth, FF), F32),
            shape((4 * depth, D), F32),
            shape((VEC_ROWS, LANES), F32),
        ),
        in_specs=[anywhere] * (1 + len(arrays)) + [vmem] * len(kept),
        out_specs=(anywhere,) * 2 + (vmem,) * 6,
        scratch_shapes=[
            pltpu.VMEM((2, hi_count // 2, 2, 2, depth, D), BF),
            pltpu.VMEM((2,) + blocks + (HALF,), BF),
            pltpu.VMEM((rows, D), BF),
            pltpu.VMEM((rows, D), BF),
            pltpu.VMEM((rows, D), BF),
            pltpu.VMEM((VEC_ROWS, D), F32),
            pltpu.VMEM((3, D), F32),
            dma((8,)),
            dma((4,)),
            dma((4,)),
            dma((6,)),
        ]
        + bufs
        + sems
        + small_bufs
        + small_sems,
        compiler_params=pltpu.CompilerParams(
            collective_id=1, has_side_effects=True, vmem_limit_bytes=VMEM
        ),
        name="backward",
    )(full, *arrays, *kept)


def rope_tables(count):
    position = np.arange(count, dtype=np.float32)
    frequency = np.exp(np.arange(HEAD_DIM // 2, dtype=np.float32) * np.float32(-2.0 * math.log(10000.0) / HEAD_DIM))
    angles = position[:, None] * frequency[None, :].astype(np.float32)
    cosine, sine = np.cos(angles).astype(np.float32), np.sin(angles).astype(np.float32)
    return (
        jnp.asarray(np.concatenate([cosine] * 4, axis=1)),
        jnp.asarray(np.concatenate([-sine, sine, -sine, sine], axis=1)),
    )


def local(
    tokens,
    segments,
    cotangent,
    w_qkv,
    b_qkv,
    w_out,
    b_out,
    gain_one,
    shift_one,
    w_up,
    b_up,
    w_down,
    b_down,
    gain_two,
    shift_two,
):
    rows = tokens.shape[0]
    shards = lax.axis_size("shard")
    hi_count = shards // 4
    depth = D // shards
    small = (b_qkv, b_out, gain_one, shift_one, b_up, b_down, gain_two, shift_two)
    widths = [a.shape[0] for a in small]
    vec = jnp.concatenate(small + (jnp.zeros((VEC_ROWS * depth - sum(widths),), F32),))
    vec = jnp.tile(vec.reshape(VEC_ROWS, depth), (1, LANES // depth))
    lane = jnp.arange(LANES, dtype=jnp.int32)[None, :]
    q_doc = (segments[:, None] == lane).astype(BF)
    cosine, sine = rope_tables(2 * rows)
    (
        full, q, k, v, q_ext, active, slope, x_all, k_doc, context, first, normed, inv_std, result,
        d_second, d_ffn, sums_two, vectors,
    ) = forward(hi_count, (w_qkv, w_out, w_up, w_down), vec[None], tokens, cotangent, q_doc, cosine, sine)
    _, _, input_grad, g_qkv, g_out, g_up, g_down, g_vec = backward(
        hi_count,
        full,
        (d_ffn, d_second, first, normed, q, k, v, q_ext, active, slope, x_all),
        (inv_std, context, k_doc, vectors, sums_two, cosine, sine),
    )
    outs = []
    at = 0
    for width in widths:
        count = width // depth
        outs.append(g_vec[at : at + count, :depth].reshape(width))
        at += count
    return (
        result,
        input_grad,
        g_qkv,
        outs[0],
        g_out,
        outs[1],
        outs[2],
        outs[3],
        g_up,
        outs[4],
        g_down,
        outs[5],
        outs[6],
        outs[7],
    )


def solution(mesh):
    act = P(("shard", "rep"), None)
    matrix = P("shard", None)
    vector = P("shard")
    params = (matrix, vector, matrix, vector, vector, vector, matrix, vector, matrix, vector, vector, vector)
    return jax.shard_map(
        local,
        mesh=mesh,
        in_specs=(act, P(("shard", "rep")), act) + params,
        out_specs=(act, act) + params,
        check_vma=False,
    )
```

```python
import functools
import math

import jax
import jax.numpy as jnp
import numpy as np
from jax import lax
from jax.experimental import pallas as pl
from jax.experimental.pallas import tpu as pltpu
from jax.sharding import PartitionSpec as P

D = 1024
HEADS = 16
HEAD_DIM = 64
FF = 4096
SLABS = 12
LANES = 128
MASKED = -1e30
MESH = pl.DeviceIdType.MESH
VMEM = 60 * 1024 * 1024
BF = jnp.bfloat16
F32 = jnp.float32

ERFC_P = 0.33
ERFC_Q = (
    0.1863661,
    0.182837329,
    0.20192357,
    0.0450108379,
    0.412542064,
    -0.355440048,
    0.462689118,
    -0.135929052,
)


def dot(a, b):
    return lax.dot_general(a, b, (((1,), (0,)), ((), ())), preferred_element_type=F32)


def dot_nt(a, b):
    return lax.dot_general(a, b, (((1,), (1,)), ((), ())), preferred_element_type=F32)


def dot_tn(a, b):
    return lax.dot_general(a, b, (((0,), (0,)), ((), ())), preferred_element_type=F32)


def swap_halves(a):
    width = a.shape[1]
    lane = lax.broadcasted_iota(jnp.int32, a.shape, 1) % HEAD_DIM
    return jnp.where(
        lane < HEAD_DIM // 2,
        pltpu.roll(a, width - HEAD_DIM // 2, 1),
        pltpu.roll(a, HEAD_DIM // 2, 1),
    )


def split3(a):
    hi = a.astype(BF)
    rest = a - hi.astype(F32)
    mid = rest.astype(BF)
    low = (rest - mid.astype(F32)).astype(BF)
    return hi, mid, low


def remote(src, dst, send, recv, device):
    return pltpu.make_async_remote_copy(
        src_ref=src, dst_ref=dst, send_sem=send, recv_sem=recv, device_id=device, device_id_type=MESH
    )


def place(hi_count):
    index = lax.axis_index("shard")
    return index // 4, (index // 2) % 2, index % 2, lax.axis_index("rep")


def shard_of(hi, mid, core):
    return {"shard": hi * 4 + mid * 2 + core}


def entry_barrier(hi_count, hi, mid, core, rep):
    barrier = pltpu.get_barrier_semaphore()
    for m in range(1, hi_count):
        pl.semaphore_signal(
            barrier, inc=1, device_id=shard_of((hi + m) % hi_count, mid, core), device_id_type=MESH
        )
    pl.semaphore_signal(barrier, inc=1, device_id=shard_of(hi, 1 - mid, core), device_id_type=MESH)
    pl.semaphore_signal(barrier, inc=1, device_id=shard_of(hi, mid, 1 - core), device_id_type=MESH)
    pl.semaphore_signal(barrier, inc=1, device_id={"rep": 1 - rep}, device_id_type=MESH)
    pl.semaphore_wait(barrier, hi_count + 2)


SWAP = 256
PARTS = 2


def normed_rows(residual):
    mean_val = jnp.mean(residual, axis=-1, keepdims=True)
    centred = residual - mean_val
    variance = jnp.mean(centred * centred, axis=-1, keepdims=True)
    inv_std = lax.rsqrt(variance + 1e-05)
    return centred * inv_std, inv_std


def norm_back(upstream, normed, inv_std, gain_vec):
    scaled = upstream * gain_vec
    return inv_std * (
        scaled
        - jnp.mean(scaled, axis=-1, keepdims=True)
        - normed * jnp.mean(scaled * normed, axis=-1, keepdims=True)
    )


def column_sum(a):
    return jnp.sum(a, axis=0, keepdims=True)


class Gather:
    def __init__(self, hi_count, packed, full, sems, swap=SWAP):
        self.hi_count = hi_count
        self.packed, self.full = packed, full
        (self.up_send, self.up_recv, self.down_send, self.down_recv, self.y_send, self.y_recv,
         self.x_send, self.x_recv, self.c_send, self.c_recv) = sems
        self.hi, self.mid, self.core, self.rep = place(hi_count)
        slabs, self.depth, width = packed.shape
        self.parts = self.parts_of(self.depth, swap)
        self.rows = self.depth // self.parts
        self.count = slabs * self.parts
        self.swap = swap
        self.mine = slice(None)
        if swap:
            self.mine = pl.ds(pl.multiple_of(self.rep * swap, LANES), width - swap)

    @staticmethod
    def parts_of(depth, swap):
        return PARTS if swap and depth % (16 * PARTS) == 0 else 1

    @staticmethod
    def scratch(hi_count, slabs, depth, swap=SWAP):
        count = slabs * Gather.parts_of(depth, swap)
        dma = pltpu.SemaphoreType.DMA
        hops = dma((count, hi_count - 1))
        return [hops] * 4 + [dma((count, hi_count))] * 2 + [dma((count,))] * 2 + [dma((count, 2))] * 2

    def only(self, which):
        return pl.ds(pl.multiple_of(which * (D - self.swap), LANES), self.swap)

    def spot(self, chunk):
        start = (chunk % self.parts) * self.rows
        if not isinstance(start, int):
            start = pl.multiple_of(start, self.rows)
        return chunk // self.parts, pl.ds(start, self.rows)

    def hop(self, chunk, distance, up):
        slab, rows = self.spot(chunk)
        origin = self.hi - distance if up else self.hi + distance
        block = self.full.at[slab, origin, self.mid, self.core, rows, self.mine]
        source = self.packed.at[slab, rows, self.mine] if distance == 0 else block
        send, recv = (self.up_send, self.up_recv) if up else (self.down_send, self.down_recv)
        device = shard_of(self.hi + 1 if up else self.hi - 1, self.mid, self.core)
        return remote(source, block, send.at[chunk, distance], recv.at[chunk, distance], device)

    def landed_hop(self, chunk, distance, up):
        slab, rows = self.spot(chunk)
        origin = self.hi - distance - 1 if up else self.hi + distance + 1
        block = self.full.at[slab, origin, self.mid, self.core, rows, self.mine]
        send, recv = (self.up_send, self.up_recv) if up else (self.down_send, self.down_recv)
        device = shard_of(self.hi, self.mid, self.core)
        return remote(block, block, send.at[chunk, distance], recv.at[chunk, distance], device)

    def sends(self, distance, up):
        if up:
            return (self.hi - distance >= 0) & (self.hi + 1 < self.hi_count)
        return (self.hi + distance < self.hi_count) & (self.hi - 1 >= 0)

    def lands(self, distance, up):
        if up:
            return self.hi - distance - 1 >= 0
        return self.hi + distance + 1 < self.hi_count

    def y_copy(self, chunk, origin, landed):
        slab, rows = self.spot(chunk)
        which = 1 - self.mid if landed else self.mid
        block = self.full.at[slab, origin, which, self.core, rows, self.mine]
        device = shard_of(self.hi, 1 - self.mid, self.core)
        return remote(block, block, self.y_send.at[chunk, origin], self.y_recv.at[chunk, origin], device)

    def x_copy(self, chunk, landed):
        slab, rows = self.spot(chunk)
        columns = self.only(1 - self.rep if landed else self.rep)
        block = self.full.at[slab, :, :, self.core, rows, columns]
        return remote(block, block, self.x_send.at[chunk], self.x_recv.at[chunk], {"rep": 1 - self.rep})

    def c_copy(self, chunk, part, landed):
        slab, rows = self.spot(chunk)
        which = 1 - self.core if landed else self.core
        columns = self.mine if part == 0 else self.only(1 - self.rep)
        block = self.full.at[slab, :, :, which, rows, columns]
        device = shard_of(self.hi, self.mid, 1 - self.core)
        return remote(block, block, self.c_send.at[chunk, part], self.c_recv.at[chunk, part], device)

    @property
    def lag(self):
        return 2 * self.hi_count + 4

    def own_copy(self, sem):
        target = self.full.at[:, self.hi, self.mid, self.core, :, self.mine]
        return pltpu.make_async_copy(self.packed.at[:, :, self.mine], target, sem)

    def tick(self, t):
        def stage(offset, act):
            if not isinstance(t, int):
                chunk = t - offset
                pl.when((chunk >= 0) & (chunk < self.count))(lambda: act(chunk))
            elif 0 <= t - offset < self.count:
                act(t - offset)

        def own(chunk):
            for up in (True, False):
                pl.when(self.sends(0, up))(lambda: self.hop(chunk, 0, up).start())
            self.y_copy(chunk, self.hi, False).start()

        def forward(distance, chunk):
            for up in (True, False):
                @pl.when(self.lands(distance - 1, up))
                def _():
                    self.landed_hop(chunk, distance - 1, up).wait_recv()
                    origin = self.hi - distance if up else self.hi + distance
                    self.y_copy(chunk, origin, False).start()

                if distance < self.hi_count - 1:
                    pl.when(self.sends(distance, up))(lambda: self.hop(chunk, distance, up).start())

        def after_y(chunk):
            for origin in range(self.hi_count):
                self.y_copy(chunk, origin, True).wait_recv()
            if self.swap:
                self.x_copy(chunk, False).start()
            self.c_copy(chunk, 0, False).start()

        def after_x(chunk):
            if self.swap:
                self.x_copy(chunk, True).wait_recv()
                self.c_copy(chunk, 1, False).start()

        def after_c(chunk):
            for part in range(2 if self.swap else 1):
                self.c_copy(chunk, part, True).wait_recv()

        stage(0, own)
        for distance in range(1, self.hi_count):
            stage(2 * distance, functools.partial(forward, distance))
        stage(2 * self.hi_count, after_y)
        stage(2 * self.hi_count + 2, after_x)
        stage(2 * self.hi_count + 4, after_c)

    def drain(self):
        @pl.loop(0, self.count)
        def _(chunk):
            for distance in range(self.hi_count - 1):
                for up in (True, False):
                    pl.when(self.sends(distance, up))(
                        lambda: self.hop(chunk, distance, up).wait_send()
                    )
            for origin in range(self.hi_count):
                self.y_copy(chunk, origin, False).wait_send()
            if self.swap:
                self.x_copy(chunk, False).wait_send()
            for part in range(2 if self.swap else 1):
                self.c_copy(chunk, part, False).wait_send()


def near_barrier(hi_count):
    hi, mid, core, rep = place(hi_count)
    barrier = pltpu.get_barrier_semaphore()

    def greet(device):
        pl.semaphore_signal(barrier, inc=1, device_id=device, device_id_type=MESH)

    pl.when(hi + 1 < hi_count)(lambda: greet(shard_of(hi + 1, mid, core)))
    pl.when(hi - 1 >= 0)(lambda: greet(shard_of(hi - 1, mid, core)))
    greet(shard_of(hi, 1 - mid, core))
    greet(shard_of(hi, mid, 1 - core))
    greet({"rep": 1 - rep})
    first, last = hi == 0, hi == hi_count - 1
    pl.semaphore_wait(barrier, 5 - first.astype(jnp.int32) - last.astype(jnp.int32))


UP, DOWN = 4, 8
HALF = D // 2
QUAD = 4 * HEAD_DIM
B_OUT, GAIN_ONE, SHIFT_ONE, B_UP, B_DOWN, GAIN_TWO, SHIFT_TWO = 3, 4, 5, 6, 10, 11, 12
VEC_ROWS = 16


def regroup(pieces, depth):
    out = None
    for u, (tile, start) in enumerate(pieces):
        shift = (u * depth - start) % LANES
        moved = pltpu.roll(tile, shift, 1) if shift else tile
        lane = lax.broadcasted_iota(jnp.int32, moved.shape, 1)
        out = moved if out is None else jnp.where(lane // depth == u, moved, out)
    return out


def tile_of(at):
    return slice(at // LANES * LANES, at // LANES * LANES + LANES)


def pack(packed, w_qkv, w_out, w_up, w_down):
    depth = w_qkv.shape[0]
    for slab in range(3):
        packed[slab] = w_qkv[:, slab * D : (slab + 1) * D].astype(BF)
    packed[3] = w_out[...].astype(BF)
    each = LANES // depth
    for j in range(4):
        packed[DOWN + j] = w_down[j * depth : (j + 1) * depth].astype(BF)
        for t in range(D // LANES):
            starts = [4 * depth * (t * each + u) + depth * j for u in range(each)]
            pieces = [(w_up[:, tile_of(at)], at % LANES) for at in starts]
            packed[UP + j, :, t * LANES : (t + 1) * LANES] = regroup(pieces, depth).astype(BF)


def unpack_vectors(vec_full, rows_out, bias, depth):
    hi_count = vec_full.shape[1]
    each = LANES // depth

    def of_shard(shard):
        return vec_full[0, shard // 4, shard // 2 % 2, shard % 2].astype(BF).astype(F32)

    def join(pieces):
        lane = lax.broadcasted_iota(jnp.int32, pieces[0].shape, 1)
        out = pieces[0]
        for u in range(1, each):
            out = jnp.where(lane // depth == u, pieces[u], out)
        return out

    for t in range(D // LANES):
        tile = slice(t * LANES, (t + 1) * LANES)
        rows_out[:, tile] = join([of_shard(t * each + u) for u in range(each)])
        for j in range(3):
            chunks = [(j * D + t * LANES) // depth + u for u in range(each)]
            bias[j : j + 1, tile] = join([of_shard(m // 3)[m % 3 : m % 3 + 1] for m in chunks])


def gelu_parts(hidden):
    gauss = jnp.exp(hidden * hidden * -0.5)
    t = 1.0 / (1.0 + (ERFC_P * math.sqrt(0.5)) * jnp.abs(hidden))
    poly = jnp.full_like(t, ERFC_Q[-1])
    for coefficient in ERFC_Q[-2::-1]:
        poly = poly * t + coefficient
    tail = 0.5 * t * poly * gauss
    cdf = jnp.where(hidden >= 0, 1.0 - tail, tail)
    return hidden * cdf, cdf + hidden * gauss * (1.0 / math.sqrt(2.0 * math.pi))


def forward_kernel(
    hi_count,
    w_qkv,
    w_out,
    w_up,
    w_down,
    vec,
    tokens,
    cotangent,
    q_doc,
    cosine,
    sine,
    full,
    q_all,
    k_all,
    v_all,
    q_ext_all,
    active_all,
    slope_all,
    x_all,
    k_doc,
    context,
    first_turned,
    normed_out,
    inv_out,
    result,
    d_second,
    d_ffn,
    sums,
    vectors,
    packed,
    vec_full,
    x_peer,
    slots,
    q_buf,
    k_buf,
    v_buf,
    ext_buf,
    first,
    first_low,
    turned,
    total,
    act_buf,
    turned_act,
    slope_buf,
    bias,
    local_sem,
    load_sem,
    flush_sem,
    t_sem,
    *sems,
):
    rows = tokens.shape[0]
    depth = w_qkv.shape[0]
    rep = lax.axis_index("rep")
    gather = Gather(hi_count, packed, full, sems[:10])
    small = Gather(hi_count, vec, vec_full, sems[10:], swap=0)
    lane_doc = lax.broadcasted_iota(jnp.int32, (rows, LANES), 1)
    other = jnp.where(q_doc[...] > 0.5, 0.0, MASKED)
    other = jnp.where(lane_doc < 61, other, jnp.where(lane_doc < 64, 1.0, 0.0))
    k_doc[:rows] = other.astype(BF)
    pack(packed, w_qkv, w_out, w_up, w_down)
    near_barrier(hi_count)
    peer = {"rep": 1 - rep}
    token_copy = remote(tokens, x_peer, t_sem.at[0], t_sem.at[1], peer)
    doc_copy = remote(k_doc.at[:rows], k_doc.at[rows:], t_sem.at[2], t_sem.at[3], peer)
    copies = [small.own_copy(local_sem.at[0]), gather.own_copy(local_sem.at[1])]
    for copy in copies:
        copy.start()
    doc_copy.start()
    token_copy.start()
    for copy in copies:
        copy.wait()
    warm = gather.lag + 1
    for t in range(warm):
        small.tick(t)
        gather.tick(t)
    unpack_vectors(vec_full, vectors, bias, depth)
    doc_copy.wait()
    token_copy.wait()
    turned[:, :rows] = tokens[...].T
    turned[:, rows:] = x_peer[...].T
    x_copy = pltpu.make_async_copy(turned, x_all, local_sem.at[0])
    x_copy.start()
    ready = 3 * gather.parts + gather.lag

    @pl.loop(warm, ready)
    def _(t):
        gather.tick(t)

    def load_whole(slab, slot):
        return pltpu.make_async_copy(full.at[slab], slots.at[slot], load_sem.at[slot])

    for slab in range(3):
        load_whole(slab, slab).start()
    for slab in range(3):
        load_whole(slab, slab).wait()

    def weight(slot, columns):
        return slots[slot, :, :, :, :, columns].reshape(D, -1)

    own_rows = pl.ds(pl.multiple_of(rep * rows, rows), rows)
    peer_rows = pl.ds(pl.multiple_of((1 - rep) * rows, rows), rows)

    def rope(a, table_rows):
        cos_part, sin_part = cosine[table_rows, :], sine[table_rows, :]
        cos_part = jnp.concatenate([cos_part, cos_part], axis=1)
        sin_part = jnp.concatenate([sin_part, sin_part], axis=1)
        return a * cos_part + swap_halves(a) * sin_part

    def flushes(i):
        return [
            pltpu.make_async_copy(q_buf.at[i], q_all.at[i], flush_sem.at[0, i]),
            pltpu.make_async_copy(k_buf.at[i], k_all.at[i], flush_sem.at[1, i]),
            pltpu.make_async_copy(v_buf.at[i], v_all.at[i], flush_sem.at[2, i]),
            pltpu.make_async_copy(
                ext_buf.at[pl.ds(4 * i, 4)], q_ext_all.at[pl.ds(4 * i, 4)], flush_sem.at[3, i]
            ),
        ]

    ones = jnp.ones((2 * rows, LANES), BF)
    piece = 256

    @pl.loop(0, HEADS // 4)
    def _(i):
        columns = pl.ds(pl.multiple_of(i * QUAD, QUAD), QUAD)
        own_x, peer_x = tokens[...], x_peer[...]
        w = weight(0, columns)
        q_rows = rope(dot(own_x, w) + bias[0:1, columns], own_rows) * HEAD_DIM**-0.5
        q_buf[i] = q_rows.astype(BF)
        w = weight(1, columns)
        k_buf[i, :rows] = rope(dot(own_x, w) + bias[1:2, columns], own_rows).astype(BF)
        k_buf[i, rows:] = rope(dot(peer_x, w) + bias[1:2, columns], peer_rows).astype(BF)
        w = weight(2, columns)
        v_buf[i, :rows] = (dot(own_x, w) + bias[2:3, columns]).astype(BF)
        v_buf[i, rows:] = (dot(peer_x, w) + bias[2:3, columns]).astype(BF)
        for pair in range(2):
            gather.tick(ready + 2 * i + pair)
            lanes = slice(pair * LANES, (pair + 1) * LANES)
            keys = jnp.concatenate([k_buf[i, :, lanes], k_doc[...]], axis=1)
            values = jnp.concatenate([v_buf[i, :, lanes], ones], axis=1)
            for start in range(0, rows, piece):
                part = slice(start, start + piece)
                q_pair = q_buf[i, part, lanes]
                lane = lax.broadcasted_iota(jnp.int32, q_pair.shape, 1)
                doc_q = q_doc[part, :]
                mixed = []
                for head in range(2):
                    in_head = (lane // HEAD_DIM) == head
                    queries = jnp.concatenate([jnp.where(in_head, q_pair, 0), doc_q], axis=1)
                    scores = dot_nt(queries, keys)
                    row_max = jnp.max(scores, axis=1, keepdims=True)
                    prob = jnp.exp(scores - row_max).astype(BF)
                    both = dot(prob, values)
                    row_sum = both[:, LANES:]
                    mixed.append(both[:, :LANES] / row_sum)
                    hi, mid, low = split3(-(row_max + jnp.log(row_sum)))
                    ext = jnp.where(lane == 61, hi, doc_q)
                    ext = jnp.where(lane == 62, mid, ext)
                    ext = jnp.where(lane == 63, low, ext)
                    ext_buf[4 * i + pair * 2 + head, part, :] = ext
                pair_lanes = pl.ds(pl.multiple_of(i * QUAD + pair * LANES, LANES), LANES)
                context[part, pair_lanes] = jnp.where(lane < HEAD_DIM, mixed[0], mixed[1]).astype(BF)
        for copy in flushes(i):
            copy.start()

    done = ready + HEADS // 2

    def vector(row):
        return vectors[row : row + 1, :]

    load_whole(3, 3).start()
    load_whole(UP, 0).start()
    load_whole(3, 3).wait()
    attn = dot(context[...], weight(3, slice(None))) + vector(B_OUT)
    normed, inv_std = normed_rows(tokens[...].astype(F32) + attn)
    first[...] = normed * vector(GAIN_ONE) + vector(SHIFT_ONE)
    first_low[...] = first[...].astype(BF)
    first_turned[...] = first_low[...].T
    normed_out[...] = normed
    inv_out[...] = jnp.broadcast_to(inv_std, inv_out.shape)
    total[...] = first[...] + vector(B_DOWN)

    def keeps(j, half):
        return [
            pltpu.make_async_copy(
                turned_act.at[half], active_all.at[2 * j + half], flush_sem.at[4, 2 * half]
            ),
            pltpu.make_async_copy(
                slope_buf.at[half], slope_all.at[2 * j + half], flush_sem.at[4, 2 * half + 1]
            ),
        ]

    gather.tick(done)

    @pl.loop(0, 4)
    def _(j):
        slot = lax.rem(j, 2)
        load_whole(UP + j, slot).wait()
        for half in range(2):
            @pl.when(j > 0)
            def _():
                for copy in keeps(j - 1, half):
                    copy.wait()

            columns = slice(half * HALF, (half + 1) * HALF)
            hidden = dot(first_low[...], weight(slot, columns)) + vectors[pl.ds(B_UP + j, 1), columns]
            act, slope = gelu_parts(hidden)
            act = act.astype(BF)
            act_buf[2 * j + half] = act
            turned_act[half] = act.T
            slope_buf[half] = slope.astype(BF)
            for copy in keeps(j, half):
                copy.start()
            gather.tick(done + 1 + 2 * j + half)
        load_whole(UP + j + 1, 1 - slot).start()

    @pl.loop(0, 4)
    def _(j):
        slot = lax.rem(j, 2)
        load_whole(DOWN + j, slot).wait()

        @pl.when(j == 0)
        def _():
            for t in range(done + 9, gather.count + gather.lag):
                gather.tick(t)

        @pl.when(j < 3)
        def _():
            load_whole(DOWN + j + 1, 1 - slot).start()

        for half in range(2):
            down = slots[slot, half * (hi_count // 2) : (half + 1) * (hi_count // 2)].reshape(HALF, D)
            total[...] += dot(act_buf[2 * j + half], down)

    for half in range(2):
        for copy in keeps(3, half):
            copy.wait()
    gain = vector(GAIN_TWO)
    normed, inv_std = normed_rows(total[...])
    result[...] = (normed * gain + vector(SHIFT_TWO)).astype(BF)
    up = cotangent[...].astype(F32)
    sums[1:2] = column_sum(up * normed)
    sums[2:3] = column_sum(up)
    grad = norm_back(up, normed, inv_std, gain)
    d_second[...] = grad
    low = grad.astype(BF)
    d_ffn[...] = low
    sums[0:1] = column_sum(low.astype(F32))
    x_copy.wait()
    small.drain()
    gather.drain()

    @pl.loop(0, HEADS // 4)
    def _(i):
        for copy in flushes(i):
            copy.wait()


def forward(hi_count, weights, vec, tokens, cotangent, q_doc, cosine, sine):
    rows = tokens.shape[0]
    depth = weights[0].shape[0]
    anywhere = pl.BlockSpec(memory_space=pl.ANY)
    vmem = pl.BlockSpec(memory_space=pltpu.VMEM)
    dma = pltpu.SemaphoreType.DMA
    quads = HEADS // 4
    shape = jax.ShapeDtypeStruct
    blocks = (hi_count, 2, 2, depth, D)
    return pl.pallas_call(
        functools.partial(forward_kernel, hi_count),
        out_shape=(
            shape((SLABS,) + blocks, BF),
            shape((quads, rows, QUAD), BF),
            shape((quads, 2 * rows, QUAD), BF),
            shape((quads, 2 * rows, QUAD), BF),
            shape((HEADS, rows, LANES), BF),
            shape((8, HALF, rows), BF),
            shape((8, rows, HALF), BF),
            shape((D, 2 * rows), BF),
            shape((2 * rows, LANES), BF),
            shape((rows, D), BF),
            shape((D, rows), BF),
            shape((rows, D), F32),
            shape((rows, LANES), F32),
            shape((rows, D), BF),
            shape((rows, D), F32),
            shape((rows, D), BF),
            shape((3, D), F32),
            shape((VEC_ROWS, D), F32),
        ),
        in_specs=[vmem] * 10,
        out_specs=(anywhere,) * 8 + (vmem,) * 10,
        scratch_shapes=[
            pltpu.VMEM((SLABS, depth, D), BF),
            pltpu.VMEM((1, hi_count, 2, 2) + vec.shape[1:], F32),
            pltpu.VMEM((rows, D), BF),
            pltpu.VMEM((4,) + blocks, BF),
            pltpu.VMEM((quads, rows, QUAD), BF),
            pltpu.VMEM((quads, 2 * rows, QUAD), BF),
            pltpu.VMEM((quads, 2 * rows, QUAD), BF),
            pltpu.VMEM((HEADS, rows, LANES), BF),
            pltpu.VMEM((rows, D), F32),
            pltpu.VMEM((rows, D), BF),
            pltpu.VMEM((D, 2 * rows), BF),
            pltpu.VMEM((rows, D), F32),
            pltpu.VMEM((8, rows, HALF), BF),
            pltpu.VMEM((2, HALF, rows), BF),
            pltpu.VMEM((2, rows, HALF), BF),
            pltpu.VMEM((3, D), F32),
            dma((2,)),
            dma((4,)),
            dma((5, quads)),
            dma((4,)),
        ]
        + Gather.scratch(hi_count, SLABS, depth)
        + Gather.scratch(hi_count, 1, vec.shape[1], swap=0),
        compiler_params=pltpu.CompilerParams(
            collective_id=0, has_side_effects=True, vmem_limit_bytes=VMEM
        ),
        name="forward",
    )(*weights, vec, tokens, cotangent, q_doc, cosine, sine)


RING = 8
EARLY = 9


class Scatter:
    stages = (0, 2, 4, 6, 8)

    def __init__(self, hi_count, depth, grads, from_core, bufs, sems):
        self.hi_count, self.depth = hi_count, depth
        self.grads, self.from_core = grads, from_core
        (self.held, self.staged, self.from_x, self.from_y, self.from_z, self.late_y, self.late_z,
         self.own, self.other) = bufs
        (self.load_sem, self.c_send, self.c_recv, self.x_send, self.x_recv, self.y_send, self.y_recv,
         self.z_send, self.z_recv, self.f_send, self.f_recv) = sems
        self.hi, self.mid, self.core, self.rep = place(hi_count)
        self.parts = Gather.parts_of(depth, SWAP)
        self.rows = depth // self.parts
        self.count = SLABS * self.parts
        self.lag = self.stages[-1]
        self.early = EARLY * self.parts

    @staticmethod
    def scratch(hi_count, depth):
        parts = Gather.parts_of(depth, SWAP)
        count, early, rows = SLABS * parts, EARLY * parts, depth // parts
        dma = pltpu.SemaphoreType.DMA
        bufs = [
            pltpu.VMEM((RING, hi_count, 2, rows, D), BF),
            pltpu.VMEM((hi_count, 2, rows, D), BF),
            pltpu.VMEM((early, hi_count, 2, rows, SWAP), BF),
            pltpu.VMEM((early, hi_count, rows, D - SWAP), BF),
            pltpu.VMEM((early, hi_count - 1, rows, D - SWAP), BF),
            pltpu.VMEM((count - early, hi_count, rows, D), BF),
            pltpu.VMEM((count - early, hi_count - 1, rows, D), BF),
            pltpu.VMEM((count, rows, D), BF),
            pltpu.VMEM((count, rows, D), BF),
        ]
        sems = [dma((2,))] + [dma((count,))] * 6 + [dma((count, hi_count - 1))] * 2 + [dma((count,))] * 2
        return bufs, sems

    def late(self, chunk):
        return isinstance(chunk, int) and chunk >= self.early

    def columns(self, chunk, which):
        if self.late(chunk):
            return slice(None)
        return pl.ds(pl.multiple_of(which * SWAP, LANES), D - SWAP)

    def only(self, which):
        return pl.ds(pl.multiple_of(which * (D - SWAP), LANES), SWAP)

    def y_land(self, chunk):
        return self.late_y.at[chunk - self.early] if self.late(chunk) else self.from_y.at[chunk]

    def z_land(self, chunk, m):
        if self.late(chunk):
            return self.late_z.at[chunk - self.early, m - 1]
        return self.from_z.at[chunk, m - 1]

    def block(self, chunk, which):
        start = (chunk % self.parts) * self.rows
        if not isinstance(start, int):
            start = pl.multiple_of(start, self.rows)
        return self.grads.at[chunk // self.parts, :, :, which, pl.ds(start, self.rows)]

    def c_copy(self, chunk):
        return remote(
            self.block(chunk, 1 - self.core),
            self.from_core.at[chunk],
            self.c_send.at[chunk],
            self.c_recv.at[chunk],
            shard_of(self.hi, self.mid, 1 - self.core),
        )

    def loads(self, chunk):
        return [
            pltpu.make_async_copy(
                self.block(chunk, self.core), self.held.at[chunk % RING], self.load_sem.at[0]
            ),
            pltpu.make_async_copy(self.from_core.at[chunk], self.staged, self.load_sem.at[1]),
        ]

    def x_copy(self, chunk):
        return remote(
            self.held.at[chunk % RING, :, :, :, self.only(1 - self.rep)],
            self.from_x.at[chunk],
            self.x_send.at[chunk],
            self.x_recv.at[chunk],
            {"rep": 1 - self.rep},
        )

    def y_copy(self, chunk):
        return remote(
            self.held.at[chunk % RING, :, 1 - self.mid, :, self.columns(chunk, self.rep)],
            self.y_land(chunk),
            self.y_send.at[chunk],
            self.y_recv.at[chunk],
            shard_of(self.hi, 1 - self.mid, self.core),
        )

    def z_copy(self, chunk, m):
        there = (self.hi + m) % self.hi_count
        return remote(
            self.held.at[chunk % RING, there, self.mid, :, self.columns(chunk, self.rep)],
            self.z_land(chunk, m),
            self.z_send.at[chunk, m - 1],
            self.z_recv.at[chunk, m - 1],
            shard_of(there, self.mid, self.core),
        )

    def f_copy(self, chunk, landed):
        columns = self.columns(chunk, 1 - self.rep if landed else self.rep)
        source = self.other if landed else self.own
        return remote(
            source.at[chunk, :, columns],
            self.other.at[chunk, :, columns],
            self.f_send.at[chunk],
            self.f_recv.at[chunk],
            {"rep": 1 - self.rep},
        )

    def hand_over(self, slab):
        for part in range(self.parts):
            self.c_copy(slab * self.parts + part).start()

    def free(self, chunk):
        if not self.late(chunk):
            self.x_copy(chunk).wait_send()
        self.y_copy(chunk).wait_send()
        for m in range(1, self.hi_count):
            self.z_copy(chunk, m).wait_send()

    def tick(self, t):
        def stage(number, act):
            chunk = t - self.stages[number]
            if isinstance(chunk, int):
                if 0 <= chunk < self.early:
                    act(chunk)
                chunk = t - self.stages[max(number - 1, 0)]
                if self.early <= chunk < self.count:
                    act(chunk)
            else:
                pl.when(chunk >= 0)(lambda: act(chunk))

        def begin(chunk):
            self.c_copy(chunk).wait_recv()
            if isinstance(chunk, int):
                if chunk >= RING:
                    self.free(chunk - RING)
            else:
                pl.when(chunk >= RING)(lambda: self.free(chunk - RING))
            for copy in self.loads(chunk):
                copy.start()

        def add_core(chunk):
            for copy in self.loads(chunk):
                copy.wait()
            slot = chunk % RING

            @pl.loop(0, self.hi_count)
            def _(h):
                for m in range(2):
                    self.held[slot, h, m] = self.held[slot, h, m] + self.staged[h, m]

            if self.late(chunk):
                self.y_copy(chunk).start()
            else:
                self.x_copy(chunk).start()

        def add_x(chunk):
            if self.late(chunk):
                return
            self.x_copy(chunk).wait_recv()
            slot, columns = chunk % RING, self.only(self.rep)

            @pl.loop(0, self.hi_count)
            def _(h):
                for m in range(2):
                    self.held[slot, h, m, :, columns] = (
                        self.held[slot, h, m, :, columns] + self.from_x[chunk, h, m]
                    )

            self.y_copy(chunk).start()

        def add_y(chunk):
            self.y_copy(chunk).wait_recv()
            slot, columns = chunk % RING, self.columns(chunk, self.rep)

            @pl.loop(0, self.hi_count)
            def _(h):
                self.held[slot, h, self.mid, :, columns] = (
                    self.held[slot, h, self.mid, :, columns] + self.y_land(chunk)[h]
                )

            for m in range(1, self.hi_count):
                self.z_copy(chunk, m).start()

        def add_z(chunk):
            columns = self.columns(chunk, self.rep)
            value = self.held[chunk % RING, self.hi, self.mid, :, columns].astype(F32)
            for m in range(1, self.hi_count):
                self.z_copy(chunk, m).wait_recv()
                value += self.z_land(chunk, m)[...].astype(F32)
            self.own[chunk, :, columns] = value.astype(BF)
            self.f_copy(chunk, False).start()

        stage(0, begin)
        stage(1, add_x)
        stage(2, add_y)
        stage(3, add_z)
        stage(4, lambda chunk: self.f_copy(chunk, True).wait_recv())
        stage(0, add_core)

    def drain(self):
        def finish(chunk):
            self.c_copy(chunk).wait_send()
            self.f_copy(chunk, False).wait_send()

        pl.loop(0, self.early)(finish)
        for chunk in range(self.early, self.count):
            finish(chunk)
        for chunk in range(self.count - RING, self.count):
            self.free(chunk)

    def whole(self, slab, columns):
        at = [slab * self.parts + part for part in range(self.parts)]
        parts = [self.own[c, :, columns].astype(F32) + self.other[c, :, columns].astype(F32) for c in at]
        return parts[0] if self.parts == 1 else jnp.concatenate(parts, axis=0)


class VectorScatter:
    def __init__(self, hi_count, bufs, sems):
        self.hi_count = hi_count
        self.mine, self.from_core, self.from_y, self.from_z, self.own, self.other = bufs
        (self.c_send, self.c_recv, self.y_send, self.y_recv, self.z_send, self.z_recv, self.f_send,
         self.f_recv) = sems
        self.hi, self.mid, self.core, self.rep = place(hi_count)

    @staticmethod
    def scratch(hi_count):
        tile = (VEC_ROWS, LANES)
        dma = pltpu.SemaphoreType.DMA
        bufs = [
            pltpu.VMEM((hi_count, 2, 2) + tile, F32),
            pltpu.VMEM((hi_count, 2) + tile, F32),
            pltpu.VMEM((hi_count,) + tile, F32),
            pltpu.VMEM((hi_count - 1,) + tile, F32),
            pltpu.VMEM(tile, F32),
            pltpu.VMEM(tile, F32),
        ]
        return bufs, [dma((1,))] * 4 + [dma((hi_count - 1,))] * 2 + [dma((1,))] * 2

    def c_copy(self):
        device = shard_of(self.hi, self.mid, 1 - self.core)
        source = self.mine.at[:, :, 1 - self.core]
        return remote(source, self.from_core, self.c_send.at[0], self.c_recv.at[0], device)

    def y_copy(self):
        device = shard_of(self.hi, 1 - self.mid, self.core)
        source = self.mine.at[:, 1 - self.mid, self.core]
        return remote(source, self.from_y, self.y_send.at[0], self.y_recv.at[0], device)

    def z_copy(self, m):
        there = (self.hi + m) % self.hi_count
        source = self.mine.at[there, self.mid, self.core]
        sems = (self.z_send.at[m - 1], self.z_recv.at[m - 1])
        return remote(source, self.from_z.at[m - 1], *sems, shard_of(there, self.mid, self.core))

    def f_copy(self):
        return remote(self.own, self.other, self.f_send.at[0], self.f_recv.at[0], {"rep": 1 - self.rep})

    def step(self, number):
        if number == 0:
            self.c_copy().start()
        elif number == 1:
            self.c_copy().wait_recv()
            self.mine[:, :, self.core] = self.mine[:, :, self.core] + self.from_core[...]
            self.y_copy().start()
        elif number == 2:
            self.y_copy().wait_recv()
            self.mine[:, self.mid, self.core] = self.mine[:, self.mid, self.core] + self.from_y[...]
            for m in range(1, self.hi_count):
                self.z_copy(m).start()
        elif number == 3:
            total = self.mine[self.hi, self.mid, self.core]
            for m in range(1, self.hi_count):
                self.z_copy(m).wait_recv()
                total += self.from_z[m - 1]
            self.own[...] = total
            self.f_copy().start()
        else:
            self.f_copy().wait()
            self.c_copy().wait_send()
            self.y_copy().wait_send()
            for m in range(1, self.hi_count):
                self.z_copy(m).wait_send()


def spread_vectors(mine, rows, bias, depth):
    hi_count = mine.shape[0]
    for shard in range(4 * hi_count):
        at = shard // 4, shard // 2 % 2, shard % 2

        def piece(ref, some, start):
            tile = ref[some, tile_of(start)]
            shift = -start % LANES
            return pltpu.roll(tile, shift, 1) if shift else tile

        mine[at] = piece(rows, slice(None), shard * depth)
        for t in range(3):
            start = (3 * shard + t) * depth
            slab = start // D
            mine[at + (slice(t, t + 1),)] = piece(bias, slice(slab, slab + 1), start % D)


def backward_kernel(
    hi_count,
    full,
    d_ffn_in,
    d_second,
    first_in,
    normed_in,
    q_all,
    k_all,
    v_all,
    q_ext_all,
    active_all,
    slope_all,
    x_all,
    inv_std,
    context,
    k_doc,
    vectors,
    sums_two,
    cosine,
    sine,
    grads,
    from_core,
    input_grad,
    g_qkv,
    g_out,
    g_up,
    g_down,
    g_vec,
    down_buf,
    up_buf,
    d_context,
    peer_part,
    peer_sum,
    rows_grad,
    bias_grad,
    load_sem,
    flush_sem,
    w_sem,
    p_sem,
    *rest,
):
    rows = context.shape[0]
    depth = g_qkv.shape[0]
    scatter = Scatter(hi_count, depth, grads, from_core, rest[:9], rest[9:20])
    small = VectorScatter(hi_count, rest[20:26], rest[26:])
    hi, mid, core, rep = place(hi_count)
    scatter.own[...] = jnp.zeros_like(scatter.own)
    scatter.other[...] = jnp.zeros_like(scatter.other)
    rows_grad[...] = jnp.zeros_like(rows_grad)
    rows_grad[B_DOWN : B_DOWN + 3] = sums_two[...]
    entry_barrier(hi_count, hi, mid, core, rep)
    upper = hi_count // 2
    own_rows = pl.ds(pl.multiple_of(rep * rows, rows), rows)
    peer_rows = pl.ds(pl.multiple_of((1 - rep) * rows, rows), rows)

    def flush_rows(slab, half):
        return pltpu.make_async_copy(
            down_buf.at[half], grads.at[slab, pl.ds(half * upper, upper)], flush_sem.at[half]
        )

    def flush_columns(slab, half):
        columns = pl.ds(half * HALF, HALF)
        return pltpu.make_async_copy(
            up_buf.at[half], grads.at[slab, :, :, :, :, columns], flush_sem.at[2 + half]
        )

    early = 4 * scatter.parts + (scatter.parts == 1)

    def ffn_phase(slots, act, slope, d_ffn, first, normed):
        def weights(j, base):
            return [
                pltpu.make_async_copy(full.at[slab + j], slots.at[base + s], w_sem.at[base + s])
                for s, slab in enumerate((UP, DOWN))
            ]

        def kept(j, half):
            return [
                pltpu.make_async_copy(active_all.at[2 * j + half], act.at[half], load_sem.at[2 * half]),
                pltpu.make_async_copy(slope_all.at[2 * j + half], slope.at[half], load_sem.at[2 * half + 1]),
            ]

        others = [
            pltpu.make_async_copy(d_ffn_in, d_ffn, p_sem.at[0]),
            pltpu.make_async_copy(first_in, first, p_sem.at[1]),
            pltpu.make_async_copy(d_second, input_grad, p_sem.at[2]),
            pltpu.make_async_copy(normed_in, normed, p_sem.at[3]),
        ]
        for copy in others[:1] + weights(0, 0) + kept(0, 0) + kept(0, 1) + others[1:]:
            copy.start()
        for copy in others:
            copy.wait()

        @pl.loop(0, 4)
        def _(j):
            base = lax.rem(j, 2) * 2
            for copy in weights(j, base):
                copy.wait()

            @pl.when(j < 3)
            def _():
                for copy in weights(j + 1, 2 - base):
                    copy.start()

            for half in range(2):
                for copy in kept(j, half):
                    copy.wait()
                low = d_ffn[...]
                down = slots[base + 1, half * upper : (half + 1) * upper].reshape(HALF, D)
                d_hidden = (dot_nt(low, down) * slope[half].astype(F32)).astype(BF)
                columns = slice(half * HALF, (half + 1) * HALF)
                rows_grad[pl.ds(B_UP + j, 1), columns] = column_sum(d_hidden.astype(F32))
                g_rows = dot(act[half], low)
                g_columns = dot(first[...], d_hidden)

                @pl.when(j < 3)
                def _():
                    for copy in kept(j + 1, half):
                        copy.start()

                down_buf[half] = g_rows.astype(BF).reshape(down_buf.shape[1:])
                up_buf[half] = g_columns.astype(BF).reshape(up_buf.shape[1:])
                flush_rows(2 * j, half).start()
                flush_columns(2 * j + 1, half).start()
                up = slots[base, :, :, :, :, columns].reshape(D, HALF)
                input_grad[...] += dot_nt(d_hidden, up)
                if half:
                    for h in range(2):
                        flush_rows(2 * j, h).wait()
                        flush_columns(2 * j + 1, h).wait()
                    scatter.hand_over(2 * j)
                    scatter.hand_over(2 * j + 1)
                t = scatter.parts * j + half - scatter.parts + 1
                if half or scatter.parts == 2:
                    pl.when(t >= 0)(lambda: scatter.tick(t))

        w_out = pltpu.make_async_copy(full.at[3], slots.at[0], w_sem.at[0])
        w_out.start()
        up = input_grad[...]
        normed_rows_ = normed[...]
        rows_grad[GAIN_ONE : GAIN_ONE + 1] = column_sum(up * normed_rows_)
        rows_grad[SHIFT_ONE : SHIFT_ONE + 1] = column_sum(up)
        grad = norm_back(up, normed_rows_, inv_std[:, 0:1], vectors[GAIN_ONE : GAIN_ONE + 1])
        input_grad[...] = grad
        d_attn = d_ffn
        d_attn[...] = grad.astype(BF)
        rows_grad[B_OUT : B_OUT + 1] = column_sum(d_attn[...].astype(F32))
        scatter.tick(early - 1)
        w_out.wait()
        for half in range(2):
            columns = slice(half * HALF, (half + 1) * HALF)
            g_rows = dot_tn(context[:, columns], d_attn[...])
            down_buf[half] = g_rows.astype(BF).reshape(down_buf.shape[1:])
            flush_rows(8, half).start()
        d_context[...] = dot_nt(d_attn[...], slots[0].reshape(D, D)).astype(BF)
        for half in range(2):
            flush_rows(8, half).wait()
        scatter.hand_over(8)

    blocks = (hi_count, 2, 2, depth, D)
    pl.run_scoped(
        ffn_phase,
        pltpu.VMEM((4,) + blocks, BF),
        pltpu.VMEM((2, HALF, rows), BF),
        pltpu.VMEM((2, rows, HALF), BF),
        pltpu.VMEM((rows, D), BF),
        pltpu.VMEM((D, rows), BF),
        pltpu.VMEM((rows, D), F32),
    )

    at = [min(early + HEADS // 2, 9 * scatter.parts)]

    def advance(handed):
        if at[0] < (9 + handed) * scatter.parts:
            scatter.tick(at[0])
            at[0] += 1

    def attention_phase(slots, q_in, k_in, v_in, ext_in, d_q, d_k, d_v, x):
        def quad(i, slot):
            return [
                pltpu.make_async_copy(q_all.at[i], q_in.at[slot], load_sem.at[slot]),
                pltpu.make_async_copy(k_all.at[i], k_in.at[slot], load_sem.at[2 + slot]),
                pltpu.make_async_copy(v_all.at[i], v_in.at[slot], load_sem.at[4 + slot]),
                pltpu.make_async_copy(q_ext_all.at[pl.ds(4 * i, 4)], ext_in.at[slot], load_sem.at[6 + slot]),
            ]

        weights = [pltpu.make_async_copy(full.at[s], slots.at[s], w_sem.at[s]) for s in range(3)]
        x_copy = pltpu.make_async_copy(x_all, x, w_sem.at[3])
        for copy in quad(0, 0) + weights + [x_copy]:
            copy.start()
        doc_k = k_doc[...]
        piece = 256

        def rope_back(a, table_rows):
            return a * cosine[table_rows, :] + swap_halves(a * sine[table_rows, :])

        @pl.loop(0, HEADS // 4)
        def _(i):
            slot = lax.rem(i, 2)
            for copy in quad(i, slot):
                copy.wait()

            @pl.when(i < HEADS // 4 - 1)
            def _():
                for copy in quad(i + 1, 1 - slot):
                    copy.start()

            for pair in range(2):
                lanes = slice(pair * LANES, (pair + 1) * LANES)
                wide = pl.ds(pl.multiple_of(i * QUAD + pair * LANES, LANES), LANES)
                k_pair, v_pair = k_in[slot, :, lanes], v_in[slot, :, lanes]
                k_lane = lax.broadcasted_iota(jnp.int32, k_pair.shape, 1)
                keys = jnp.concatenate([k_pair, doc_k], axis=1)
                minus = jnp.where(k_lane < 3, -1.0, 0.0).astype(BF)
                values = jnp.concatenate([v_pair, minus], axis=1)
                dk = dv = None
                for start in range(0, rows, piece):
                    part = slice(start, start + piece)
                    q_pair, g_pair = q_in[slot, part, lanes], d_context[part, wide]
                    lane = lax.broadcasted_iota(jnp.int32, q_pair.shape, 1)
                    product = g_pair.astype(F32) * context[part, wide].astype(F32)
                    dq = None
                    for head in range(2):
                        in_head = (lane // HEAD_DIM) == head
                        q_head = jnp.where(in_head, q_pair, 0)
                        g_head = jnp.where(in_head, g_pair, 0)
                        inner = jnp.sum(jnp.where(in_head, product, 0.0), axis=1, keepdims=True)
                        top, middle, low = split3(jnp.broadcast_to(inner, q_pair.shape))
                        g_ext = jnp.where(lane == 0, top, jnp.where(lane == 1, middle, low))
                        g_ext = jnp.where(lane < 3, g_ext, 0)
                        q_wide = jnp.concatenate([q_head, ext_in[slot, pair * 2 + head, part, :]], axis=1)
                        prob = jnp.exp(dot_nt(keys, q_wide))
                        d_prob = dot_nt(values, jnp.concatenate([g_head, g_ext], axis=1))
                        d_score = (prob * d_prob).astype(BF)
                        dv_part = dot(prob.astype(BF), g_head)
                        dk_part = dot(d_score, q_head)
                        k_head = jnp.where((k_lane // HEAD_DIM) == head, k_pair, 0)
                        dq_part = dot_tn(d_score, k_head)
                        dv = dv_part if dv is None else dv + dv_part
                        dk = dk_part if dk is None else dk + dk_part
                        dq = dq_part if dq is None else dq + dq_part
                    table_rows = pl.ds(pl.multiple_of(rep * rows + start, piece), piece)
                    d_q[part, wide] = rope_back(dq * HEAD_DIM**-0.5, table_rows).astype(BF)
                d_k[:rows, wide] = rope_back(dk[:rows], own_rows).astype(BF)
                d_k[rows:, wide] = rope_back(dk[rows:], peer_rows).astype(BF)
                d_v[:, wide] = dv.astype(BF)
                t = early + 2 * i + pair
                pl.when(t < 9 * scatter.parts)(lambda: scatter.tick(t))

        for copy in weights + [x_copy]:
            copy.wait()
        def slab_grad(s, count, d_rows):
            for half in range(2):
                columns = slice(half * HALF, (half + 1) * HALF)
                if s > 0:
                    flush_columns(8 + s, half).wait()
                g_columns = dot(x[:, :count], d_rows[:, columns])
                up_buf[half] = g_columns.astype(BF).reshape(up_buf.shape[1:])
                flush_columns(9 + s, half).start()
            if s > 0:
                scatter.hand_over(8 + s)
            bias_grad[s : s + 1] = column_sum(d_rows[...].astype(F32))

        slab_grad(0, rows, d_q)
        advance(0)
        slab_grad(1, 2 * rows, d_k)
        advance(1)
        slab_grad(2, 2 * rows, d_v)
        advance(2)
        for half in range(2):
            flush_columns(11, half).wait()
        scatter.hand_over(11)
        w_k, w_v = slots[1].reshape(D, D), slots[2].reshape(D, D)
        peer_part[...] = (dot_nt(d_k[rows:], w_k) + dot_nt(d_v[rows:], w_v)).astype(BF)
        peer_copy = remote(peer_part, peer_sum, p_sem.at[4], p_sem.at[5], {"rep": 1 - rep})
        peer_copy.start()
        advance(3)
        spread_vectors(small.mine, rows_grad, bias_grad, depth)
        small.step(0)
        advance(3)
        small.step(1)
        input_grad[...] += dot_nt(d_q[...], slots[0].reshape(D, D))
        advance(3)
        input_grad[...] += dot_nt(d_k[:rows], w_k)
        advance(3)
        small.step(2)
        input_grad[...] += dot_nt(d_v[:rows], w_v)
        peer_copy.wait()
        input_grad[...] += peer_sum[...].astype(F32)

    pl.run_scoped(
        attention_phase,
        pltpu.VMEM((3,) + blocks, BF),
        pltpu.VMEM((2, rows, QUAD), BF),
        pltpu.VMEM((2, 2 * rows, QUAD), BF),
        pltpu.VMEM((2, 2 * rows, QUAD), BF),
        pltpu.VMEM((2, 4, rows, LANES), BF),
        pltpu.VMEM((rows, D), BF),
        pltpu.VMEM((2 * rows, D), BF),
        pltpu.VMEM((2 * rows, D), BF),
        pltpu.VMEM((D, 2 * rows), BF),
    )

    end = scatter.count + scatter.stages[-2]
    settled = EARLY * scatter.parts + scatter.lag
    for t in range(at[0], settled):
        scatter.tick(t)
    g_out[...] = scatter.whole(8, slice(None))
    for j in range(4):
        g_down[j * depth : (j + 1) * depth] = scatter.whole(2 * j, slice(None))
    for t in range(settled, end - 1):
        scatter.tick(t)
    small.step(3)
    each = LANES // depth
    for t in range(FF // LANES):
        pieces = []
        for u in range(each):
            shard, j = divmod(t * each + u, 4)
            pieces.append((scatter.whole(2 * j + 1, tile_of(shard * depth)), shard * depth % LANES))
        g_up[:, t * LANES : (t + 1) * LANES] = regroup(pieces, depth)
    scatter.tick(end - 1)
    for s in range(3):
        g_qkv[:, s * D : (s + 1) * D] = scatter.whole(9 + s, slice(None))
    small.step(4)
    g_vec[...] = small.own[...] + small.other[...]
    scatter.drain()


def backward(hi_count, full, arrays, kept):
    context, depth = kept[1], full.shape[4]
    rows = context.shape[0]
    anywhere = pl.BlockSpec(memory_space=pl.ANY)
    vmem = pl.BlockSpec(memory_space=pltpu.VMEM)
    dma = pltpu.SemaphoreType.DMA
    shape = jax.ShapeDtypeStruct
    blocks = (hi_count, 2, 2, depth)
    parts = Gather.parts_of(depth, SWAP)
    bufs, sems = Scatter.scratch(hi_count, depth)
    small_bufs, small_sems = VectorScatter.scratch(hi_count)
    return pl.pallas_call(
        functools.partial(backward_kernel, hi_count),
        out_shape=(
            shape((SLABS,) + blocks + (D,), BF),
            shape((SLABS * parts, hi_count, 2, depth // parts, D), BF),
            shape((rows, D), F32),
            shape((depth, 3 * D), F32),
            shape((depth, D), F32),
            shape((depth, FF), F32),
            shape((4 * depth, D), F32),
            shape((VEC_ROWS, LANES), F32),
        ),
        in_specs=[anywhere] * (1 + len(arrays)) + [vmem] * len(kept),
        out_specs=(anywhere,) * 2 + (vmem,) * 6,
        scratch_shapes=[
            pltpu.VMEM((2, hi_count // 2, 2, 2, depth, D), BF),
            pltpu.VMEM((2,) + blocks + (HALF,), BF),
            pltpu.VMEM((rows, D), BF),
            pltpu.VMEM((rows, D), BF),
            pltpu.VMEM((rows, D), BF),
            pltpu.VMEM((VEC_ROWS, D), F32),
            pltpu.VMEM((3, D), F32),
            dma((8,)),
            dma((4,)),
            dma((4,)),
            dma((6,)),
        ]
        + bufs
        + sems
        + small_bufs
        + small_sems,
        compiler_params=pltpu.CompilerParams(
            collective_id=1, has_side_effects=True, vmem_limit_bytes=VMEM
        ),
        name="backward",
    )(full, *arrays, *kept)


def rope_tables(count):
    position = np.arange(count, dtype=np.float32)
    frequency = np.exp(np.arange(HEAD_DIM // 2, dtype=np.float32) * np.float32(-2.0 * math.log(10000.0) / HEAD_DIM))
    angles = position[:, None] * frequency[None, :].astype(np.float32)
    cosine, sine = np.cos(angles).astype(np.float32), np.sin(angles).astype(np.float32)
    return (
        jnp.asarray(np.concatenate([cosine] * 4, axis=1)),
        jnp.asarray(np.concatenate([-sine, sine, -sine, sine], axis=1)),
    )


def local(
    tokens,
    segments,
    cotangent,
    w_qkv,
    b_qkv,
    w_out,
    b_out,
    gain_one,
    shift_one,
    w_up,
    b_up,
    w_down,
    b_down,
    gain_two,
    shift_two,
):
    rows = tokens.shape[0]
    shards = lax.axis_size("shard")
    hi_count = shards // 4
    depth = D // shards
    small = (b_qkv, b_out, gain_one, shift_one, b_up, b_down, gain_two, shift_two)
    widths = [a.shape[0] for a in small]
    vec = jnp.concatenate(small + (jnp.zeros((VEC_ROWS * depth - sum(widths),), F32),))
    vec = jnp.tile(vec.reshape(VEC_ROWS, depth), (1, LANES // depth))
    lane = jnp.arange(LANES, dtype=jnp.int32)[None, :]
    q_doc = (segments[:, None] == lane).astype(BF)
    cosine, sine = rope_tables(2 * rows)
    (
        full, q, k, v, q_ext, active, slope, x_all, k_doc, context, first, normed, inv_std, result,
        d_second, d_ffn, sums_two, vectors,
    ) = forward(hi_count, (w_qkv, w_out, w_up, w_down), vec[None], tokens, cotangent, q_doc, cosine, sine)
    _, _, input_grad, g_qkv, g_out, g_up, g_down, g_vec = backward(
        hi_count,
        full,
        (d_ffn, d_second, first, normed, q, k, v, q_ext, active, slope, x_all),
        (inv_std, context, k_doc, vectors, sums_two, cosine, sine),
    )
    outs = []
    at = 0
    for width in widths:
        count = width // depth
        outs.append(g_vec[at : at + count, :depth].reshape(width))
        at += count
    return (
        result,
        input_grad,
        g_qkv,
        outs[0],
        g_out,
        outs[1],
        outs[2],
        outs[3],
        g_up,
        outs[4],
        g_down,
        outs[5],
        outs[6],
        outs[7],
    )


def solution(mesh):
    act = P(("shard", "rep"), None)
    matrix = P("shard", None)
    vector = P("shard")
    params = (matrix, vector, matrix, vector, vector, vector, matrix, vector, matrix, vector, vector, vector)
    return jax.shard_map(
        local,
        mesh=mesh,
        in_specs=(act, P(("shard", "rep")), act) + params,
        out_specs=(act, act) + params,
        check_vma=False,
    )
```

```python
import functools
import math

import jax
import jax.numpy as jnp
import numpy as np
from jax import lax
from jax.experimental import pallas as pl
from jax.experimental.pallas import tpu as pltpu
from jax.sharding import PartitionSpec as P

D = 1024
HEADS = 16
HEAD_DIM = 64
FF = 4096
SLABS = 12
LANES = 128
MASKED = -1e30
MESH = pl.DeviceIdType.MESH
VMEM = 60 * 1024 * 1024
BF = jnp.bfloat16
F32 = jnp.float32

ERFC_P = 0.33
ERFC_Q = (
    0.1863661,
    0.182837329,
    0.20192357,
    0.0450108379,
    0.412542064,
    -0.355440048,
    0.462689118,
    -0.135929052,
)


def dot(a, b):
    return lax.dot_general(a, b, (((1,), (0,)), ((), ())), preferred_element_type=F32)


def dot_nt(a, b):
    return lax.dot_general(a, b, (((1,), (1,)), ((), ())), preferred_element_type=F32)


def dot_tn(a, b):
    return lax.dot_general(a, b, (((0,), (0,)), ((), ())), preferred_element_type=F32)


def swap_halves(a):
    width = a.shape[1]
    lane = lax.broadcasted_iota(jnp.int32, a.shape, 1) % HEAD_DIM
    return jnp.where(
        lane < HEAD_DIM // 2,
        pltpu.roll(a, width - HEAD_DIM // 2, 1),
        pltpu.roll(a, HEAD_DIM // 2, 1),
    )


def split3(a):
    hi = a.astype(BF)
    rest = a - hi.astype(F32)
    mid = rest.astype(BF)
    low = (rest - mid.astype(F32)).astype(BF)
    return hi, mid, low


def remote(src, dst, send, recv, device):
    return pltpu.make_async_remote_copy(
        src_ref=src, dst_ref=dst, send_sem=send, recv_sem=recv, device_id=device, device_id_type=MESH
    )


def place(hi_count):
    index = lax.axis_index("shard")
    return index // 4, (index // 2) % 2, index % 2, lax.axis_index("rep")


def shard_of(hi, mid, core):
    return {"shard": hi * 4 + mid * 2 + core}


def entry_barrier(hi_count, hi, mid, core, rep):
    barrier = pltpu.get_barrier_semaphore()
    for m in range(1, hi_count):
        pl.semaphore_signal(
            barrier, inc=1, device_id=shard_of((hi + m) % hi_count, mid, core), device_id_type=MESH
        )
    pl.semaphore_signal(barrier, inc=1, device_id=shard_of(hi, 1 - mid, core), device_id_type=MESH)
    pl.semaphore_signal(barrier, inc=1, device_id=shard_of(hi, mid, 1 - core), device_id_type=MESH)
    pl.semaphore_signal(barrier, inc=1, device_id={"rep": 1 - rep}, device_id_type=MESH)
    pl.semaphore_wait(barrier, hi_count + 2)


SWAP = 256
PARTS = 2


def normed_rows(residual):
    mean_val = jnp.mean(residual, axis=-1, keepdims=True)
    centred = residual - mean_val
    variance = jnp.mean(centred * centred, axis=-1, keepdims=True)
    inv_std = lax.rsqrt(variance + 1e-05)
    return centred * inv_std, inv_std


def norm_back(upstream, normed, inv_std, gain_vec):
    scaled = upstream * gain_vec
    return inv_std * (
        scaled
        - jnp.mean(scaled, axis=-1, keepdims=True)
        - normed * jnp.mean(scaled * normed, axis=-1, keepdims=True)
    )


def column_sum(a):
    return jnp.sum(a, axis=0, keepdims=True)


class Gather:
    def __init__(self, hi_count, packed, full, sems, swap=SWAP):
        self.hi_count = hi_count
        self.packed, self.full = packed, full
        (self.up_send, self.up_recv, self.down_send, self.down_recv, self.y_send, self.y_recv,
         self.x_send, self.x_recv, self.c_send, self.c_recv) = sems
        self.hi, self.mid, self.core, self.rep = place(hi_count)
        slabs, self.depth, width = packed.shape
        self.parts = self.parts_of(self.depth, swap)
        self.rows = self.depth // self.parts
        self.count = slabs * self.parts
        self.swap = swap
        self.mine = slice(None)
        if swap:
            self.mine = pl.ds(pl.multiple_of(self.rep * swap, LANES), width - swap)

    @staticmethod
    def parts_of(depth, swap):
        return PARTS if swap and depth % (16 * PARTS) == 0 else 1

    @staticmethod
    def scratch(hi_count, slabs, depth, swap=SWAP):
        count = slabs * Gather.parts_of(depth, swap)
        dma = pltpu.SemaphoreType.DMA
        hops = dma((count, hi_count - 1))
        return [hops] * 4 + [dma((count, hi_count))] * 2 + [dma((count,))] * 2 + [dma((count, 2))] * 2

    def only(self, which):
        return pl.ds(pl.multiple_of(which * (D - self.swap), LANES), self.swap)

    def spot(self, chunk):
        start = (chunk % self.parts) * self.rows
        if not isinstance(start, int):
            start = pl.multiple_of(start, self.rows)
        return chunk // self.parts, pl.ds(start, self.rows)

    def hop(self, chunk, distance, up):
        slab, rows = self.spot(chunk)
        origin = self.hi - distance if up else self.hi + distance
        block = self.full.at[slab, origin, self.mid, self.core, rows, self.mine]
        source = self.packed.at[slab, rows, self.mine] if distance == 0 else block
        send, recv = (self.up_send, self.up_recv) if up else (self.down_send, self.down_recv)
        device = shard_of(self.hi + 1 if up else self.hi - 1, self.mid, self.core)
        return remote(source, block, send.at[chunk, distance], recv.at[chunk, distance], device)

    def landed_hop(self, chunk, distance, up):
        slab, rows = self.spot(chunk)
        origin = self.hi - distance - 1 if up else self.hi + distance + 1
        block = self.full.at[slab, origin, self.mid, self.core, rows, self.mine]
        send, recv = (self.up_send, self.up_recv) if up else (self.down_send, self.down_recv)
        device = shard_of(self.hi, self.mid, self.core)
        return remote(block, block, send.at[chunk, distance], recv.at[chunk, distance], device)

    def sends(self, distance, up):
        if up:
            return (self.hi - distance >= 0) & (self.hi + 1 < self.hi_count)
        return (self.hi + distance < self.hi_count) & (self.hi - 1 >= 0)

    def lands(self, distance, up):
        if up:
            return self.hi - distance - 1 >= 0
        return self.hi + distance + 1 < self.hi_count

    def y_copy(self, chunk, origin, landed):
        slab, rows = self.spot(chunk)
        which = 1 - self.mid if landed else self.mid
        block = self.full.at[slab, origin, which, self.core, rows, self.mine]
        device = shard_of(self.hi, 1 - self.mid, self.core)
        return remote(block, block, self.y_send.at[chunk, origin], self.y_recv.at[chunk, origin], device)

    def x_copy(self, chunk, landed):
        slab, rows = self.spot(chunk)
        columns = self.only(1 - self.rep if landed else self.rep)
        block = self.full.at[slab, :, :, self.core, rows, columns]
        return remote(block, block, self.x_send.at[chunk], self.x_recv.at[chunk], {"rep": 1 - self.rep})

    def c_copy(self, chunk, part, landed):
        slab, rows = self.spot(chunk)
        which = 1 - self.core if landed else self.core
        columns = self.mine if part == 0 else self.only(1 - self.rep)
        block = self.full.at[slab, :, :, which, rows, columns]
        device = shard_of(self.hi, self.mid, 1 - self.core)
        return remote(block, block, self.c_send.at[chunk, part], self.c_recv.at[chunk, part], device)

    @property
    def lag(self):
        return 2 * self.hi_count + 4

    def own_copy(self, sem):
        target = self.full.at[:, self.hi, self.mid, self.core, :, self.mine]
        return pltpu.make_async_copy(self.packed.at[:, :, self.mine], target, sem)

    def tick(self, t):
        def stage(offset, act):
            if not isinstance(t, int):
                chunk = t - offset
                pl.when((chunk >= 0) & (chunk < self.count))(lambda: act(chunk))
            elif 0 <= t - offset < self.count:
                act(t - offset)

        def own(chunk):
            for up in (True, False):
                pl.when(self.sends(0, up))(lambda: self.hop(chunk, 0, up).start())
            self.y_copy(chunk, self.hi, False).start()

        def forward(distance, chunk):
            for up in (True, False):
                @pl.when(self.lands(distance - 1, up))
                def _():
                    self.landed_hop(chunk, distance - 1, up).wait_recv()
                    origin = self.hi - distance if up else self.hi + distance
                    self.y_copy(chunk, origin, False).start()

                if distance < self.hi_count - 1:
                    pl.when(self.sends(distance, up))(lambda: self.hop(chunk, distance, up).start())

        def after_y(chunk):
            for origin in range(self.hi_count):
                self.y_copy(chunk, origin, True).wait_recv()
            if self.swap:
                self.x_copy(chunk, False).start()
            self.c_copy(chunk, 0, False).start()

        def after_x(chunk):
            if self.swap:
                self.x_copy(chunk, True).wait_recv()
                self.c_copy(chunk, 1, False).start()

        def after_c(chunk):
            for part in range(2 if self.swap else 1):
                self.c_copy(chunk, part, True).wait_recv()

        stage(0, own)
        for distance in range(1, self.hi_count):
            stage(2 * distance, functools.partial(forward, distance))
        stage(2 * self.hi_count, after_y)
        stage(2 * self.hi_count + 2, after_x)
        stage(2 * self.hi_count + 4, after_c)

    def drain(self):
        @pl.loop(0, self.count)
        def _(chunk):
            for distance in range(self.hi_count - 1):
                for up in (True, False):
                    pl.when(self.sends(distance, up))(
                        lambda: self.hop(chunk, distance, up).wait_send()
                    )
            for origin in range(self.hi_count):
                self.y_copy(chunk, origin, False).wait_send()
            if self.swap:
                self.x_copy(chunk, False).wait_send()
            for part in range(2 if self.swap else 1):
                self.c_copy(chunk, part, False).wait_send()


def near_barrier(hi_count):
    hi, mid, core, rep = place(hi_count)
    barrier = pltpu.get_barrier_semaphore()

    def greet(device):
        pl.semaphore_signal(barrier, inc=1, device_id=device, device_id_type=MESH)

    pl.when(hi + 1 < hi_count)(lambda: greet(shard_of(hi + 1, mid, core)))
    pl.when(hi - 1 >= 0)(lambda: greet(shard_of(hi - 1, mid, core)))
    greet(shard_of(hi, 1 - mid, core))
    greet(shard_of(hi, mid, 1 - core))
    greet({"rep": 1 - rep})
    first, last = hi == 0, hi == hi_count - 1
    pl.semaphore_wait(barrier, 5 - first.astype(jnp.int32) - last.astype(jnp.int32))


UP, DOWN = 4, 8
HALF = D // 2
QUAD = 4 * HEAD_DIM
B_OUT, GAIN_ONE, SHIFT_ONE, B_UP, B_DOWN, GAIN_TWO, SHIFT_TWO = 3, 4, 5, 6, 10, 11, 12
VEC_ROWS = 16


def regroup(pieces, depth):
    out = None
    for u, (tile, start) in enumerate(pieces):
        shift = (u * depth - start) % LANES
        moved = pltpu.roll(tile, shift, 1) if shift else tile
        lane = lax.broadcasted_iota(jnp.int32, moved.shape, 1)
        out = moved if out is None else jnp.where(lane // depth == u, moved, out)
    return out


def tile_of(at):
    return slice(at // LANES * LANES, at // LANES * LANES + LANES)


def pack(packed, w_qkv, w_out, w_up, w_down):
    depth = w_qkv.shape[0]
    for slab in range(3):
        packed[slab] = w_qkv[:, slab * D : (slab + 1) * D].astype(BF)
    packed[3] = w_out[...].astype(BF)
    each = LANES // depth
    for j in range(4):
        packed[DOWN + j] = w_down[j * depth : (j + 1) * depth].astype(BF)
        for t in range(D // LANES):
            starts = [4 * depth * (t * each + u) + depth * j for u in range(each)]
            pieces = [(w_up[:, tile_of(at)], at % LANES) for at in starts]
            packed[UP + j, :, t * LANES : (t + 1) * LANES] = regroup(pieces, depth).astype(BF)


def unpack_vectors(vec_full, rows_out, bias, depth):
    hi_count = vec_full.shape[1]
    each = LANES // depth

    def of_shard(shard):
        return vec_full[0, shard // 4, shard // 2 % 2, shard % 2].astype(BF).astype(F32)

    def join(pieces):
        lane = lax.broadcasted_iota(jnp.int32, pieces[0].shape, 1)
        out = pieces[0]
        for u in range(1, each):
            out = jnp.where(lane // depth == u, pieces[u], out)
        return out

    for t in range(D // LANES):
        tile = slice(t * LANES, (t + 1) * LANES)
        rows_out[:, tile] = join([of_shard(t * each + u) for u in range(each)])
        for j in range(3):
            chunks = [(j * D + t * LANES) // depth + u for u in range(each)]
            bias[j : j + 1, tile] = join([of_shard(m // 3)[m % 3 : m % 3 + 1] for m in chunks])


def gelu_parts(hidden):
    gauss = jnp.exp(hidden * hidden * -0.5)
    t = 1.0 / (1.0 + (ERFC_P * math.sqrt(0.5)) * jnp.abs(hidden))
    poly = jnp.full_like(t, ERFC_Q[-1])
    for coefficient in ERFC_Q[-2::-1]:
        poly = poly * t + coefficient
    tail = 0.5 * t * poly * gauss
    cdf = jnp.where(hidden >= 0, 1.0 - tail, tail)
    return hidden * cdf, cdf + hidden * gauss * (1.0 / math.sqrt(2.0 * math.pi))


def forward_kernel(
    hi_count,
    w_qkv,
    w_out,
    w_up,
    w_down,
    vec,
    tokens,
    cotangent,
    q_doc,
    cosine,
    sine,
    full,
    q_all,
    k_all,
    v_all,
    q_ext_all,
    active_all,
    slope_all,
    x_all,
    k_doc,
    context,
    first_turned,
    normed_out,
    inv_out,
    result,
    d_second,
    d_ffn,
    sums,
    vectors,
    packed,
    vec_full,
    x_peer,
    slots,
    q_buf,
    k_buf,
    v_buf,
    ext_buf,
    first,
    first_low,
    turned,
    total,
    act_buf,
    turned_act,
    slope_buf,
    bias,
    local_sem,
    load_sem,
    flush_sem,
    t_sem,
    *sems,
):
    rows = tokens.shape[0]
    depth = w_qkv.shape[0]
    rep = lax.axis_index("rep")
    gather = Gather(hi_count, packed, full, sems[:10])
    small = Gather(hi_count, vec, vec_full, sems[10:], swap=0)
    lane_doc = lax.broadcasted_iota(jnp.int32, (rows, LANES), 1)
    other = jnp.where(q_doc[...] > 0.5, 0.0, MASKED)
    other = jnp.where(lane_doc < 61, other, jnp.where(lane_doc < 64, 1.0, 0.0))
    k_doc[:rows] = other.astype(BF)
    pack(packed, w_qkv, w_out, w_up, w_down)
    near_barrier(hi_count)
    peer = {"rep": 1 - rep}
    token_copy = remote(tokens, x_peer, t_sem.at[0], t_sem.at[1], peer)
    doc_copy = remote(k_doc.at[:rows], k_doc.at[rows:], t_sem.at[2], t_sem.at[3], peer)
    copies = [small.own_copy(local_sem.at[0]), gather.own_copy(local_sem.at[1])]
    for copy in copies:
        copy.start()
    doc_copy.start()
    token_copy.start()
    for copy in copies:
        copy.wait()
    warm = gather.lag + 1
    for t in range(warm):
        small.tick(t)
        gather.tick(t)
    unpack_vectors(vec_full, vectors, bias, depth)
    doc_copy.wait()
    token_copy.wait()
    turned[:, :rows] = tokens[...].T
    turned[:, rows:] = x_peer[...].T
    x_copy = pltpu.make_async_copy(turned, x_all, local_sem.at[0])
    x_copy.start()
    ready = 3 * gather.parts + gather.lag

    @pl.loop(warm, ready)
    def _(t):
        gather.tick(t)

    def load_whole(slab, slot):
        return pltpu.make_async_copy(full.at[slab], slots.at[slot], load_sem.at[slot])

    for slab in range(3):
        load_whole(slab, slab).start()
    for slab in range(3):
        load_whole(slab, slab).wait()

    def weight(slot, columns):
        return slots[slot, :, :, :, :, columns].reshape(D, -1)

    own_rows = pl.ds(pl.multiple_of(rep * rows, rows), rows)
    peer_rows = pl.ds(pl.multiple_of((1 - rep) * rows, rows), rows)

    def rope(a, table_rows):
        cos_part, sin_part = cosine[table_rows, :], sine[table_rows, :]
        cos_part = jnp.concatenate([cos_part, cos_part], axis=1)
        sin_part = jnp.concatenate([sin_part, sin_part], axis=1)
        return a * cos_part + swap_halves(a) * sin_part

    def flushes(i):
        return [
            pltpu.make_async_copy(q_buf.at[i], q_all.at[i], flush_sem.at[0, i]),
            pltpu.make_async_copy(k_buf.at[i], k_all.at[i], flush_sem.at[1, i]),
            pltpu.make_async_copy(v_buf.at[i], v_all.at[i], flush_sem.at[2, i]),
            pltpu.make_async_copy(
                ext_buf.at[pl.ds(4 * i, 4)], q_ext_all.at[pl.ds(4 * i, 4)], flush_sem.at[3, i]
            ),
        ]

    ones = jnp.ones((2 * rows, LANES), BF)
    piece = 256

    @pl.loop(0, HEADS // 4)
    def _(i):
        columns = pl.ds(pl.multiple_of(i * QUAD, QUAD), QUAD)
        own_x, peer_x = tokens[...], x_peer[...]
        w = weight(0, columns)
        q_rows = rope(dot(own_x, w) + bias[0:1, columns], own_rows) * HEAD_DIM**-0.5
        q_buf[i] = q_rows.astype(BF)
        w = weight(1, columns)
        k_buf[i, :rows] = rope(dot(own_x, w) + bias[1:2, columns], own_rows).astype(BF)
        k_buf[i, rows:] = rope(dot(peer_x, w) + bias[1:2, columns], peer_rows).astype(BF)
        w = weight(2, columns)
        v_buf[i, :rows] = (dot(own_x, w) + bias[2:3, columns]).astype(BF)
        v_buf[i, rows:] = (dot(peer_x, w) + bias[2:3, columns]).astype(BF)
        for pair in range(2):
            gather.tick(ready + 2 * i + pair)
            lanes = slice(pair * LANES, (pair + 1) * LANES)
            keys = jnp.concatenate([k_buf[i, :, lanes], k_doc[...]], axis=1)
            values = jnp.concatenate([v_buf[i, :, lanes], ones], axis=1)
            for start in range(0, rows, piece):
                part = slice(start, start + piece)
                q_pair = q_buf[i, part, lanes]
                lane = lax.broadcasted_iota(jnp.int32, q_pair.shape, 1)
                doc_q = q_doc[part, :]
                mixed = []
                for head in range(2):
                    in_head = (lane // HEAD_DIM) == head
                    queries = jnp.concatenate([jnp.where(in_head, q_pair, 0), doc_q], axis=1)
                    scores = dot_nt(queries, keys)
                    row_max = jnp.max(scores, axis=1, keepdims=True)
                    prob = jnp.exp(scores - row_max).astype(BF)
                    both = dot(prob, values)
                    row_sum = both[:, LANES:]
                    mixed.append(both[:, :LANES] / row_sum)
                    hi, mid, low = split3(-(row_max + jnp.log(row_sum)))
                    ext = jnp.where(lane == 61, hi, doc_q)
                    ext = jnp.where(lane == 62, mid, ext)
                    ext = jnp.where(lane == 63, low, ext)
                    ext_buf[4 * i + pair * 2 + head, part, :] = ext
                pair_lanes = pl.ds(pl.multiple_of(i * QUAD + pair * LANES, LANES), LANES)
                context[part, pair_lanes] = jnp.where(lane < HEAD_DIM, mixed[0], mixed[1]).astype(BF)
        for copy in flushes(i):
            copy.start()

    done = ready + HEADS // 2

    def vector(row):
        return vectors[row : row + 1, :]

    load_whole(3, 3).start()
    load_whole(UP, 0).start()
    load_whole(3, 3).wait()
    attn = dot(context[...], weight(3, slice(None))) + vector(B_OUT)
    normed, inv_std = normed_rows(tokens[...].astype(F32) + attn)
    first[...] = normed * vector(GAIN_ONE) + vector(SHIFT_ONE)
    first_low[...] = first[...].astype(BF)
    first_turned[...] = first_low[...].T
    normed_out[...] = normed
    inv_out[...] = jnp.broadcast_to(inv_std, inv_out.shape)
    total[...] = first[...] + vector(B_DOWN)

    def keeps(j, half):
        return [
            pltpu.make_async_copy(
                turned_act.at[half], active_all.at[2 * j + half], flush_sem.at[4, 2 * half]
            ),
            pltpu.make_async_copy(
                slope_buf.at[half], slope_all.at[2 * j + half], flush_sem.at[4, 2 * half + 1]
            ),
        ]

    gather.tick(done)

    @pl.loop(0, 4)
    def _(j):
        slot = lax.rem(j, 2)
        load_whole(UP + j, slot).wait()
        for half in range(2):
            @pl.when(j > 0)
            def _():
                for copy in keeps(j - 1, half):
                    copy.wait()

            columns = slice(half * HALF, (half + 1) * HALF)
            hidden = dot(first_low[...], weight(slot, columns)) + vectors[pl.ds(B_UP + j, 1), columns]
            act, slope = gelu_parts(hidden)
            act = act.astype(BF)
            act_buf[2 * j + half] = act
            turned_act[half] = act.T
            slope_buf[half] = slope.astype(BF)
            for copy in keeps(j, half):
                copy.start()
            gather.tick(done + 1 + 2 * j + half)
        load_whole(UP + j + 1, 1 - slot).start()

    @pl.loop(0, 4)
    def _(j):
        slot = lax.rem(j, 2)
        load_whole(DOWN + j, slot).wait()

        @pl.when(j == 0)
        def _():
            for t in range(done + 9, gather.count + gather.lag):
                gather.tick(t)

        @pl.when(j < 3)
        def _():
            load_whole(DOWN + j + 1, 1 - slot).start()

        for half in range(2):
            down = slots[slot, half * (hi_count // 2) : (half + 1) * (hi_count // 2)].reshape(HALF, D)
            total[...] += dot(act_buf[2 * j + half], down)

    for half in range(2):
        for copy in keeps(3, half):
            copy.wait()
    gain = vector(GAIN_TWO)
    normed, inv_std = normed_rows(total[...])
    result[...] = (normed * gain + vector(SHIFT_TWO)).astype(BF)
    up = cotangent[...].astype(F32)
    sums[1:2] = column_sum(up * normed)
    sums[2:3] = column_sum(up)
    grad = norm_back(up, normed, inv_std, gain)
    d_second[...] = grad
    low = grad.astype(BF)
    d_ffn[...] = low
    sums[0:1] = column_sum(low.astype(F32))
    x_copy.wait()
    small.drain()
    gather.drain()

    @pl.loop(0, HEADS // 4)
    def _(i):
        for copy in flushes(i):
            copy.wait()


def forward(hi_count, weights, vec, tokens, cotangent, q_doc, cosine, sine):
    rows = tokens.shape[0]
    depth = weights[0].shape[0]
    anywhere = pl.BlockSpec(memory_space=pl.ANY)
    vmem = pl.BlockSpec(memory_space=pltpu.VMEM)
    dma = pltpu.SemaphoreType.DMA
    quads = HEADS // 4
    shape = jax.ShapeDtypeStruct
    blocks = (hi_count, 2, 2, depth, D)
    return pl.pallas_call(
        functools.partial(forward_kernel, hi_count),
        out_shape=(
            shape((SLABS,) + blocks, BF),
            shape((quads, rows, QUAD), BF),
            shape((quads, 2 * rows, QUAD), BF),
            shape((quads, 2 * rows, QUAD), BF),
            shape((HEADS, rows, LANES), BF),
            shape((8, HALF, rows), BF),
            shape((8, rows, HALF), BF),
            shape((D, 2 * rows), BF),
            shape((2 * rows, LANES), BF),
            shape((rows, D), BF),
            shape((D, rows), BF),
            shape((rows, D), F32),
            shape((rows, LANES), F32),
            shape((rows, D), BF),
            shape((rows, D), F32),
            shape((rows, D), BF),
            shape((3, D), F32),
            shape((VEC_ROWS, D), F32),
        ),
        in_specs=[vmem] * 10,
        out_specs=(anywhere,) * 8 + (vmem,) * 10,
        scratch_shapes=[
            pltpu.VMEM((SLABS, depth, D), BF),
            pltpu.VMEM((1, hi_count, 2, 2) + vec.shape[1:], F32),
            pltpu.VMEM((rows, D), BF),
            pltpu.VMEM((4,) + blocks, BF),
            pltpu.VMEM((quads, rows, QUAD), BF),
            pltpu.VMEM((quads, 2 * rows, QUAD), BF),
            pltpu.VMEM((quads, 2 * rows, QUAD), BF),
            pltpu.VMEM((HEADS, rows, LANES), BF),
            pltpu.VMEM((rows, D), F32),
            pltpu.VMEM((rows, D), BF),
            pltpu.VMEM((D, 2 * rows), BF),
            pltpu.VMEM((rows, D), F32),
            pltpu.VMEM((8, rows, HALF), BF),
            pltpu.VMEM((2, HALF, rows), BF),
            pltpu.VMEM((2, rows, HALF), BF),
            pltpu.VMEM((3, D), F32),
            dma((2,)),
            dma((4,)),
            dma((5, quads)),
            dma((4,)),
        ]
        + Gather.scratch(hi_count, SLABS, depth)
        + Gather.scratch(hi_count, 1, vec.shape[1], swap=0),
        compiler_params=pltpu.CompilerParams(
            collective_id=0, has_side_effects=True, vmem_limit_bytes=VMEM
        ),
        name="forward",
    )(*weights, vec, tokens, cotangent, q_doc, cosine, sine)


RING = 8
EARLY = 9


class Scatter:
    stages = (0, 2, 4, 6, 8)

    def __init__(self, hi_count, depth, grads, from_core, bufs, sems):
        self.hi_count, self.depth = hi_count, depth
        self.grads, self.from_core = grads, from_core
        (self.held, self.staged, self.from_x, self.from_y, self.from_z, self.late_y, self.late_z,
         self.own, self.other) = bufs
        (self.load_sem, self.c_send, self.c_recv, self.x_send, self.x_recv, self.y_send, self.y_recv,
         self.z_send, self.z_recv, self.f_send, self.f_recv) = sems
        self.hi, self.mid, self.core, self.rep = place(hi_count)
        self.parts = Gather.parts_of(depth, SWAP)
        self.rows = depth // self.parts
        self.count = SLABS * self.parts
        self.lag = self.stages[-1]
        self.early = EARLY * self.parts

    @staticmethod
    def scratch(hi_count, depth):
        parts = Gather.parts_of(depth, SWAP)
        count, early, rows = SLABS * parts, EARLY * parts, depth // parts
        dma = pltpu.SemaphoreType.DMA
        bufs = [
            pltpu.VMEM((RING, hi_count, 2, rows, D), BF),
            pltpu.VMEM((hi_count, 2, rows, D), BF),
            pltpu.VMEM((early, hi_count, 2, rows, SWAP), BF),
            pltpu.VMEM((early, hi_count, rows, D - SWAP), BF),
            pltpu.VMEM((early, hi_count - 1, rows, D - SWAP), BF),
            pltpu.VMEM((count - early, hi_count, rows, D), BF),
            pltpu.VMEM((count - early, hi_count - 1, rows, D), BF),
            pltpu.VMEM((count, rows, D), BF),
            pltpu.VMEM((count, rows, D), BF),
        ]
        sems = [dma((2,))] + [dma((count,))] * 6 + [dma((count, hi_count - 1))] * 2 + [dma((count,))] * 2
        return bufs, sems

    def late(self, chunk):
        return isinstance(chunk, int) and chunk >= self.early

    def columns(self, chunk, which):
        if self.late(chunk):
            return slice(None)
        return pl.ds(pl.multiple_of(which * SWAP, LANES), D - SWAP)

    def only(self, which):
        return pl.ds(pl.multiple_of(which * (D - SWAP), LANES), SWAP)

    def y_land(self, chunk):
        return self.late_y.at[chunk - self.early] if self.late(chunk) else self.from_y.at[chunk]

    def z_land(self, chunk, m):
        if self.late(chunk):
            return self.late_z.at[chunk - self.early, m - 1]
        return self.from_z.at[chunk, m - 1]

    def block(self, chunk, which):
        start = (chunk % self.parts) * self.rows
        if not isinstance(start, int):
            start = pl.multiple_of(start, self.rows)
        return self.grads.at[chunk // self.parts, :, :, which, pl.ds(start, self.rows)]

    def c_copy(self, chunk):
        return remote(
            self.block(chunk, 1 - self.core),
            self.from_core.at[chunk],
            self.c_send.at[chunk],
            self.c_recv.at[chunk],
            shard_of(self.hi, self.mid, 1 - self.core),
        )

    def loads(self, chunk):
        return [
            pltpu.make_async_copy(
                self.block(chunk, self.core), self.held.at[chunk % RING], self.load_sem.at[0]
            ),
            pltpu.make_async_copy(self.from_core.at[chunk], self.staged, self.load_sem.at[1]),
        ]

    def x_copy(self, chunk):
        return remote(
            self.held.at[chunk % RING, :, :, :, self.only(1 - self.rep)],
            self.from_x.at[chunk],
            self.x_send.at[chunk],
            self.x_recv.at[chunk],
            {"rep": 1 - self.rep},
        )

    def y_copy(self, chunk):
        return remote(
            self.held.at[chunk % RING, :, 1 - self.mid, :, self.columns(chunk, self.rep)],
            self.y_land(chunk),
            self.y_send.at[chunk],
            self.y_recv.at[chunk],
            shard_of(self.hi, 1 - self.mid, self.core),
        )

    def z_copy(self, chunk, m):
        there = (self.hi + m) % self.hi_count
        return remote(
            self.held.at[chunk % RING, there, self.mid, :, self.columns(chunk, self.rep)],
            self.z_land(chunk, m),
            self.z_send.at[chunk, m - 1],
            self.z_recv.at[chunk, m - 1],
            shard_of(there, self.mid, self.core),
        )

    def f_copy(self, chunk, landed):
        columns = self.columns(chunk, 1 - self.rep if landed else self.rep)
        source = self.other if landed else self.own
        return remote(
            source.at[chunk, :, columns],
            self.other.at[chunk, :, columns],
            self.f_send.at[chunk],
            self.f_recv.at[chunk],
            {"rep": 1 - self.rep},
        )

    def hand_over(self, slab):
        for part in range(self.parts):
            self.c_copy(slab * self.parts + part).start()

    def free(self, chunk):
        if not self.late(chunk):
            self.x_copy(chunk).wait_send()
        self.y_copy(chunk).wait_send()
        for m in range(1, self.hi_count):
            self.z_copy(chunk, m).wait_send()

    def tick(self, t):
        def stage(number, act):
            chunk = t - self.stages[number]
            if isinstance(chunk, int):
                if 0 <= chunk < self.early:
                    act(chunk)
                chunk = t - self.stages[max(number - 1, 0)]
                if self.early <= chunk < self.count:
                    act(chunk)
            else:
                pl.when(chunk >= 0)(lambda: act(chunk))

        def begin(chunk):
            self.c_copy(chunk).wait_recv()
            if isinstance(chunk, int):
                if chunk >= RING:
                    self.free(chunk - RING)
            else:
                pl.when(chunk >= RING)(lambda: self.free(chunk - RING))
            for copy in self.loads(chunk):
                copy.start()

        def add_core(chunk):
            for copy in self.loads(chunk):
                copy.wait()
            slot = chunk % RING

            @pl.loop(0, self.hi_count)
            def _(h):
                for m in range(2):
                    self.held[slot, h, m] = self.held[slot, h, m] + self.staged[h, m]

            if self.late(chunk):
                self.y_copy(chunk).start()
            else:
                self.x_copy(chunk).start()

        def add_x(chunk):
            if self.late(chunk):
                return
            self.x_copy(chunk).wait_recv()
            slot, columns = chunk % RING, self.only(self.rep)

            @pl.loop(0, self.hi_count)
            def _(h):
                for m in range(2):
                    self.held[slot, h, m, :, columns] = (
                        self.held[slot, h, m, :, columns] + self.from_x[chunk, h, m]
                    )

            self.y_copy(chunk).start()

        def add_y(chunk):
            self.y_copy(chunk).wait_recv()
            slot, columns = chunk % RING, self.columns(chunk, self.rep)

            @pl.loop(0, self.hi_count)
            def _(h):
                self.held[slot, h, self.mid, :, columns] = (
                    self.held[slot, h, self.mid, :, columns] + self.y_land(chunk)[h]
                )

            for m in range(1, self.hi_count):
                self.z_copy(chunk, m).start()

        def add_z(chunk):
            columns = self.columns(chunk, self.rep)
            value = self.held[chunk % RING, self.hi, self.mid, :, columns].astype(F32)
            for m in range(1, self.hi_count):
                self.z_copy(chunk, m).wait_recv()
                value += self.z_land(chunk, m)[...].astype(F32)
            self.own[chunk, :, columns] = value.astype(BF)
            self.f_copy(chunk, False).start()

        stage(0, begin)
        stage(1, add_x)
        stage(2, add_y)
        stage(3, add_z)
        stage(4, lambda chunk: self.f_copy(chunk, True).wait_recv())
        stage(0, add_core)

    def drain(self):
        def finish(chunk):
            self.c_copy(chunk).wait_send()
            self.f_copy(chunk, False).wait_send()

        pl.loop(0, self.early)(finish)
        for chunk in range(self.early, self.count):
            finish(chunk)
        for chunk in range(self.count - RING, self.count):
            self.free(chunk)

    def whole(self, slab, columns):
        at = [slab * self.parts + part for part in range(self.parts)]
        parts = [self.own[c, :, columns].astype(F32) + self.other[c, :, columns].astype(F32) for c in at]
        return parts[0] if self.parts == 1 else jnp.concatenate(parts, axis=0)


class VectorScatter:
    def __init__(self, hi_count, bufs, sems):
        self.hi_count = hi_count
        self.mine, self.from_core, self.from_y, self.from_z, self.own, self.other = bufs
        (self.c_send, self.c_recv, self.y_send, self.y_recv, self.z_send, self.z_recv, self.f_send,
         self.f_recv) = sems
        self.hi, self.mid, self.core, self.rep = place(hi_count)

    @staticmethod
    def scratch(hi_count):
        tile = (VEC_ROWS, LANES)
        dma = pltpu.SemaphoreType.DMA
        bufs = [
            pltpu.VMEM((hi_count, 2, 2) + tile, F32),
            pltpu.VMEM((hi_count, 2) + tile, F32),
            pltpu.VMEM((hi_count,) + tile, F32),
            pltpu.VMEM((hi_count - 1,) + tile, F32),
            pltpu.VMEM(tile, F32),
            pltpu.VMEM(tile, F32),
        ]
        return bufs, [dma((1,))] * 4 + [dma((hi_count - 1,))] * 2 + [dma((1,))] * 2

    def c_copy(self):
        device = shard_of(self.hi, self.mid, 1 - self.core)
        source = self.mine.at[:, :, 1 - self.core]
        return remote(source, self.from_core, self.c_send.at[0], self.c_recv.at[0], device)

    def y_copy(self):
        device = shard_of(self.hi, 1 - self.mid, self.core)
        source = self.mine.at[:, 1 - self.mid, self.core]
        return remote(source, self.from_y, self.y_send.at[0], self.y_recv.at[0], device)

    def z_copy(self, m):
        there = (self.hi + m) % self.hi_count
        source = self.mine.at[there, self.mid, self.core]
        sems = (self.z_send.at[m - 1], self.z_recv.at[m - 1])
        return remote(source, self.from_z.at[m - 1], *sems, shard_of(there, self.mid, self.core))

    def f_copy(self):
        return remote(self.own, self.other, self.f_send.at[0], self.f_recv.at[0], {"rep": 1 - self.rep})

    def step(self, number):
        if number == 0:
            self.c_copy().start()
        elif number == 1:
            self.c_copy().wait_recv()
            self.mine[:, :, self.core] = self.mine[:, :, self.core] + self.from_core[...]
            self.y_copy().start()
        elif number == 2:
            self.y_copy().wait_recv()
            self.mine[:, self.mid, self.core] = self.mine[:, self.mid, self.core] + self.from_y[...]
            for m in range(1, self.hi_count):
                self.z_copy(m).start()
        elif number == 3:
            total = self.mine[self.hi, self.mid, self.core]
            for m in range(1, self.hi_count):
                self.z_copy(m).wait_recv()
                total += self.from_z[m - 1]
            self.own[...] = total
            self.f_copy().start()
        else:
            self.f_copy().wait()
            self.c_copy().wait_send()
            self.y_copy().wait_send()
            for m in range(1, self.hi_count):
                self.z_copy(m).wait_send()


def spread_vectors(mine, rows, bias, depth):
    hi_count = mine.shape[0]
    for shard in range(4 * hi_count):
        at = shard // 4, shard // 2 % 2, shard % 2

        def piece(ref, some, start):
            tile = ref[some, tile_of(start)]
            shift = -start % LANES
            return pltpu.roll(tile, shift, 1) if shift else tile

        mine[at] = piece(rows, slice(None), shard * depth)
        for t in range(3):
            start = (3 * shard + t) * depth
            slab = start // D
            mine[at + (slice(t, t + 1),)] = piece(bias, slice(slab, slab + 1), start % D)


def backward_kernel(
    hi_count,
    full,
    d_ffn_in,
    d_second,
    first_in,
    normed_in,
    q_all,
    k_all,
    v_all,
    q_ext_all,
    active_all,
    slope_all,
    x_all,
    inv_std,
    context,
    k_doc,
    vectors,
    sums_two,
    cosine,
    sine,
    grads,
    from_core,
    input_grad,
    g_qkv,
    g_out,
    g_up,
    g_down,
    g_vec,
    down_buf,
    up_buf,
    d_context,
    peer_part,
    peer_sum,
    rows_grad,
    bias_grad,
    load_sem,
    flush_sem,
    w_sem,
    p_sem,
    *rest,
):
    rows = context.shape[0]
    depth = g_qkv.shape[0]
    scatter = Scatter(hi_count, depth, grads, from_core, rest[:9], rest[9:20])
    small = VectorScatter(hi_count, rest[20:26], rest[26:])
    hi, mid, core, rep = place(hi_count)
    scatter.own[...] = jnp.zeros_like(scatter.own)
    scatter.other[...] = jnp.zeros_like(scatter.other)
    rows_grad[...] = jnp.zeros_like(rows_grad)
    rows_grad[B_DOWN : B_DOWN + 3] = sums_two[...]
    entry_barrier(hi_count, hi, mid, core, rep)
    upper = hi_count // 2
    own_rows = pl.ds(pl.multiple_of(rep * rows, rows), rows)
    peer_rows = pl.ds(pl.multiple_of((1 - rep) * rows, rows), rows)

    def flush_rows(slab, half):
        return pltpu.make_async_copy(
            down_buf.at[half], grads.at[slab, pl.ds(half * upper, upper)], flush_sem.at[half]
        )

    def flush_columns(slab, half):
        columns = pl.ds(half * HALF, HALF)
        return pltpu.make_async_copy(
            up_buf.at[half], grads.at[slab, :, :, :, :, columns], flush_sem.at[2 + half]
        )

    early = 4 * scatter.parts + (scatter.parts == 1)

    def ffn_phase(slots, act, slope, d_ffn, first, normed):
        def weights(j, base):
            return [
                pltpu.make_async_copy(full.at[slab + j], slots.at[base + s], w_sem.at[base + s])
                for s, slab in enumerate((UP, DOWN))
            ]

        def kept(j, half):
            return [
                pltpu.make_async_copy(active_all.at[2 * j + half], act.at[half], load_sem.at[2 * half]),
                pltpu.make_async_copy(slope_all.at[2 * j + half], slope.at[half], load_sem.at[2 * half + 1]),
            ]

        others = [
            pltpu.make_async_copy(d_ffn_in, d_ffn, p_sem.at[0]),
            pltpu.make_async_copy(first_in, first, p_sem.at[1]),
            pltpu.make_async_copy(d_second, input_grad, p_sem.at[2]),
            pltpu.make_async_copy(normed_in, normed, p_sem.at[3]),
        ]
        for copy in others[:1] + weights(0, 0) + kept(0, 0) + kept(0, 1) + others[1:]:
            copy.start()
        for copy in others:
            copy.wait()

        @pl.loop(0, 4)
        def _(j):
            base = lax.rem(j, 2) * 2
            for copy in weights(j, base):
                copy.wait()

            @pl.when(j < 3)
            def _():
                for copy in weights(j + 1, 2 - base):
                    copy.start()

            for half in range(2):
                for copy in kept(j, half):
                    copy.wait()
                low = d_ffn[...]
                down = slots[base + 1, half * upper : (half + 1) * upper].reshape(HALF, D)
                d_hidden = (dot_nt(low, down) * slope[half].astype(F32)).astype(BF)
                columns = slice(half * HALF, (half + 1) * HALF)
                rows_grad[pl.ds(B_UP + j, 1), columns] = column_sum(d_hidden.astype(F32))
                g_rows = dot(act[half], low)
                g_columns = dot(first[...], d_hidden)

                @pl.when(j < 3)
                def _():
                    for copy in kept(j + 1, half):
                        copy.start()

                down_buf[half] = g_rows.astype(BF).reshape(down_buf.shape[1:])
                up_buf[half] = g_columns.astype(BF).reshape(up_buf.shape[1:])
                flush_rows(2 * j, half).start()
                flush_columns(2 * j + 1, half).start()
                up = slots[base, :, :, :, :, columns].reshape(D, HALF)
                input_grad[...] += dot_nt(d_hidden, up)
                if half:
                    for h in range(2):
                        flush_rows(2 * j, h).wait()
                        flush_columns(2 * j + 1, h).wait()
                    scatter.hand_over(2 * j)
                    scatter.hand_over(2 * j + 1)
                t = scatter.parts * j + half - scatter.parts + 1
                if half or scatter.parts == 2:
                    pl.when(t >= 0)(lambda: scatter.tick(t))

        w_out = pltpu.make_async_copy(full.at[3], slots.at[0], w_sem.at[0])
        w_out.start()
        up = input_grad[...]
        normed_rows_ = normed[...]
        rows_grad[GAIN_ONE : GAIN_ONE + 1] = column_sum(up * normed_rows_)
        rows_grad[SHIFT_ONE : SHIFT_ONE + 1] = column_sum(up)
        grad = norm_back(up, normed_rows_, inv_std[:, 0:1], vectors[GAIN_ONE : GAIN_ONE + 1])
        input_grad[...] = grad
        d_attn = d_ffn
        d_attn[...] = grad.astype(BF)
        rows_grad[B_OUT : B_OUT + 1] = column_sum(d_attn[...].astype(F32))
        scatter.tick(early - 1)
        w_out.wait()
        for half in range(2):
            columns = slice(half * HALF, (half + 1) * HALF)
            g_rows = dot_tn(context[:, columns], d_attn[...])
            down_buf[half] = g_rows.astype(BF).reshape(down_buf.shape[1:])
            flush_rows(8, half).start()
        d_context[...] = dot_nt(d_attn[...], slots[0].reshape(D, D)).astype(BF)
        for half in range(2):
            flush_rows(8, half).wait()
        scatter.hand_over(8)

    blocks = (hi_count, 2, 2, depth, D)
    pl.run_scoped(
        ffn_phase,
        pltpu.VMEM((4,) + blocks, BF),
        pltpu.VMEM((2, HALF, rows), BF),
        pltpu.VMEM((2, rows, HALF), BF),
        pltpu.VMEM((rows, D), BF),
        pltpu.VMEM((D, rows), BF),
        pltpu.VMEM((rows, D), F32),
    )

    at = [min(early + HEADS // 2, 9 * scatter.parts)]

    def advance(handed):
        if at[0] < (9 + handed) * scatter.parts:
            scatter.tick(at[0])
            at[0] += 1

    def attention_phase(slots, q_in, k_in, v_in, ext_in, d_q, d_k, d_v, x):
        def quad(i, slot):
            return [
                pltpu.make_async_copy(q_all.at[i], q_in.at[slot], load_sem.at[slot]),
                pltpu.make_async_copy(k_all.at[i], k_in.at[slot], load_sem.at[2 + slot]),
                pltpu.make_async_copy(v_all.at[i], v_in.at[slot], load_sem.at[4 + slot]),
                pltpu.make_async_copy(q_ext_all.at[pl.ds(4 * i, 4)], ext_in.at[slot], load_sem.at[6 + slot]),
            ]

        weights = [pltpu.make_async_copy(full.at[s], slots.at[s], w_sem.at[s]) for s in range(3)]
        x_copy = pltpu.make_async_copy(x_all, x, w_sem.at[3])
        for copy in quad(0, 0) + weights + [x_copy]:
            copy.start()
        doc_k = k_doc[...]
        piece = 256

        def rope_back(a, table_rows):
            return a * cosine[table_rows, :] + swap_halves(a * sine[table_rows, :])

        @pl.loop(0, HEADS // 4)
        def _(i):
            slot = lax.rem(i, 2)
            for copy in quad(i, slot):
                copy.wait()

            @pl.when(i < HEADS // 4 - 1)
            def _():
                for copy in quad(i + 1, 1 - slot):
                    copy.start()

            for pair in range(2):
                lanes = slice(pair * LANES, (pair + 1) * LANES)
                wide = pl.ds(pl.multiple_of(i * QUAD + pair * LANES, LANES), LANES)
                k_pair, v_pair = k_in[slot, :, lanes], v_in[slot, :, lanes]
                k_lane = lax.broadcasted_iota(jnp.int32, k_pair.shape, 1)
                keys = jnp.concatenate([k_pair, doc_k], axis=1)
                minus = jnp.where(k_lane < 3, -1.0, 0.0).astype(BF)
                values = jnp.concatenate([v_pair, minus], axis=1)
                dk = dv = None
                for start in range(0, rows, piece):
                    part = slice(start, start + piece)
                    q_pair, g_pair = q_in[slot, part, lanes], d_context[part, wide]
                    lane = lax.broadcasted_iota(jnp.int32, q_pair.shape, 1)
                    product = g_pair.astype(F32) * context[part, wide].astype(F32)
                    dq = None
                    for head in range(2):
                        in_head = (lane // HEAD_DIM) == head
                        q_head = jnp.where(in_head, q_pair, 0)
                        g_head = jnp.where(in_head, g_pair, 0)
                        inner = jnp.sum(jnp.where(in_head, product, 0.0), axis=1, keepdims=True)
                        top, middle, low = split3(jnp.broadcast_to(inner, q_pair.shape))
                        g_ext = jnp.where(lane == 0, top, jnp.where(lane == 1, middle, low))
                        g_ext = jnp.where(lane < 3, g_ext, 0)
                        q_wide = jnp.concatenate([q_head, ext_in[slot, pair * 2 + head, part, :]], axis=1)
                        prob = jnp.exp(dot_nt(keys, q_wide))
                        d_prob = dot_nt(values, jnp.concatenate([g_head, g_ext], axis=1))
                        d_score = (prob * d_prob).astype(BF)
                        dv_part = dot(prob.astype(BF), g_head)
                        dk_part = dot(d_score, q_head)
                        k_head = jnp.where((k_lane // HEAD_DIM) == head, k_pair, 0)
                        dq_part = dot_tn(d_score, k_head)
                        dv = dv_part if dv is None else dv + dv_part
                        dk = dk_part if dk is None else dk + dk_part
                        dq = dq_part if dq is None else dq + dq_part
                    table_rows = pl.ds(pl.multiple_of(rep * rows + start, piece), piece)
                    d_q[part, wide] = rope_back(dq * HEAD_DIM**-0.5, table_rows).astype(BF)
                d_k[:rows, wide] = rope_back(dk[:rows], own_rows).astype(BF)
                d_k[rows:, wide] = rope_back(dk[rows:], peer_rows).astype(BF)
                d_v[:, wide] = dv.astype(BF)
                t = early + 2 * i + pair
                pl.when(t < 9 * scatter.parts)(lambda: scatter.tick(t))

        for copy in weights + [x_copy]:
            copy.wait()
        def slab_grad(s, count, d_rows):
            for half in range(2):
                columns = slice(half * HALF, (half + 1) * HALF)
                if s > 0:
                    flush_columns(8 + s, half).wait()
                g_columns = dot(x[:, :count], d_rows[:, columns])
                up_buf[half] = g_columns.astype(BF).reshape(up_buf.shape[1:])
                flush_columns(9 + s, half).start()
            if s > 0:
                scatter.hand_over(8 + s)
            bias_grad[s : s + 1] = column_sum(d_rows[...].astype(F32))

        slab_grad(0, rows, d_q)
        advance(0)
        slab_grad(1, 2 * rows, d_k)
        advance(1)
        slab_grad(2, 2 * rows, d_v)
        advance(2)
        for half in range(2):
            flush_columns(11, half).wait()
        scatter.hand_over(11)
        w_k, w_v = slots[1].reshape(D, D), slots[2].reshape(D, D)
        peer_part[...] = (dot_nt(d_k[rows:], w_k) + dot_nt(d_v[rows:], w_v)).astype(BF)
        peer_copy = remote(peer_part, peer_sum, p_sem.at[4], p_sem.at[5], {"rep": 1 - rep})
        peer_copy.start()
        advance(3)
        spread_vectors(small.mine, rows_grad, bias_grad, depth)
        small.step(0)
        advance(3)
        small.step(1)
        input_grad[...] += dot_nt(d_q[...], slots[0].reshape(D, D))
        advance(3)
        input_grad[...] += dot_nt(d_k[:rows], w_k)
        advance(3)
        small.step(2)
        input_grad[...] += dot_nt(d_v[:rows], w_v)

    pl.run_scoped(
        attention_phase,
        pltpu.VMEM((3,) + blocks, BF),
        pltpu.VMEM((2, rows, QUAD), BF),
        pltpu.VMEM((2, 2 * rows, QUAD), BF),
        pltpu.VMEM((2, 2 * rows, QUAD), BF),
        pltpu.VMEM((2, 4, rows, LANES), BF),
        pltpu.VMEM((rows, D), BF),
        pltpu.VMEM((2 * rows, D), BF),
        pltpu.VMEM((2 * rows, D), BF),
        pltpu.VMEM((D, 2 * rows), BF),
    )

    end = scatter.count + scatter.stages[-2]
    settled = EARLY * scatter.parts + scatter.lag
    for t in range(at[0], settled):
        scatter.tick(t)
    g_out[...] = scatter.whole(8, slice(None))
    for j in range(4):
        g_down[j * depth : (j + 1) * depth] = scatter.whole(2 * j, slice(None))
    for t in range(settled, end - 1):
        scatter.tick(t)
    small.step(3)
    each = LANES // depth
    for t in range(FF // LANES):
        pieces = []
        for u in range(each):
            shard, j = divmod(t * each + u, 4)
            pieces.append((scatter.whole(2 * j + 1, tile_of(shard * depth)), shard * depth % LANES))
        g_up[:, t * LANES : (t + 1) * LANES] = regroup(pieces, depth)
    scatter.tick(end - 1)
    for s in range(3):
        g_qkv[:, s * D : (s + 1) * D] = scatter.whole(9 + s, slice(None))
    peer_copy = remote(peer_part, peer_sum, p_sem.at[4], p_sem.at[5], {"rep": 1 - rep})
    peer_copy.wait()
    input_grad[...] += peer_sum[...].astype(F32)
    small.step(4)
    g_vec[...] = small.own[...] + small.other[...]
    scatter.drain()


def backward(hi_count, full, arrays, kept):
    context, depth = kept[1], full.shape[4]
    rows = context.shape[0]
    anywhere = pl.BlockSpec(memory_space=pl.ANY)
    vmem = pl.BlockSpec(memory_space=pltpu.VMEM)
    dma = pltpu.SemaphoreType.DMA
    shape = jax.ShapeDtypeStruct
    blocks = (hi_count, 2, 2, depth)
    parts = Gather.parts_of(depth, SWAP)
    bufs, sems = Scatter.scratch(hi_count, depth)
    small_bufs, small_sems = VectorScatter.scratch(hi_count)
    return pl.pallas_call(
        functools.partial(backward_kernel, hi_count),
        out_shape=(
            shape((SLABS,) + blocks + (D,), BF),
            shape((SLABS * parts, hi_count, 2, depth // parts, D), BF),
            shape((rows, D), F32),
            shape((depth, 3 * D), F32),
            shape((depth, D), F32),
            shape((depth, FF), F32),
            shape((4 * depth, D), F32),
            shape((VEC_ROWS, LANES), F32),
        ),
        in_specs=[anywhere] * (1 + len(arrays)) + [vmem] * len(kept),
        out_specs=(anywhere,) * 2 + (vmem,) * 6,
        scratch_shapes=[
            pltpu.VMEM((2, hi_count // 2, 2, 2, depth, D), BF),
            pltpu.VMEM((2,) + blocks + (HALF,), BF),
            pltpu.VMEM((rows, D), BF),
            pltpu.VMEM((rows, D), BF),
            pltpu.VMEM((rows, D), BF),
            pltpu.VMEM((VEC_ROWS, D), F32),
            pltpu.VMEM((3, D), F32),
            dma((8,)),
            dma((4,)),
            dma((4,)),
            dma((6,)),
        ]
        + bufs
        + sems
        + small_bufs
        + small_sems,
        compiler_params=pltpu.CompilerParams(
            collective_id=1, has_side_effects=True, vmem_limit_bytes=VMEM
        ),
        name="backward",
    )(full, *arrays, *kept)


def rope_tables(count):
    position = np.arange(count, dtype=np.float32)
    frequency = np.exp(np.arange(HEAD_DIM // 2, dtype=np.float32) * np.float32(-2.0 * math.log(10000.0) / HEAD_DIM))
    angles = position[:, None] * frequency[None, :].astype(np.float32)
    cosine, sine = np.cos(angles).astype(np.float32), np.sin(angles).astype(np.float32)
    return (
        jnp.asarray(np.concatenate([cosine] * 4, axis=1)),
        jnp.asarray(np.concatenate([-sine, sine, -sine, sine], axis=1)),
    )


def local(
    tokens,
    segments,
    cotangent,
    w_qkv,
    b_qkv,
    w_out,
    b_out,
    gain_one,
    shift_one,
    w_up,
    b_up,
    w_down,
    b_down,
    gain_two,
    shift_two,
):
    rows = tokens.shape[0]
    shards = lax.axis_size("shard")
    hi_count = shards // 4
    depth = D // shards
    small = (b_qkv, b_out, gain_one, shift_one, b_up, b_down, gain_two, shift_two)
    widths = [a.shape[0] for a in small]
    vec = jnp.concatenate(small + (jnp.zeros((VEC_ROWS * depth - sum(widths),), F32),))
    vec = jnp.tile(vec.reshape(VEC_ROWS, depth), (1, LANES // depth))
    lane = jnp.arange(LANES, dtype=jnp.int32)[None, :]
    q_doc = (segments[:, None] == lane).astype(BF)
    cosine, sine = rope_tables(2 * rows)
    (
        full, q, k, v, q_ext, active, slope, x_all, k_doc, context, first, normed, inv_std, result,
        d_second, d_ffn, sums_two, vectors,
    ) = forward(hi_count, (w_qkv, w_out, w_up, w_down), vec[None], tokens, cotangent, q_doc, cosine, sine)
    _, _, input_grad, g_qkv, g_out, g_up, g_down, g_vec = backward(
        hi_count,
        full,
        (d_ffn, d_second, first, normed, q, k, v, q_ext, active, slope, x_all),
        (inv_std, context, k_doc, vectors, sums_two, cosine, sine),
    )
    outs = []
    at = 0
    for width in widths:
        count = width // depth
        outs.append(g_vec[at : at + count, :depth].reshape(width))
        at += count
    return (
        result,
        input_grad,
        g_qkv,
        outs[0],
        g_out,
        outs[1],
        outs[2],
        outs[3],
        g_up,
        outs[4],
        g_down,
        outs[5],
        outs[6],
        outs[7],
    )


def solution(mesh):
    act = P(("shard", "rep"), None)
    matrix = P("shard", None)
    vector = P("shard")
    params = (matrix, vector, matrix, vector, vector, vector, matrix, vector, matrix, vector, vector, vector)
    return jax.shard_map(
        local,
        mesh=mesh,
        in_specs=(act, P(("shard", "rep")), act) + params,
        out_specs=(act, act) + params,
        check_vma=False,
    )
```
